32 devices in a mesh: crop: 8 (over z, y), head: 4 (over x, core).
Axes of the slice: x: 2, y: 2, z: 4, core: 2. Of those that a mesh axis runs over, the one named last changes fastest.
Arguments:
- tokens: bfloat16 [16384, 768], P(('crop', 'head')), may hold values from -6 to 6
- mix_weight: float32 [16384], P(('crop', 'head')), may hold values from 0.5 to 0.9
- partner_row: int32 [16384], P(('crop', 'head')), may hold values from 0 to 511
- crop_lengths: int32 [8, 2], P('crop'), may hold values from 416 to 1632, as said below
- ln1_gain: bfloat16 [768], replicated, may hold values from 0.5 to 1.5
- ln1_bias: bfloat16 [768], replicated, may hold values from -1.5 to 1.5
- w_qkv: bfloat16 [768, 2304], replicated, may hold values from -0.21875 to 0.21875
- b_query: bfloat16 [768], replicated, may hold values from -1.5 to 1.5
- b_value: bfloat16 [768], replicated, may hold values from -1.5 to 1.5
- w_out: bfloat16 [768, 768], replicated, may hold values from -2.5 to 2.5
- b_out: bfloat16 [768], replicated, may hold values from -1.5 to 1.5
- ln2_gain: bfloat16 [768], replicated, may hold values from 0.5 to 1.5
- ln2_bias: bfloat16 [768], replicated, may hold values from -1.5 to 1.5
- w_fc1: bfloat16 [768, 3072], replicated, may hold values from -0.21875 to 0.21875
- b_fc1: bfloat16 [3072], replicated, may hold values from -1.5 to 1.5
- w_fc2: bfloat16 [3072, 768], replicated, may hold values from -0.109375 to 0.109375
- b_fc2: bfloat16 [768], replicated, may hold values from -1.5 to 1.5
- cotangent: bfloat16 [16384, 768], P(('crop', 'head')), may hold values from -6 to 6
Outputs:
- layer_out: bfloat16 [16384, 768], P(('crop', 'head'))
- input_grad: bfloat16 [16384, 768], P(('crop', 'head'))
- grad_ln1_gain: float32 [768], P('crop')
- grad_ln1_bias: float32 [768], P('crop')
- grad_w_qkv: float32 [768, 2304], P('crop')
- grad_b_query: float32 [768], P('crop')
- grad_b_value: float32 [768], P('crop')
- grad_w_out: float32 [768, 768], P('crop')
- grad_b_out: float32 [768], P('crop')
- grad_ln2_gain: float32 [768], P('crop')
- grad_ln2_bias: float32 [768], P('crop')
- grad_w_fc1: float32 [768, 3072], P('crop')
- grad_b_fc1: float32 [3072], P('crop')
- grad_w_fc2: float32 [3072, 768], P('crop')
- grad_b_fc2: float32 [768], P('crop')
The draws below stay inside these ranges and needn't reach their ends.
Inputs may be any that keep to these rules, and one draw needn't show every extreme that they name: `crop_lengths`: each row holds the 2 crop lengths of one group; they sum to 2048; in every group one crop starts within the first 512 rows of the group and ends within its last 512 rows.
All inputs are finite; a program needn't handle non-finite values.
Results may differ from the reference program's by a relative error of at most 0.014.
Values may be sent and summed in bfloat16 or wider, within the bound.
A program may use at most 192 MiB of HBM per device.

```python
from functools import partial
import jax
import jax.numpy as jnp
from jax import lax

D = 768
HEADS = 12
HEAD_DIM = 64
FF = 3072
TOK_DEV = 512
CROPS = 2
GROUPS = 8
GROUP_TOK = 2048
TOKENS = 16384
N_CROP = 8
N_HEAD = 4


def draw_crop_lengths(key, part):
    key = jax.random.fold_in(key, 11)
    first_key, second_key = jax.random.split(key)
    least = TOK_DEV * 13 // 16
    most = TOK_DEV * 15 // 16
    remainder = jax.random.randint(first_key, (GROUPS, 1), least, most + 1)
    group_index = jnp.arange(GROUPS)[:, None]
    remainder = jnp.where(group_index == 0, least, remainder)
    long_slot = jax.random.randint(second_key, (GROUPS, 1), 0, CROPS)
    slot_index = jnp.arange(CROPS)[None, :]
    is_long = slot_index == long_slot
    return jnp.where(is_long, GROUP_TOK - remainder, remainder).astype(jnp.int32)


def set_ends(values, stream_key, smallest, high):
    longest = values.shape.index(max(values.shape))
    spots = []
    for shift in (0, 1):
        where = [jax.random.randint(jax.random.fold_in(stream_key, axis), (), 0, length) for axis, length in enumerate(values.shape)]
        where[longest] = (where[longest] + shift) % values.shape[longest]
        spots.append(tuple(where))
    return values.at[spots[0]].set(smallest).at[spots[1]].set(high)


def shard_levels(stream_key, dims, cuts, low, largest):
    loudness = 1.0
    for axis_at, shards_of in cuts:
        steps = jax.random.uniform(jax.random.fold_in(jax.random.fold_in(stream_key, 6), axis_at), (shards_of,), jnp.float32, low / len(cuts), largest / len(cuts))
        loudness = loudness * jnp.repeat(jnp.exp(steps), dims[axis_at] // shards_of).reshape((-1,) + (1,) * (len(dims) - 1 - axis_at))
    return loudness


def bell_draw(own_key, dims, spread, most, cuts=(), kind=jnp.bfloat16):
    values = jax.random.normal(own_key, dims, jnp.float32) * spread
    if len(cuts) > 0:
        values = shard_levels(own_key, dims, cuts, -0.22, 0.18) * values
    return jnp.clip(values, min=-most, max=most).astype(kind)


def setup_inputs(seed: int = 0) -> dict:
    keys = jax.random.split(jax.random.key(seed), 19)
    return {
        "tokens": bell_draw(keys[0], (TOKENS, D), 1.0, 6.0, ((0, 32),)),
        "mix_weight": jnp.clip(0.5 + 0.39999998 * jax.random.uniform(keys[1], (TOKENS,), jnp.float32) ** shard_levels(keys[1], (TOKENS,), ((0, 32),), -0.2, 0.2), 0.5, 0.9),
        "partner_row": set_ends(jax.random.randint(keys[2], (TOKENS,), 0, TOK_DEV), jax.random.fold_in(keys[2], 1), 0, TOK_DEV - 1).astype(jnp.int32),
        "crop_lengths": draw_crop_lengths(jax.random.fold_in(keys[18], 71), 0),
        "ln1_gain": jnp.clip(1.0 + 0.1 * jax.random.normal(keys[4], (D,), jnp.float32), 0.5, 1.5).astype(jnp.bfloat16),
        "ln1_bias": bell_draw(keys[5], (D,), 0.3, 1.5),
        "w_qkv": bell_draw(keys[6], (D, 3 * D), D ** -0.5, 0.21875),
        "b_query": bell_draw(keys[7], (D,), 0.3, 1.5),
        "b_value": bell_draw(keys[8], (D,), 0.3, 1.5),
        "w_out": bell_draw(keys[9], (D, D), (max(1, 4 * D // TOK_DEV)) ** -0.5, 2.5),
        "b_out": bell_draw(keys[10], (D,), 0.3, 1.5),
        "ln2_gain": jnp.clip(1.0 + 0.1 * jax.random.normal(keys[11], (D,), jnp.float32), 0.5, 1.5).astype(jnp.bfloat16),
        "ln2_bias": bell_draw(keys[12], (D,), 0.3, 1.5),
        "w_fc1": bell_draw(keys[13], (D, FF), D ** -0.5, 0.21875),
        "b_fc1": bell_draw(keys[14], (FF,), 0.3, 1.5),
        "w_fc2": bell_draw(keys[15], (FF, D), FF ** -0.5, 0.109375),
        "b_fc2": bell_draw(keys[16], (D,), 0.3, 1.5),
        "cotangent": bell_draw(keys[17], (TOKENS, D), 1.0, 6.0, ((0, 32),)),
    }


@jax.custom_vjp
def low(v):
    return lax.optimization_barrier(v.astype(jnp.bfloat16)).astype(jnp.float32)

@jax.custom_vjp
def low_back(v):
    return v

def low_keep(v):
    return (low(v), None)

def low_pass(kept, grad):
    return (grad,)

def back_keep(v):
    return (v, None)

def back_low(kept, grad):
    return (low(grad),)
low.defvjp(low_keep, low_pass)
low_back.defvjp(back_keep, back_low)
highest = lax.Precision.HIGHEST

def layer_norm(hidden, norm_gain, norm_bias):
    row_mean = lax.optimization_barrier(jnp.mean(hidden, axis=-1, keepdims=True))
    centered = hidden - row_mean
    variance = lax.optimization_barrier(jnp.mean(centered * centered, axis=-1, keepdims=True))
    return centered * lax.rsqrt(variance + 1e-06) * norm_gain + norm_bias

def group_layer(params, hidden, segment):
    gain1, bias1, wqkv, bquery, bvalue, wout, bout, gain2, bias2, wfc1, bfc1, wfc2, bfc2 = params
    row_count = hidden.shape[0]
    normed = low(layer_norm(hidden, gain1, bias1))
    bias_full = jnp.stack([bquery.reshape(HEADS, HEAD_DIM), jnp.zeros_like(bquery).reshape(HEADS, HEAD_DIM), bvalue.reshape(HEADS, HEAD_DIM)], axis=1).reshape(3 * D)
    packed = jnp.dot(normed, wqkv, precision=highest) + bias_full
    packed = low_back(low(packed)).reshape(row_count, HEADS, 3, HEAD_DIM)
    query_rows = packed[:, :, 0]
    key_rows = packed[:, :, 1]
    value_rows = packed[:, :, 2]
    scores = jnp.einsum('qhe,khe->hqk', query_rows, key_rows, precision=highest) * HEAD_DIM ** (-0.5)
    scores = low_back(scores)
    same_crop = segment[:, None] == segment[None, :]
    scores = jnp.where(same_crop[None], scores, -1e+30)
    probs = low(jax.nn.softmax(scores, axis=-1))
    attended = jnp.einsum('hqk,khe->qhe', probs, value_rows, precision=highest)
    attended = low_back(low(attended)).reshape(row_count, D)
    projected = low_back(jnp.dot(attended, wout, precision=highest) + bout)
    middle = hidden + projected
    normed2 = low(layer_norm(middle, gain2, bias2))
    hidden_pre = low_back(jnp.dot(normed2, wfc1, precision=highest) + bfc1)
    active = low(jax.nn.gelu(hidden_pre, approximate=False))
    branch = low_back(jnp.dot(active, wfc2, precision=highest) + bfc2)
    return middle + branch

def reference(tokens, mix_weight, partner_row, crop_lengths, ln1_gain, ln1_bias, w_qkv, b_query, b_value, w_out, b_out, ln2_gain, ln2_bias, w_fc1, b_fc1, w_fc2, b_fc2, cotangent):
    params = (ln1_gain.astype(jnp.float32), ln1_bias.astype(jnp.float32), w_qkv.astype(jnp.float32), b_query.astype(jnp.float32), b_value.astype(jnp.float32), w_out.astype(jnp.float32), b_out.astype(jnp.float32), ln2_gain.astype(jnp.float32), ln2_bias.astype(jnp.float32), w_fc1.astype(jnp.float32), b_fc1.astype(jnp.float32), w_fc2.astype(jnp.float32), b_fc2.astype(jnp.float32))
    inputs = tokens.astype(jnp.float32)
    device = jnp.arange(TOKENS, dtype=jnp.int32) // TOK_DEV
    crop_of = device // N_HEAD
    head_of = device % N_HEAD
    source = (crop_of + N_CROP // 2) % N_CROP * N_HEAD + head_of
    partner_index = (source * TOK_DEV + partner_row).astype(jnp.int32)
    crop_ends = jnp.cumsum(crop_lengths, axis=1).astype(jnp.int32)
    positions = jnp.arange(GROUP_TOK, dtype=jnp.int32)
    segments = lax.optimization_barrier(jnp.sum((positions[None, :, None] >= crop_ends[:, None, :]).astype(jnp.int32), axis=2)).astype(jnp.int32)
    mix_share = mix_weight.astype(jnp.float32)[:, None]

    def forward(inputs, params):
        mixed = mix_share * inputs + (1.0 - mix_share) * jnp.take(inputs, partner_index, axis=0)
        grouped = mixed.reshape(GROUPS, GROUP_TOK, D)
        group_step = jax.checkpoint(partial(group_layer, params))

        def scan_step(carry, scan_input):
            return (carry, group_step(scan_input[0], scan_input[1]))
        unused, outputs = lax.scan(scan_step, None, (grouped, segments))
        return outputs.reshape(TOKENS, D)
    result, pullback = jax.vjp(forward, inputs, params)
    input_grad, gradients = pullback(cotangent.astype(jnp.float32))
    return (result.astype(jnp.bfloat16), input_grad.astype(jnp.bfloat16), gradients[0], gradients[1], gradients[2], gradients[3], gradients[4], gradients[5], gradients[6], gradients[7], gradients[8], gradients[9], gradients[10], gradients[11], gradients[12])
```

```python
import functools

import jax
import jax.numpy as jnp
from jax import lax
from jax.experimental import pallas as pl
from jax.experimental.pallas import tpu as pltpu
from jax.sharding import PartitionSpec as P

HEADS = 12
HEAD_DIM = 64
EPS = 1e-06
NEG = -1e30
MESH = pl.DeviceIdType.MESH
F32 = jnp.float32
BF16 = jnp.bfloat16
MiB = 1 << 20


def dot(left, right):
    return jnp.dot(left, right, preferred_element_type=F32)


def dot_nt(left, right):
    return lax.dot_general(left, right, (((1,), (1,)), ((), ())), preferred_element_type=F32)


def dot_tn(left, right):
    return lax.dot_general(left, right, (((0,), (0,)), ((), ())), preferred_element_type=F32)


def as_line(ref):
    return ref[...].reshape(1, ref.shape[0])


def as_column(row):
    return jnp.transpose(jnp.broadcast_to(row, (8, row.shape[1])))[:, 0:1]


def as_row(column):
    return jnp.transpose(jnp.broadcast_to(column, (column.shape[0], 128)))[0:8]


def halves_to_lanes(block):
    half = block.shape[0] // 2
    return jnp.concatenate([block[:half], block[half:]], axis=1)


def lanes_to_halves(block):
    return jnp.concatenate([block[:, :HEAD_DIM], block[:, HEAD_DIM:]], axis=0)


def greet(peers):
    barrier = pltpu.get_barrier_semaphore()
    for peer in peers:
        pl.semaphore_signal(barrier, inc=1, device_id=peer, device_id_type=MESH)
    pl.semaphore_wait(barrier, len(peers))


def sorted_blocks(first_case, parts):
    end = lax.select(first_case, parts[0], parts[3])
    full = lax.select(first_case, parts[3], parts[0])
    q = end.shape[0] // 4
    near = lax.select(first_case, end[:q], end[3 * q :])
    either = lax.select(first_case, end[3 * q :], end[:q])
    return [near, end[q : 3 * q], either, full, parts[1], parts[2]]


def unsorted_blocks(first_case, block):
    n = block.shape[0] // 4
    q = n // 4
    low, mid, top = block[:q], block[q : 3 * q], block[3 * q : n]
    head = lax.select(first_case, low, top)
    tail = lax.select(first_case, top, low)
    end = jnp.concatenate([head, mid, tail], axis=0)
    full = block[n : 2 * n]
    return [
        lax.select(first_case, end, full),
        block[2 * n : 3 * n],
        block[3 * n :],
        lax.select(first_case, full, end),
    ]


def either_in_long(first_case, bound, shape, axis, group):
    place = lax.broadcasted_iota(jnp.int32, shape, axis)
    row = place + jnp.where(first_case, group // 4 - 128, group - group // 4)
    past = row >= bound
    return jnp.where(first_case, past.astype(F32), 1.0 - past.astype(F32))


def front_kernel(
    n_crop,
    n_head,
    tokens, mixw_r, prow_r, crop, gain_r, bias_r, bq_r, bv_r, wqkv,
    mixed_o, normed_o, grp_o, att_o, own_o, lse_o,
    prt, mixed_s, normed_s, msg, grp, q_s, k_s, v_s, o_s, own_s, att_r,
    prt_sem, qkv_send, qkv_recv, att_send, att_recv, own_sem, out_sem,
):
    rows, width = tokens.shape
    group = rows * n_head
    local = HEADS // n_head
    c, h = lax.axis_index("crop"), lax.axis_index("head")
    far = lax.rem(c + n_crop // 2, n_crop)
    others = [lax.rem(h + o, n_head) for o in range(1, n_head)]
    greet([(far, h)] + [(c, other) for other in others])

    partner_copy = pltpu.make_async_remote_copy(
        src_ref=tokens, dst_ref=prt, send_sem=prt_sem.at[0], recv_sem=prt_sem.at[1], device_id=(far, h), device_id_type=MESH
    )
    partner_copy.start()
    mixw, prow = as_line(mixw_r), as_line(prow_r)
    gain, bias, query_bias, value_bias = [as_line(r).astype(F32) for r in (gain_r, bias_r, bq_r, bv_r)]
    share = as_column(mixw)
    chosen = lax.broadcasted_iota(jnp.int32, (rows, rows), 0) == prow
    chosen = chosen.astype(F32).astype(BF16)
    partner_copy.wait()
    step = 128
    for r in range(0, rows, step):
        part = slice(r, r + step)
        gathered = dot_tn(chosen[:, part], prt[...])
        mix = share[part] * tokens[part].astype(F32) + (1.0 - share[part]) * gathered
        mixed_s[part] = mix
        mean = jnp.mean(mix, axis=1, keepdims=True)
        centered = mix - mean
        variance = jnp.mean(centered * centered, axis=1, keepdims=True)
        normed = centered * lax.rsqrt(variance + EPS) * gain + bias
        normed_s[part] = normed.astype(BF16)
    outs = [
        pltpu.make_async_copy(mixed_s, mixed_o, out_sem.at[0]),
        pltpu.make_async_copy(normed_s, normed_o, out_sem.at[1]),
    ]
    for out in outs:
        out.start()

    qkv_copies = []
    for j in range(local):
        for d in range(n_head):
            i = d * local + j
            odd = i % 2
            base = 3 * HEAD_DIM * i - HEAD_DIM * odd
            res = dot(normed_s[...], wqkv[:, base : base + 4 * HEAD_DIM])
            res = res[:, HEAD_DIM * odd : HEAD_DIM * odd + 3 * HEAD_DIM]
            bq = query_bias[:, HEAD_DIM * i : HEAD_DIM * (i + 1)]
            bv = value_bias[:, HEAD_DIM * i : HEAD_DIM * (i + 1)]
            res = res + jnp.concatenate([bq, jnp.zeros_like(bq), bv], axis=1)
            msg[i, 0:rows] = res[:, : 2 * HEAD_DIM].astype(BF16)
            msg[i, rows : rows + rows // 2] = halves_to_lanes(res[:, 2 * HEAD_DIM :]).astype(BF16)
        batch = [pltpu.make_async_copy(msg.at[h * local + j], grp.at[j, h], own_sem.at[j])]
        for o, other in enumerate(others):
            batch.append(
                pltpu.make_async_remote_copy(
                    src_ref=msg.at[other * local + j],
                    dst_ref=grp.at[j, h],
                    send_sem=qkv_send.at[j, o],
                    recv_sem=qkv_recv.at[j, o],
                    device_id=(c, other),
                    device_id_type=MESH,
                )
            )
        for copy in batch:
            copy.start()
        qkv_copies.append(batch)

    bound = crop[0, 0]
    first_case = bound < group // 2
    quarter = rows // 4
    short, long0 = 3 * quarter, 4 * quarter
    mask_row = either_in_long(first_case, bound, (1, quarter), 1, group)
    mask_col = either_in_long(first_case, bound, (quarter, 1), 0, group)
    to_long = jnp.where(mask_row > 0.5, 0.0, NEG)
    to_short = jnp.where(mask_row > 0.5, NEG, 0.0)
    att_copies = []
    for j in range(local):
        for copy in qkv_copies[j]:
            copy.wait()
        qk = sorted_blocks(first_case, [grp[j, s, 0:rows] for s in range(n_head)])
        vv = sorted_blocks(first_case, [lanes_to_halves(grp[j, s, rows : rows + rows // 2]) for s in range(n_head)])
        at = 0
        for a, b in zip(qk, vv):
            n = a.shape[0]
            q_s[at : at + n] = a[:, :HEAD_DIM] * BF16(HEAD_DIM**-0.5)
            k_s[at : at + n] = a[:, HEAD_DIM:]
            v_s[at : at + n] = b
            at += n

        def finish(first, count, pieces, values):
            top = functools.reduce(jnp.maximum, [jnp.max(s, axis=1, keepdims=True) for s in pieces])
            total, out = 0.0, 0.0
            for s, v in zip(pieces, values):
                p = jnp.exp(s - top)
                total = total + jnp.sum(p, axis=1, keepdims=True)
                out = out + dot(p.astype(BF16), v)
            o_s[pl.ds(first, count)] = (out * (1.0 / total)).astype(BF16)
            lse_o[j, :, pl.ds(first, count)] = as_row(top + jnp.log(total))

        queries = q_s[0:short]
        finish(
            0, short,
            [dot_nt(queries, k_s[0:short]), dot_nt(queries, k_s[short:long0]) + to_short],
            [v_s[0:short], v_s[short:long0]],
        )
        queries = q_s[short:long0]
        into_long = jnp.where(mask_col > 0.5, 0.0, NEG)
        into_short = jnp.where(mask_col > 0.5, NEG, 0.0)
        finish(
            short, quarter,
            [
                dot_nt(queries, k_s[0:short]) + into_short,
                dot_nt(queries, k_s[short:long0]) + jnp.where(mask_col > 0.5, to_long, to_short),
                dot_nt(queries, k_s[long0:]) + into_long,
            ],
            [v_s[0:short], v_s[short:long0], v_s[long0:]],
        )
        tile = rows // 2

        @pl.loop(0, (group - long0) // tile)
        def _(t):
            first = pl.multiple_of(long0 + t * tile, tile)
            queries = q_s[pl.ds(first, tile)]
            finish(
                first, tile,
                [dot_nt(queries, k_s[short:long0]) + to_long, dot_nt(queries, k_s[long0:])],
                [v_s[short:long0], v_s[long0:]],
            )

        for s, block in enumerate(unsorted_blocks(first_case, o_s[...])):
            own_s[j, s] = halves_to_lanes(block)
        batch = [pltpu.make_async_copy(own_s.at[j, h], att_r.at[h * local + j], own_sem.at[j])]
        for o, other in enumerate(others):
            batch.append(
                pltpu.make_async_remote_copy(
                    src_ref=own_s.at[j, other],
                    dst_ref=att_r.at[h * local + j],
                    send_sem=att_send.at[j, o],
                    recv_sem=att_recv.at[j, o],
                    device_id=(c, other),
                    device_id_type=MESH,
                )
            )
        for copy in batch:
            copy.start()
        att_copies.append(batch)
    late = [pltpu.make_async_copy(grp, grp_o, out_sem.at[2]), pltpu.make_async_copy(own_s, own_o, out_sem.at[3])]
    for out in late:
        out.start()
    outs += late
    for batch in att_copies:
        for copy in batch:
            copy.wait()
    for p in range(HEADS // 2):
        even, odd = att_r[2 * p], att_r[2 * p + 1]
        top = jnp.concatenate([even[:, :HEAD_DIM], odd[:, :HEAD_DIM]], axis=1)
        low = jnp.concatenate([even[:, HEAD_DIM:], odd[:, HEAD_DIM:]], axis=1)
        att_o[:, 128 * p : 128 * (p + 1)] = jnp.concatenate([top, low], axis=0)
    for out in outs:
        out.wait()


def front(n_crop, n_head, tokens, mixw, prow, crop, small, wqkv):
    rows, width = tokens.shape
    group, local = rows * n_head, HEADS // n_head
    dma = pltpu.SemaphoreType.DMA
    vmem = pl.BlockSpec(memory_space=pltpu.VMEM)
    hbm = pl.BlockSpec(memory_space=pl.ANY)
    block = rows + rows // 2
    shape = jax.ShapeDtypeStruct
    return pl.pallas_call(
        functools.partial(front_kernel, n_crop, n_head),
        out_shape=(
            shape((rows, width), F32),
            shape((rows, width), BF16),
            shape((local, n_head, block, 128), BF16),
            shape((rows, width), BF16),
            shape((local, n_head, rows // 2, 128), BF16),
            shape((local, 8, group), F32),
        ),
        in_specs=[vmem, vmem, vmem, pl.BlockSpec(memory_space=pltpu.SMEM), vmem, vmem, vmem, vmem, vmem],
        out_specs=(hbm, hbm, hbm, vmem, hbm, vmem),
        scratch_shapes=[
            pltpu.VMEM((rows, width), BF16),
            pltpu.VMEM((rows, width), F32),
            pltpu.VMEM((rows, width), BF16),
            pltpu.VMEM((HEADS, block, 128), BF16),
            pltpu.VMEM((local, n_head, block, 128), BF16),
            pltpu.VMEM((group, HEAD_DIM), BF16),
            pltpu.VMEM((group, HEAD_DIM), BF16),
            pltpu.VMEM((group, HEAD_DIM), BF16),
            pltpu.VMEM((group, HEAD_DIM), BF16),
            pltpu.VMEM((local, n_head, rows // 2, 128), BF16),
            pltpu.VMEM((HEADS, rows // 2, 128), BF16),
            dma((2,)),
            dma((local, n_head - 1)),
            dma((local, n_head - 1)),
            dma((local, n_head - 1)),
            dma((local, n_head - 1)),
            dma((local,)),
            dma((4,)),
        ],
        compiler_params=pltpu.CompilerParams(collective_id=1, has_side_effects=True, vmem_limit_bytes=56 * MiB),
        cost_estimate=pl.CostEstimate(flops=10**10, bytes_accessed=2 * 10**7, transcendentals=10**7),
        name="front",
    )(tokens, mixw, prow, crop, *small, wqkv)


GELU_POLY = (0.254829592, -0.284496736, 1.421413741, -1.453152027, 1.061405429)
FC_TILE = 768
PIECE = 384


def gelu_and_slope(pre):
    bell = jnp.exp(-0.5 * pre * pre)
    t = 1.0 / (1.0 + (0.3275911 * 0.7071067811865476) * jnp.abs(pre))
    poly = GELU_POLY[4]
    for coefficient in GELU_POLY[3::-1]:
        poly = poly * t + coefficient
    tail = 0.5 * poly * t * bell
    phi = jnp.where(pre >= 0.0, 1.0 - tail, tail)
    return pre * phi, phi + pre * bell * 0.3989422804014327


def put_blocks(ref, lead, value):
    if len(ref.shape) == len(lead) + 5:
        rows = value.shape[0] // 8
        for c in range(8):
            ref[(*lead, c % 2, c // 2 % 2, c // 4)] = value[c * rows : (c + 1) * rows].astype(BF16)
    else:
        ref[lead] = value.astype(BF16)


def middle_kernel(
    cut,
    att, mixed, cot, bout_r, gain_r, bias_r, bfc2_r, bfc1_r, wout_h, w1_h, w2_h,
    layer_o, attg_o, mg_o, j1_o, j2_o, gout_o, sm_o,
    wout, w1, w2, mid_s, n2_s, n2t_s, cott_s, out_s, dn_s, pre_s, gw_s, act_s, pg_s, proj_s, b1_s, j1, j2,
    w_sem, j_sem,
):
    rows, width = cot.shape
    tiles = w1_h.shape[1] // FC_TILE
    wout_copy = pltpu.make_async_copy(wout_h, wout, w_sem.at[0, 0])
    wout_copy.start()
    w_copies = []
    for t in range(tiles):
        at = slice(t * FC_TILE, (t + 1) * FC_TILE)
        pair = (
            pltpu.make_async_copy(w1_h.at[:, at], w1.at[t], w_sem.at[1, t]),
            pltpu.make_async_copy(w2_h.at[at], w2.at[t], w_sem.at[2, t]),
        )
        for copy in pair:
            copy.start()
        w_copies.append(pair)
    sm_o[...] = jnp.zeros_like(sm_o)
    bout, gain, bias, bfc2, bfc1 = [as_line(r).astype(F32) for r in (bout_r, gain_r, bias_r, bfc2_r, bfc1_r)]
    for t in range(tiles):
        b1_s[t : t + 1, :] = bfc1[:, t * FC_TILE : (t + 1) * FC_TILE]
    cott_s[...] = jnp.transpose(cot[...])
    wout_copy.wait()
    step = 128
    mid_s[...] = mixed[...] + dot(att[...], wout[...]) + bout

    def norm2(part):
        mid = mid_s[part]
        mean = jnp.mean(mid, axis=1, keepdims=True)
        centered = mid - mean
        rstd = lax.rsqrt(jnp.mean(centered * centered, axis=1, keepdims=True) + EPS)
        return mid, centered * rstd, rstd

    total = jnp.zeros((1, width), F32)
    for r in range(0, rows, step):
        part = slice(r, r + step)
        mid, unit, _ = norm2(part)
        n2_s[part] = (unit * gain + bias).astype(BF16)
        out_s[part] = mid + bfc2
        dn_s[part] = jnp.zeros((step, width), F32)
        total = total + jnp.sum(cot[part].astype(F32), axis=0, keepdims=True)
    sm_o[7:8, :] = total
    n2t_s[...] = jnp.transpose(n2_s[...])

    @pl.loop(0, tiles)
    def _(t):
        pltpu.make_async_copy(w1.at[t], w1.at[t], w_sem.at[1, t]).wait()
        pltpu.make_async_copy(w2.at[t], w2.at[t], w_sem.at[2, t]).wait()
        pre_s[...] = dot(n2_s[...], w1[t]) + b1_s[pl.ds(t, 1), :]
        gw_s[...] = dot_nt(cot[...], w2[t])
        sums = jnp.zeros((1, FC_TILE), F32)
        for r in range(0, rows, 64):
            part = slice(r, r + 64)
            act, slope = gelu_and_slope(pre_s[part])
            act_s[part] = act.astype(BF16)
            pg = (gw_s[part] * slope).astype(BF16)
            pg_s[part] = pg
            sums = sums + jnp.sum(pg.astype(F32), axis=0, keepdims=True)
        sm_o[pl.ds(8 + t, 1), :] = sums
        out_s[...] += dot(act_s[...], w2[t])
        dn_s[...] += dot_nt(pg_s[...], w1[t])
        put_blocks(j1, (lax.rem(t, 2), lax.div(t, 2)), dot(n2t_s[...], pg_s[...]))
        g2 = dot(cott_s[...], act_s[...])
        if cut:
            for q in range(4):
                for s in range(2):
                    piece = g2[width // 4 * q : width // 4 * (q + 1), PIECE * s : PIECE * (s + 1)]
                    j2[q % 2, q // 2, s, lax.rem(t, 2), lax.div(t, 2)] = piece.astype(BF16)
        else:
            j2[lax.rem(t, 2), lax.div(t, 2)] = g2.astype(BF16)

    j_copies = [pltpu.make_async_copy(j1, j1_o, j_sem.at[0]), pltpu.make_async_copy(j2, j2_o, j_sem.at[1])]
    for copy in j_copies:
        copy.start()
    sums = [jnp.zeros((1, width), F32)] * 3
    for r in range(0, rows, step):
        part = slice(r, r + step)
        layer_o[part] = out_s[part].astype(BF16)
        _, unit, rstd = norm2(part)
        dn = dn_s[part]
        e = dn * gain
        inner = e - jnp.mean(e, axis=1, keepdims=True) - unit * jnp.mean(e * unit, axis=1, keepdims=True)
        mg = cot[part].astype(F32) + rstd * inner
        mg_o[part] = mg
        proj = mg.astype(BF16)
        proj_s[part] = proj
        for k, term in enumerate((proj.astype(F32), dn * unit, dn)):
            sums[k] = sums[k] + jnp.sum(term, axis=0, keepdims=True)
    for k in range(3):
        sm_o[4 + k : 5 + k, :] = sums[k]
    attg = dot_nt(proj_s[...], wout[...])
    for i in range(HEADS):
        attg_o[i] = halves_to_lanes(attg[:, HEAD_DIM * i : HEAD_DIM * (i + 1)]).astype(BF16)
    gout = dot_tn(att[...], proj_s[...])
    for k in range(2):
        put_blocks(gout_o, (k,), gout[:, PIECE * k : PIECE * (k + 1)])
    for copy in j_copies:
        copy.wait()


def middle(cut, att, mixed, cot, small, wout, w1, w2):
    rows, width = cot.shape
    vmem = pl.BlockSpec(memory_space=pltpu.VMEM)
    hbm = pl.BlockSpec(memory_space=pl.ANY)
    dma = pltpu.SemaphoreType.DMA
    shape = jax.ShapeDtypeStruct
    ff = w1.shape[1]
    j1_dims = (2, 2, 2, 2, 2, 96, FC_TILE) if cut else (2, 2, width, FC_TILE)
    j2_dims = (2, 2, 2, 2, 2, 192, PIECE) if cut else (2, 2, width, FC_TILE)
    gout_dims = (2, 2, 2, 2, 96, PIECE) if cut else (2, width, PIECE)
    full = lambda kind: pltpu.VMEM((rows, width), kind)
    tile = lambda kind: pltpu.VMEM((rows, FC_TILE), kind)
    return pl.pallas_call(
        functools.partial(middle_kernel, cut),
        out_shape=(
            shape((rows, width), BF16),
            shape((HEADS, rows // 2, 128), BF16),
            shape((rows, width), F32),
            shape(j1_dims, BF16),
            shape(j2_dims, BF16),
            shape(gout_dims, BF16),
            shape((16, width), F32),
        ),
        in_specs=[vmem] * 8 + [hbm] * 3,
        out_specs=(vmem, vmem, vmem, hbm, hbm, vmem, vmem),
        scratch_shapes=[
            pltpu.VMEM((width, width), BF16),
            pltpu.VMEM((ff // FC_TILE, width, FC_TILE), BF16),
            pltpu.VMEM((ff // FC_TILE, FC_TILE, width), BF16),
            full(F32), full(BF16),
            pltpu.VMEM((width, rows), BF16), pltpu.VMEM((width, rows), BF16),
            full(F32), full(F32), tile(F32), tile(F32), tile(BF16), tile(BF16), full(BF16), pltpu.VMEM((8, FC_TILE), F32),
            pltpu.VMEM(j1_dims, BF16), pltpu.VMEM(j2_dims, BF16),
            dma((3, 4)), dma((2,)),
        ],
        compiler_params=pltpu.CompilerParams(vmem_limit_bytes=60 * MiB),
        cost_estimate=pl.CostEstimate(flops=2 * 8 * 10**9, bytes_accessed=3 * 10**7, transcendentals=4 * 10**6),
        name="middle",
    )(att, mixed, cot, *small, wout, w1, w2)


class Reduction:
    AXES = ("x", "y", "lo", "hi")

    def __init__(self, acc, received, fin, send_sem, recv_sem, bits, peers, order):
        self.acc, self.received, self.fin = acc, received, fin
        self.send_sem, self.recv_sem = send_sem, recv_sem
        self.bits, self.peers, self.order = bits, peers, order

    def remote(self, k, src, dst, axis):
        return pltpu.make_async_remote_copy(
            src_ref=src, dst_ref=dst, send_sem=self.send_sem.at[k], recv_sem=self.recv_sem.at[k],
            device_id=self.peers[axis], device_id_type=MESH,
        )

    def add(self, into, received, lead, free):
        count = 1 << len(free)

        def one(i):
            place = [(i >> (len(free) - 1 - n)) & 1 if isinstance(i, int) else lax.rem(lax.div(i, 1 << (len(free) - 1 - n)), 2) for n in range(len(free))]
            index = list(lead)
            for axis, p in zip(free, place):
                index[self.AXES.index(axis)] = p
            index, place = tuple(index), tuple(place)
            into[index] = (into[index].astype(F32) + received[place].astype(F32)).astype(BF16)

        if count > 2:
            pl.loop(0, count)(one)
        else:
            for i in range(count):
                one(i)

    def steps(self, source, core_half):
        copy = self.remote(0, source, self.received[0], "core")
        copy.start()
        if core_half is not None:
            core_half.start()
        yield
        copy.wait()
        if core_half is not None:
            core_half.wait()
        self.add(self.acc, self.received[0], [None] * 4, list(self.AXES))
        lead = [slice(None)] * 4
        free = list(self.AXES)
        for k, axis in enumerate(self.order):
            at = self.AXES.index(axis)
            lead[at] = 1 - self.bits[axis]
            copy = self.remote(1 + k, self.acc.at[tuple(lead)], self.received[1 + k], axis)
            copy.start()
            lead[at] = self.bits[axis]
            free.remove(axis)
            yield
            copy.wait()
            self.add(self.acc, self.received[1 + k], lead, free)
        bc, bx = self.bits["core"], self.bits["x"]
        mine = pltpu.make_async_copy(self.acc.at[tuple(lead)], self.fin.at[bc, bx], self.send_sem.at[7])
        mine.start()
        mine.wait()
        copy = self.remote(5, self.fin.at[bc, bx], self.fin.at[bc, bx], "x")
        copy.start()
        yield
        copy.wait()
        copy = self.remote(6, self.fin.at[bc], self.fin.at[bc], "core")
        copy.start()
        yield
        copy.wait()


def tick(*jobs):
    for job in jobs:
        next(job, None)


def back_kernel(
    n_crop, n_head, cut,
    attg, grp_h, own, lse, j1_h, j2_h, gout, wqkv_h, normed_h, mixed_h, mg_h, mixw_r, prow_r, crop, gain_r, sm_in,
    *rest,
):
    (
        grad_o, f1_o, f2_o, fa_o, fb_o, sm_o,
        grp, wqkv, normed, mixed, mg_s, dor, q_s, k_s, v_s, do_s, kt_s, dz_s, zq_s, dkv_s, dq_s, di_s, msg, ret, dn_s, sent_s, back_s,
        ja, jb, load_sem, do_send, do_recv, dq_send, dq_recv, own_sem, far_sem,
        *reduce_refs,
    ) = rest
    rows, width = mixed.shape
    group = rows * n_head
    local = HEADS // n_head
    c, h = lax.axis_index("crop"), lax.axis_index("head")
    far = lax.rem(c + n_crop // 2, n_crop)
    others = [lax.rem(h + o, n_head) for o in range(1, n_head)]
    peers = [(far, h)] + [(c, other) for other in others]
    if cut:
        bits = {"core": lax.rem(h, 2), "x": lax.div(h, 2), "y": lax.rem(c, 2), "lo": lax.rem(lax.div(c, 2), 2), "hi": lax.div(c, 4)}
        near = {
            "core": (c, h + 1 - 2 * bits["core"]),
            "x": (c, h + 2 - 4 * bits["x"]),
            "y": (c + 1 - 2 * bits["y"], h),
            "lo": (c + 2 - 4 * bits["lo"], h),
            "hi": (far, h),
        }
        peers += [near["y"], near["lo"]]
    greet(peers)

    def spread(j, source, target, send_sem, recv_sem):
        copies = [pltpu.make_async_copy(source(h), target(h), own_sem.at[j])]
        for o, other in enumerate(others):
            copies.append(
                pltpu.make_async_remote_copy(
                    src_ref=source(other), dst_ref=target(h), send_sem=send_sem.at[j, o], recv_sem=recv_sem.at[j, o],
                    device_id=(c, other), device_id_type=MESH,
                )
            )
        for copy in copies:
            copy.start()
        return copies

    do_copies = [
        spread(j, lambda d, j=j: attg.at[d * local + j], lambda s, j=j: dor.at[j, s], do_send, do_recv) for j in range(local)
    ]
    loads = [
        pltpu.make_async_copy(a, b, load_sem.at[k])
        for k, (a, b) in enumerate([(grp_h, grp), (normed_h, normed), (wqkv_h, wqkv), (mixed_h, mixed), (mg_h, mg_s)])
    ]
    for load in loads:
        load.start()
    jobs = []
    if cut:
        send_sem, recv_sem, half_sem, sm_send, sm_recv, sm_r = reduce_refs[:6]
        buffers = reduce_refs[6:]
        n = len(buffers) // 4
        red = []
        orders = [("y", "x", "lo", "hi"), ("lo", "y", "hi", "x"), ("y", "lo", "hi", "x"), ("y", "x", "lo", "hi")]
        for k in range(4):
            mine = list(buffers[n * k : n * (k + 1)])
            own_half = mine.pop(0)
            acc = own_half if k < 2 else (ja, jb)[k - 2].at[bits["core"]]
            fin = (f1_o, f2_o, fa_o, fb_o)[k]
            red.append(Reduction(acc, mine[:5], fin, send_sem.at[k], recv_sem.at[k], bits, near, orders[k]))
        job1 = red[0].steps(j1_h.at[1 - bits["core"]], pltpu.make_async_copy(j1_h.at[bits["core"]], red[0].acc, half_sem.at[0]))
        job2 = red[1].steps(j2_h.at[1 - bits["core"]], pltpu.make_async_copy(j2_h.at[bits["core"]], red[1].acc, half_sem.at[1]))
        joba = red[2].steps(ja.at[1 - bits["core"]], None)
        jobb = red[3].steps(jb.at[1 - bits["core"]], None)
        for k in range(2):
            ja[k, 0] = gout[k]
        tick(job1, job2)
        plan = {
            (0, "near"): (job1, job2),
            (1, 2): (job1, job2),
            (1, "end"): (joba,),
            (2, "near"): (joba,),
            (2, 1): (job1, job2),
            (2, "end"): (joba,),
            "last": (jobb, job1, job2),
            "norm": (jobb, joba),
        }
    else:
        plan = {}
        for k in range(2):
            ja[k, 0] = gout[k]

    bound = crop[0, 0]
    first_case = bound < group // 2
    quarter = rows // 4
    short, long0 = 3 * quarter, 4 * quarter
    in_col = either_in_long(first_case, bound, (quarter, 1), 0, group) > 0.5
    in_row = either_in_long(first_case, bound, (1, quarter), 1, group) > 0.5
    col_long, col_short = jnp.where(in_col, 0.0, NEG), jnp.where(in_col, NEG, 0.0)
    row_long, row_short = jnp.where(in_row, 0.0, NEG), jnp.where(in_row, NEG, 0.0)
    lane = lax.broadcasted_iota(jnp.int32, (8, 128), 1) // HEAD_DIM
    ones = (lane == lax.broadcasted_iota(jnp.int32, (8, 128), 0)).astype(F32).astype(BF16)
    sums_q, sums_v = [None] * HEADS, [None] * HEADS
    dn_s[...] = jnp.zeros_like(dn_s)
    dq_copies = []

    def head_grads(j):
        for copy in dq_copies[j]:
            copy.wait()
        for pair in range(n_head // 2):
            packs = []
            for d in (2 * pair, 2 * pair + 1):
                i = d * local + j
                vk = ret[i, 0:rows]
                dq = lanes_to_halves(ret[i, rows : rows + rows // 2])
                dk, dv = vk[:, HEAD_DIM:], vk[:, :HEAD_DIM]
                sums_q[i] = jnp.sum(dq.astype(F32), axis=0, keepdims=True)
                sums_v[i] = jnp.sum(dv.astype(F32), axis=0, keepdims=True)
                odd = i % 2
                base = 3 * HEAD_DIM * i - HEAD_DIM * odd
                none = jnp.zeros_like(dq)
                wide = jnp.concatenate([none, dq, dk, dv] if odd else [dq, dk, dv, none], axis=1)
                dn_s[...] += dot_nt(wide, wqkv[:, base : base + 4 * HEAD_DIM])
                packs += [dq, dk, dv]
            grad = dot_tn(normed[...], jnp.concatenate(packs, axis=1))
            if j == 0:
                put_blocks(ja, (pair, 1), grad)
            else:
                put_blocks(jb, (pair, j - 1), grad)

    for j in range(local):
        for copy in do_copies[j]:
            copy.wait()
        if j == 0:
            loads[0].wait()
        rowd = []
        for s in range(n_head):
            prod = dor[j, s].astype(F32) * own[j, s].astype(F32)
            hi = prod.astype(BF16)
            d8 = dot_nt(ones, hi) + dot_nt(ones, (prod - hi.astype(F32)).astype(BF16))
            rowd.append(jnp.concatenate([d8[0:1], d8[1:2]], axis=1))
        end = lax.select(first_case, rowd[0], rowd[3])
        full = lax.select(first_case, rowd[3], rowd[0])
        ends = [end[:, quarter * k : quarter * (k + 1)] for k in range(4)]
        first, last = lax.select(first_case, ends[0], ends[3]), lax.select(first_case, ends[3], ends[0])
        di_s[0:1, :] = jnp.concatenate([first, ends[1], ends[2], last, full, rowd[1], rowd[2]], axis=1)
        qk = sorted_blocks(first_case, [grp[j, s, 0:rows] for s in range(n_head)])
        vv = sorted_blocks(first_case, [lanes_to_halves(grp[j, s, rows : rows + rows // 2]) for s in range(n_head)])
        dd = sorted_blocks(first_case, [lanes_to_halves(dor[j, s]) for s in range(n_head)])
        at = 0
        for a, b, d in zip(qk, vv, dd):
            n = a.shape[0]
            q = a[:, :HEAD_DIM] * BF16(HEAD_DIM**-0.5)
            q_s[at : at + n] = q
            k_s[at : at + n] = a[:, HEAD_DIM:]
            v_s[at : at + n] = b
            do_s[at : at + n] = d
            dz_s[at : at + n] = jnp.concatenate([d, jnp.zeros_like(d)], axis=1)
            zq_s[at : at + n] = jnp.concatenate([jnp.zeros_like(q), q], axis=1)
            at += n
        kt_s[...] = jnp.transpose(k_s[...])
        dkv_s[...] = jnp.zeros_like(dkv_s)

        def area(queries, count, pieces):
            q, do, dz, zq = q_s[queries], do_s[queries], dz_s[queries], zq_s[queries]
            lse_row, di_row = lse[j, 0:1, queries], di_s[0:1, queries]
            dqt = 0.0
            for start, number, mask in pieces:
                keys = slice(start, start + number)
                score = dot_nt(k_s[keys], q)
                if mask is not None:
                    score = score + mask
                p = jnp.exp(score - lse_row)
                ds = (p * (dot_nt(v_s[keys], do) - di_row)).astype(BF16)
                dkv_s[keys] += dot(p.astype(BF16), dz) + dot(ds, zq)
                dqt = dqt + dot(kt_s[:, keys], ds)
            dq_s[queries] = jnp.transpose(dqt * HEAD_DIM**-0.5).astype(BF16)

        area(slice(0, short), short, [(0, short, None), (short, quarter, col_short)])
        either = jnp.where(in_row, col_long, col_short)
        pieces = [(0, short, row_short), (short, quarter, either)]
        pieces += [(long0 + rows * n, rows, row_long) for n in range(n_head - 1)]
        area(slice(short, long0), quarter, pieces)
        tick(*plan.get((j, "near"), ()))
        for t in range(n_head - 1):
            pieces = [(short, quarter, col_long)] + [(long0 + rows * n, rows, None) for n in range(n_head - 1)]
            area(slice(long0 + t * rows, long0 + (t + 1) * rows), rows, pieces)
            tick(*plan.get((j, t), ()))

        dkv = unsorted_blocks(first_case, dkv_s[...])
        dqu = unsorted_blocks(first_case, dq_s[...])
        for s in range(n_head):
            msg[j, s, 0:rows] = dkv[s].astype(BF16)
            msg[j, s, rows : rows + rows // 2] = halves_to_lanes(dqu[s])
        dq_copies.append(spread(j, lambda d, j=j: msg.at[j, d], lambda s, j=j: ret.at[s * local + j], dq_send, dq_recv))
        if j == 0:
            for load in loads[1:]:
                load.wait()
        else:
            head_grads(j - 1)
        tick(*plan.get((j, "end"), ()))

    head_grads(local - 1)
    tick(*plan.get("last", ()))
    share = as_column(as_line(mixw_r))
    gain = as_line(gain_r).astype(F32)
    sums = [jnp.zeros((1, width), F32)] * 2
    scaled = []
    step = 128
    for r in range(0, rows, step):
        part = slice(r, r + step)
        mix = mixed[part]
        mean = jnp.mean(mix, axis=1, keepdims=True)
        centered = mix - mean
        rstd = lax.rsqrt(jnp.mean(centered * centered, axis=1, keepdims=True) + EPS)
        unit = centered * rstd
        dn = dn_s[part]
        e = dn * gain
        inner = e - jnp.mean(e, axis=1, keepdims=True) - unit * jnp.mean(e * unit, axis=1, keepdims=True)
        grad = mg_s[part] + rstd * inner
        sums[0] = sums[0] + jnp.sum(dn * unit, axis=0, keepdims=True)
        sums[1] = sums[1] + jnp.sum(dn, axis=0, keepdims=True)
        mixed[part] = share[part] * grad
        dn_s[part] = (1.0 - share[part]) * grad
    chosen = lax.broadcasted_iota(jnp.int32, (rows, rows), 0) == as_line(prow_r)
    chosen = chosen.astype(F32).astype(BF16)
    given = dn_s[...]
    high = given.astype(BF16)
    low = (given - high.astype(F32)).astype(BF16)
    sent_s[...] = (dot(chosen, high) + dot(chosen, low)).astype(BF16)
    far_copy = pltpu.make_async_remote_copy(
        src_ref=sent_s, dst_ref=back_s, send_sem=far_sem.at[0], recv_sem=far_sem.at[1], device_id=(far, h), device_id_type=MESH
    )
    far_copy.start()
    tick(*plan.get("norm", ()))
    sm_o[...] = sm_in[...]
    sm_o[0:1, :] = sums[0]
    sm_o[1:2, :] = sums[1]
    sm_o[2:3, :] = jnp.concatenate(sums_q, axis=1)
    sm_o[3:4, :] = jnp.concatenate(sums_v, axis=1)
    if cut:
        def small_sum():
            for k, axis in enumerate(("core", "x", "y", "lo", "hi")):
                copy = pltpu.make_async_remote_copy(
                    src_ref=sm_o, dst_ref=sm_r.at[k], send_sem=sm_send.at[k], recv_sem=sm_recv.at[k],
                    device_id=near[axis], device_id_type=MESH,
                )
                copy.start()
                yield
                copy.wait()
                sm_o[...] += sm_r[k]

        small = small_sum()
        tick(small)
        for _ in range(7):
            tick(job1, job2, joba, small, jobb)
    else:
        fa_o[...] = ja[...]
        fb_o[...] = jb[...]
    far_copy.wait()
    for r in range(0, rows, step):
        part = slice(r, r + step)
        grad_o[part] = (mixed[part] + back_s[part].astype(F32)).astype(BF16)


def back(n_crop, n_head, cut, attg, grp, own, lse, j1, j2, gout, wqkv, normed, mixed, mg, mixw, prow, crop, gain, sm):
    rows, width = mixed.shape
    group, local = rows * n_head, HEADS // n_head
    vmem = pl.BlockSpec(memory_space=pltpu.VMEM)
    hbm = pl.BlockSpec(memory_space=pl.ANY)
    smem = pl.BlockSpec(memory_space=pltpu.SMEM)
    dma = pltpu.SemaphoreType.DMA
    shape = jax.ShapeDtypeStruct
    block = rows + rows // 2
    jq_dims = (2, 2, 2, 2, 2, 96, PIECE) if cut else (2, 2, width, PIECE)
    if cut:
        finals = [(2, 2, 96, FC_TILE), (2, 2, 192, PIECE), (2, 2, 96, PIECE), (2, 2, 96, PIECE)]
    else:
        finals = [(8, 128), (8, 128), jq_dims, jq_dims]
    square = lambda n, kind: pltpu.VMEM((group, n), kind)
    scratch = [
        pltpu.VMEM((local, n_head, block, 128), BF16),
        pltpu.VMEM(wqkv.shape, BF16),
        pltpu.VMEM((rows, width), BF16),
        pltpu.VMEM((rows, width), F32),
        pltpu.VMEM((rows, width), F32),
        pltpu.VMEM((local, n_head, rows // 2, 128), BF16),
        square(HEAD_DIM, BF16), square(HEAD_DIM, BF16), square(HEAD_DIM, BF16), square(HEAD_DIM, BF16),
        pltpu.VMEM((HEAD_DIM, group), BF16),
        square(128, BF16), square(128, BF16), square(128, F32), square(HEAD_DIM, BF16),
        pltpu.VMEM((8, group), F32),
        pltpu.VMEM((local, n_head, block, 128), BF16),
        pltpu.VMEM((HEADS, block, 128), BF16),
        pltpu.VMEM((rows, width), F32),
        pltpu.VMEM((rows, width), BF16),
        pltpu.VMEM((rows, width), BF16),
        pltpu.VMEM(jq_dims, BF16),
        pltpu.VMEM(jq_dims, BF16),
        dma((5,)),
        dma((local, n_head - 1)), dma((local, n_head - 1)), dma((local, n_head - 1)), dma((local, n_head - 1)),
        dma((local,)),
        dma((2,)),
    ]
    if cut:
        scratch += [dma((4, 8)), dma((4, 8)), dma((2,)), dma((5,)), dma((5,)), pltpu.VMEM((5, 16, width), F32)]
        for k, (a, b) in enumerate([(96, FC_TILE), (192, PIECE), (96, PIECE), (96, PIECE)]):
            scratch.append(pltpu.VMEM((2, 2, 2, 2, a, b) if k < 2 else (8, 128), BF16))
            scratch += [pltpu.VMEM((2,) * n + (a, b), BF16) for n in (4, 3, 2, 1, 0)]
    return pl.pallas_call(
        functools.partial(back_kernel, n_crop, n_head, cut),
        out_shape=(shape((rows, width), BF16), *(shape(dims, BF16) for dims in finals), shape((16, width), F32)),
        in_specs=[hbm, hbm, vmem, vmem, hbm, hbm, vmem, hbm, hbm, hbm, hbm, vmem, vmem, smem, vmem, vmem],
        out_specs=(vmem,) * 6,
        scratch_shapes=scratch,
        compiler_params=pltpu.CompilerParams(collective_id=2, has_side_effects=True, vmem_limit_bytes=60 * MiB),
        cost_estimate=pl.CostEstimate(flops=2 * 10**10, bytes_accessed=3 * 10**7, transcendentals=10**7),
        name="back",
    )(attg, grp, own, lse, j1, j2, gout, wqkv, normed, mixed, mg, mixw, prow, crop, gain, sm)


def finish_kernel(n_crop, n_head, grad, f1, f2, fa, fb, sm, *outs):
    grad_o, g1_o, b1_o, gq_o, bq_o, bv_o, go_o, bo_o, g2_o, b2_o, gf1_o, bf1_o, gf2_o, bf2_o = outs
    c = lax.axis_index("crop")
    local = HEADS // n_head
    grad_o[...] = grad[...]
    for k in range(4):
        core, x = k % 2, k // 2
        gf1_o[:, FC_TILE * k : FC_TILE * (k + 1)] = f1[core, x].astype(F32)
        gf2_o[:, 192 * k : 192 * (k + 1)] = jnp.transpose(f2[core, x].astype(F32))
    for k in range(2):
        go_o[:, PIECE * k : PIECE * (k + 1)] = fa[k, 0].astype(F32)
    parts = []
    for i in range(HEADS):
        d, j = i // local, i % local
        piece = fa[d // 2, 1] if j == 0 else fb[d // 2, j - 1]
        parts.append(piece[:, 192 * (d % 2) : 192 * (d % 2 + 1)].astype(F32))
    gq_o[...] = jnp.concatenate(parts, axis=1)
    piece = jnp.zeros((16, 96), F32)
    wide = jnp.zeros((1, PIECE), F32)
    for k in range(n_crop):
        piece = lax.select(c == k, sm[:, 96 * k : 96 * (k + 1)], piece)
        wide = lax.select(c == k, sm[8 + k // 2 : 9 + k // 2, PIECE * (k % 2) : PIECE * (k % 2 + 1)], wide)
    for row, out in ((0, g1_o), (1, b1_o), (2, bq_o), (3, bv_o), (4, bo_o), (5, g2_o), (6, b2_o), (7, bf2_o)):
        out[...] = piece[row : row + 1].reshape(96)
    bf1_o[...] = wide.reshape(PIECE)


def finish(n_crop, n_head, grad, f1, f2, fa, fb, sm):
    rows, width = grad.shape
    vmem = pl.BlockSpec(memory_space=pltpu.VMEM)
    shape = jax.ShapeDtypeStruct
    short = shape((96,), F32)
    outs = (
        shape((rows, width), BF16), short, short, shape((96, 3 * width), F32), short, short, shape((96, width), F32), short,
        short, short, shape((96, 4 * width), F32), shape((PIECE,), F32), shape((PIECE, width), F32), short,
    )
    return pl.pallas_call(
        functools.partial(finish_kernel, n_crop, n_head),
        out_shape=outs,
        in_specs=[vmem] * 6,
        out_specs=(vmem,) * len(outs),
        compiler_params=pltpu.CompilerParams(vmem_limit_bytes=60 * MiB),
        name="finish",
    )(grad, f1, f2, fa, fb, sm)


def sum_everywhere(grads, small, n_crop, n_head):
    c = lax.axis_index("crop")

    def scatter(value):
        part = lax.psum_scatter(value.astype(F32), "crop", scatter_dimension=0, tiled=True)
        return lax.psum(part.astype(BF16), "head").astype(F32)

    j1, j2, ja, jb = grads
    width = j1.shape[2]
    local = HEADS // n_head
    g1 = jnp.concatenate([j1[t % 2, t // 2] for t in range(4)], axis=1)
    g2 = jnp.concatenate([j2[t % 2, t // 2] for t in range(4)], axis=1).T
    go = jnp.concatenate([ja[0, 0], ja[1, 0]], axis=1)
    parts = []
    for i in range(HEADS):
        d, j = i // local, i % local
        piece = ja[d // 2, 1] if j == 0 else jb[d // 2, j - 1]
        parts.append(piece[:, 192 * (d % 2) : 192 * (d % 2 + 1)])
    gq = jnp.concatenate(parts, axis=1)
    total = lax.psum(small, ("crop", "head"))

    def mine(vector):
        count = vector.shape[0] // n_crop
        return lax.dynamic_slice_in_dim(vector, c * count, count, 0)

    rows = [mine(total[k]) for k in range(8)]
    return [
        rows[0], rows[1], scatter(gq), rows[2], rows[3], scatter(go), rows[4], rows[5], rows[6],
        scatter(g1), mine(total[8:12].reshape(4 * width)), scatter(g2), rows[7],
    ]


def shards(
    tokens, mix_weight, partner_row, crop_lengths, ln1_gain, ln1_bias, w_qkv, b_query, b_value, w_out, b_out,
    ln2_gain, ln2_bias, w_fc1, b_fc1, w_fc2, b_fc2, cotangent,
):
    n_crop, n_head = lax.axis_size("crop"), lax.axis_size("head")
    cut = n_crop == 8 and n_head == 4
    small1, small2 = (ln1_gain, ln1_bias, b_query, b_value), (b_out, ln2_gain, ln2_bias, b_fc2, b_fc1)
    mixed, normed, grp, att, own, lse = front(n_crop, n_head, tokens, mix_weight, partner_row, crop_lengths, small1, w_qkv)
    layer_out, attg, mg, j1, j2, gout, sm = middle(cut, att, mixed, cotangent, small2, w_out, w_fc1, w_fc2)
    grad, f1, f2, fa, fb, sm = back(
        n_crop, n_head, cut, attg, grp, own, lse, j1, j2, gout, w_qkv, normed, mixed, mg, mix_weight, partner_row, crop_lengths, ln1_gain, sm
    )
    if not cut:
        return (layer_out, grad, *sum_everywhere((j1, j2, fa, fb), sm, n_crop, n_head))
    outs = finish(n_crop, n_head, grad, f1, f2, fa, fb, sm)
    return (layer_out, *outs)


def solution(mesh):
    rows, one = P(("crop", "head"), None), P(("crop", "head"))
    in_specs = (rows, one, one, P("crop", None)) + (P(),) * 13 + (rows,)
    vector, matrix = P("crop"), P("crop", None)
    out_specs = (
        rows, rows, vector, vector, matrix, vector, vector, matrix, vector, vector, vector, matrix, vector, matrix, vector,
    )
    return jax.shard_map(shards, mesh=mesh, in_specs=in_specs, out_specs=out_specs, check_vma=False)
```

```python
import functools

import jax
import jax.numpy as jnp
from jax import lax
from jax.experimental import pallas as pl
from jax.experimental.pallas import tpu as pltpu
from jax.sharding import PartitionSpec as P

HEADS = 12
HEAD_DIM = 64
EPS = 1e-06
NEG = -1e30
KEYS = 128
MESH = pl.DeviceIdType.MESH
F32 = jnp.float32
BF16 = jnp.bfloat16
MiB = 1 << 20


def dot(left, right):
    return jnp.dot(left, right, preferred_element_type=F32)


def dot_nt(left, right):
    return lax.dot_general(left, right, (((1,), (1,)), ((), ())), preferred_element_type=F32)


def dot_tn(left, right):
    return lax.dot_general(left, right, (((0,), (0,)), ((), ())), preferred_element_type=F32)


def as_line(ref):
    return ref[...].reshape(1, ref.shape[0])


def as_column(row):
    return jnp.transpose(jnp.broadcast_to(row, (8, row.shape[1])))[:, 0:1]


def as_row(column):
    return jnp.transpose(jnp.broadcast_to(column, (column.shape[0], 128)))[0:8]


def halves_to_lanes(block):
    half = block.shape[0] // 2
    return jnp.concatenate([block[:half], block[half:]], axis=1)


def lanes_to_halves(block):
    return jnp.concatenate([block[:, :HEAD_DIM], block[:, HEAD_DIM:]], axis=0)


def greet(peers):
    barrier = pltpu.get_barrier_semaphore()
    for peer in peers:
        pl.semaphore_signal(barrier, inc=1, device_id=peer, device_id_type=MESH)
    pl.semaphore_wait(barrier, len(peers))


def sorted_blocks(first_case, parts):
    end = lax.select(first_case, parts[0], parts[3])
    full = lax.select(first_case, parts[3], parts[0])
    q = end.shape[0] // 4
    near = lax.select(first_case, end[:q], end[3 * q :])
    either = lax.select(first_case, end[3 * q :], end[:q])
    return [near, end[q : 3 * q], either, full, parts[1], parts[2]]


def unsorted_blocks(first_case, block):
    n = block.shape[0] // 4
    q = n // 4
    low, mid, top = block[:q], block[q : 3 * q], block[3 * q : n]
    head = lax.select(first_case, low, top)
    tail = lax.select(first_case, top, low)
    end = jnp.concatenate([head, mid, tail], axis=0)
    full = block[n : 2 * n]
    return [
        lax.select(first_case, end, full),
        block[2 * n : 3 * n],
        block[3 * n :],
        lax.select(first_case, full, end),
    ]


def either_in_long(first_case, bound, shape, axis, group):
    place = lax.broadcasted_iota(jnp.int32, shape, axis)
    row = place + jnp.where(first_case, group // 4 - 128, group - group // 4)
    past = row >= bound
    return jnp.where(first_case, past.astype(F32), 1.0 - past.astype(F32))


def front_kernel(
    n_crop,
    n_head,
    tokens, mixw_r, prow_r, crop, gain_r, bias_r, bq_r, bv_r, wqkv,
    mixed_o, normed_o, grp_o, att_o, own_o, lse_o,
    prt, mixed_s, normed_s, msg, grp, q_s, k_s, v_s, o_s, qt_s, vt_s, ot_s, s_s, p_s, own_s, att_r,
    prt_sem, qkv_send, qkv_recv, att_send, att_recv, own_sem, out_sem,
):
    rows, width = tokens.shape
    group = rows * n_head
    local = HEADS // n_head
    c, h = lax.axis_index("crop"), lax.axis_index("head")
    far = lax.rem(c + n_crop // 2, n_crop)
    others = [lax.rem(h + o, n_head) for o in range(1, n_head)]
    greet([(far, h)] + [(c, other) for other in others])

    partner_copy = pltpu.make_async_remote_copy(
        src_ref=tokens, dst_ref=prt, send_sem=prt_sem.at[0], recv_sem=prt_sem.at[1], device_id=(far, h), device_id_type=MESH
    )
    partner_copy.start()
    mixw, prow = as_line(mixw_r), as_line(prow_r)
    gain, bias, query_bias, value_bias = [as_line(r).astype(F32) for r in (gain_r, bias_r, bq_r, bv_r)]
    share = as_column(mixw)
    chosen = lax.broadcasted_iota(jnp.int32, (rows, rows), 0) == prow
    chosen = chosen.astype(F32).astype(BF16)
    partner_copy.wait()
    step = 128
    for r in range(0, rows, step):
        part = slice(r, r + step)
        gathered = dot_tn(chosen[:, part], prt[...])
        mix = share[part] * tokens[part].astype(F32) + (1.0 - share[part]) * gathered
        mixed_s[part] = mix
        mean = jnp.mean(mix, axis=1, keepdims=True)
        centered = mix - mean
        variance = jnp.mean(centered * centered, axis=1, keepdims=True)
        normed = centered * lax.rsqrt(variance + EPS) * gain + bias
        normed_s[part] = normed.astype(BF16)
    outs = [
        pltpu.make_async_copy(mixed_s, mixed_o, out_sem.at[0]),
        pltpu.make_async_copy(normed_s, normed_o, out_sem.at[1]),
    ]
    for out in outs:
        out.start()

    qkv_copies = []
    for j in range(local):
        for d in range(n_head):
            i = d * local + j
            odd = i % 2
            base = 3 * HEAD_DIM * i - HEAD_DIM * odd
            res = dot(normed_s[...], wqkv[:, base : base + 4 * HEAD_DIM])
            res = res[:, HEAD_DIM * odd : HEAD_DIM * odd + 3 * HEAD_DIM]
            bq = query_bias[:, HEAD_DIM * i : HEAD_DIM * (i + 1)]
            bv = value_bias[:, HEAD_DIM * i : HEAD_DIM * (i + 1)]
            res = res + jnp.concatenate([bq, jnp.zeros_like(bq), bv], axis=1)
            msg[i, 0:rows] = res[:, : 2 * HEAD_DIM].astype(BF16)
            msg[i, rows : rows + rows // 2] = halves_to_lanes(res[:, 2 * HEAD_DIM :]).astype(BF16)
        batch = [pltpu.make_async_copy(msg.at[h * local + j], grp.at[j, h], own_sem.at[j])]
        for o, other in enumerate(others):
            batch.append(
                pltpu.make_async_remote_copy(
                    src_ref=msg.at[other * local + j],
                    dst_ref=grp.at[j, h],
                    send_sem=qkv_send.at[j, o],
                    recv_sem=qkv_recv.at[j, o],
                    device_id=(c, other),
                    device_id_type=MESH,
                )
            )
        for copy in batch:
            copy.start()
        qkv_copies.append(batch)

    bound = crop[0, 0]
    first_case = bound < group // 2
    quarter = rows // 4
    short, long0 = 3 * quarter, 4 * quarter
    in_col = either_in_long(first_case, bound, (quarter, 1), 0, group) > 0.5
    in_row = either_in_long(first_case, bound, (1, quarter), 1, group) > 0.5
    col_long, col_short = jnp.where(in_col, 0.0, NEG), jnp.where(in_col, NEG, 0.0)
    row_long, row_short = jnp.where(in_row, 0.0, NEG), jnp.where(in_row, NEG, 0.0)
    att_copies = []
    for j in range(local):
        for copy in qkv_copies[j]:
            copy.wait()
        qk = sorted_blocks(first_case, [grp[j, s, 0:rows] for s in range(n_head)])
        vv = sorted_blocks(first_case, [lanes_to_halves(grp[j, s, rows : rows + rows // 2]) for s in range(n_head)])
        at = 0
        for a, b in zip(qk, vv):
            n = a.shape[0]
            q_s[at : at + n] = a[:, :HEAD_DIM] * BF16(HEAD_DIM**-0.5)
            k_s[at : at + n] = a[:, HEAD_DIM:]
            v_s[at : at + n] = b
            at += n

        qt_s[...] = jnp.transpose(q_s[...])
        vt_s[...] = jnp.transpose(v_s[...])

        def area(slot, q0, count, k0, k1, masks):
            lanes = slice(q0, q0 + count)
            queries = qt_s[:, lanes]
            top = jnp.full((8, count), NEG, F32)
            for k in range(k0, k1, KEYS):
                score = dot(k_s[k : k + KEYS], queries)
                if k in masks:
                    score = score + masks[k]
                s_s[slot, k - k0 : k - k0 + KEYS, :count] = score
                top = jnp.maximum(top, jnp.max(score.reshape(KEYS // 8, 8, count), axis=0))
            top = jnp.max(top, axis=0, keepdims=True)
            total = jnp.zeros((8, count), F32)
            for k in range(k0, k1, KEYS):
                p = jnp.exp(s_s[slot, k - k0 : k - k0 + KEYS, :count] - top)
                total = total + jnp.sum(p.reshape(KEYS // 8, 8, count), axis=0)
                p_s[slot, k - k0 : k - k0 + KEYS, :count] = p.astype(BF16)
            total = jnp.sum(total, axis=0, keepdims=True)
            out = dot(vt_s[:, k0:k1], p_s[slot, : k1 - k0, :count])
            ot_s[:, lanes] = out * (1.0 / total)
            lse_o[j : j + 1, lanes] = top + jnp.log(total)

        area(0, 0, short, 0, long0, {short: col_short})
        either = {k: row_short for k in range(0, short, KEYS)}
        either[short] = jnp.where(in_row, col_long, col_short)
        either.update({k: row_long for k in range(long0, group, KEYS)})
        area(1, short, quarter, 0, group, either)
        tile = rows // 2
        for t in range((group - long0) // tile):
            area(t % 2, long0 + t * tile, tile, short, group, {short: col_long})
        o_s[...] = jnp.transpose(ot_s[...]).astype(BF16)

        for s, block in enumerate(unsorted_blocks(first_case, o_s[...])):
            own_s[j, s] = halves_to_lanes(block)
        batch = [pltpu.make_async_copy(own_s.at[j, h], att_r.at[h * local + j], own_sem.at[j])]
        for o, other in enumerate(others):
            batch.append(
                pltpu.make_async_remote_copy(
                    src_ref=own_s.at[j, other],
                    dst_ref=att_r.at[h * local + j],
                    send_sem=att_send.at[j, o],
                    recv_sem=att_recv.at[j, o],
                    device_id=(c, other),
                    device_id_type=MESH,
                )
            )
        for copy in batch:
            copy.start()
        att_copies.append(batch)
    late = [pltpu.make_async_copy(grp, grp_o, out_sem.at[2]), pltpu.make_async_copy(own_s, own_o, out_sem.at[3])]
    for out in late:
        out.start()
    outs += late
    for batch in att_copies:
        for copy in batch:
            copy.wait()
    for p in range(HEADS // 2):
        even, odd = att_r[2 * p], att_r[2 * p + 1]
        top = jnp.concatenate([even[:, :HEAD_DIM], odd[:, :HEAD_DIM]], axis=1)
        low = jnp.concatenate([even[:, HEAD_DIM:], odd[:, HEAD_DIM:]], axis=1)
        att_o[:, 128 * p : 128 * (p + 1)] = jnp.concatenate([top, low], axis=0)
    for out in outs:
        out.wait()


def front(n_crop, n_head, tokens, mixw, prow, crop, small, wqkv):
    rows, width = tokens.shape
    group, local = rows * n_head, HEADS // n_head
    dma = pltpu.SemaphoreType.DMA
    vmem = pl.BlockSpec(memory_space=pltpu.VMEM)
    hbm = pl.BlockSpec(memory_space=pl.ANY)
    block = rows + rows // 2
    shape = jax.ShapeDtypeStruct
    return pl.pallas_call(
        functools.partial(front_kernel, n_crop, n_head),
        out_shape=(
            shape((rows, width), F32),
            shape((rows, width), BF16),
            shape((local, n_head, block, 128), BF16),
            shape((rows, width), BF16),
            shape((local, n_head, rows // 2, 128), BF16),
            shape((8, group), F32),
        ),
        in_specs=[vmem, vmem, vmem, pl.BlockSpec(memory_space=pltpu.SMEM), vmem, vmem, vmem, vmem, vmem],
        out_specs=(hbm, hbm, hbm, vmem, hbm, vmem),
        scratch_shapes=[
            pltpu.VMEM((rows, width), BF16),
            pltpu.VMEM((rows, width), F32),
            pltpu.VMEM((rows, width), BF16),
            pltpu.VMEM((HEADS, block, 128), BF16),
            pltpu.VMEM((local, n_head, block, 128), BF16),
            pltpu.VMEM((group, HEAD_DIM), BF16),
            pltpu.VMEM((group, HEAD_DIM), BF16),
            pltpu.VMEM((group, HEAD_DIM), BF16),
            pltpu.VMEM((group, HEAD_DIM), BF16),
            pltpu.VMEM((HEAD_DIM, group), BF16),
            pltpu.VMEM((HEAD_DIM, group), BF16),
            pltpu.VMEM((HEAD_DIM, group), F32),
            pltpu.VMEM((2, group, 384), F32),
            pltpu.VMEM((2, group, 384), BF16),
            pltpu.VMEM((local, n_head, rows // 2, 128), BF16),
            pltpu.VMEM((HEADS, rows // 2, 128), BF16),
            dma((2,)),
            dma((local, n_head - 1)),
            dma((local, n_head - 1)),
            dma((local, n_head - 1)),
            dma((local, n_head - 1)),
            dma((local,)),
            dma((4,)),
        ],
        compiler_params=pltpu.CompilerParams(collective_id=1, has_side_effects=True, vmem_limit_bytes=56 * MiB),
        cost_estimate=pl.CostEstimate(flops=10**10, bytes_accessed=2 * 10**7, transcendentals=10**7),
        name="front",
    )(tokens, mixw, prow, crop, *small, wqkv)


GELU_POLY = (0.254829592, -0.284496736, 1.421413741, -1.453152027, 1.061405429)
FC_TILE = 768
PIECE = 384


def gelu_and_slope(pre):
    bell = jnp.exp(-0.5 * pre * pre)
    t = 1.0 / (1.0 + (0.3275911 * 0.7071067811865476) * jnp.abs(pre))
    poly = GELU_POLY[4]
    for coefficient in GELU_POLY[3::-1]:
        poly = poly * t + coefficient
    tail = 0.5 * poly * t * bell
    phi = jnp.where(pre >= 0.0, 1.0 - tail, tail)
    return pre * phi, phi + pre * bell * 0.3989422804014327


def put_blocks(ref, lead, value):
    if len(ref.shape) == len(lead) + 5:
        rows = value.shape[0] // 8
        for c in range(8):
            ref[(*lead, c % 2, c // 2 % 2, c // 4)] = value[c * rows : (c + 1) * rows].astype(BF16)
    else:
        ref[lead] = value.astype(BF16)


def middle_kernel(
    cut,
    att, mixed, cot, bout_r, gain_r, bias_r, bfc2_r, bfc1_r, wout_h, w1_h, w2_h,
    layer_o, attg_o, mg_o, jfc_o, gout_o, sm_o,
    wout, w1, w2, mid_s, n2_s, n2t_s, cott_s, out_s, dn_s, pre_s, gw_s, act_s, pg_s, proj_s, b1_s, jfc,
    w_sem, j_sem,
):
    rows, width = cot.shape
    tiles = w1_h.shape[1] // FC_TILE
    wout_copy = pltpu.make_async_copy(wout_h, wout, w_sem.at[0, 0])
    wout_copy.start()
    w_copies = []
    for t in range(tiles):
        at = slice(t * FC_TILE, (t + 1) * FC_TILE)
        pair = (
            pltpu.make_async_copy(w1_h.at[:, at], w1.at[t], w_sem.at[1, t]),
            pltpu.make_async_copy(w2_h.at[at], w2.at[t], w_sem.at[2, t]),
        )
        for copy in pair:
            copy.start()
        w_copies.append(pair)
    sm_o[...] = jnp.zeros_like(sm_o)
    bout, gain, bias, bfc2, bfc1 = [as_line(r).astype(F32) for r in (bout_r, gain_r, bias_r, bfc2_r, bfc1_r)]
    for t in range(tiles):
        b1_s[t : t + 1, :] = bfc1[:, t * FC_TILE : (t + 1) * FC_TILE]
    cott_s[...] = jnp.transpose(cot[...])
    wout_copy.wait()
    step = 128
    mid_s[...] = mixed[...] + dot(att[...], wout[...]) + bout

    def norm2(part):
        mid = mid_s[part]
        mean = jnp.mean(mid, axis=1, keepdims=True)
        centered = mid - mean
        rstd = lax.rsqrt(jnp.mean(centered * centered, axis=1, keepdims=True) + EPS)
        return mid, centered * rstd, rstd

    total = jnp.zeros((1, width), F32)
    for r in range(0, rows, step):
        part = slice(r, r + step)
        mid, unit, _ = norm2(part)
        n2_s[part] = (unit * gain + bias).astype(BF16)
        out_s[part] = mid + bfc2
        dn_s[part] = jnp.zeros((step, width), F32)
        total = total + jnp.sum(cot[part].astype(F32), axis=0, keepdims=True)
    sm_o[7:8, :] = total
    n2t_s[...] = jnp.transpose(n2_s[...])

    @pl.loop(0, tiles)
    def _(t):
        pltpu.make_async_copy(w1.at[t], w1.at[t], w_sem.at[1, t]).wait()
        pltpu.make_async_copy(w2.at[t], w2.at[t], w_sem.at[2, t]).wait()
        pre_s[...] = dot(n2_s[...], w1[t]) + b1_s[pl.ds(t, 1), :]
        gw_s[...] = dot_nt(cot[...], w2[t])
        sums = jnp.zeros((1, FC_TILE), F32)
        for r in range(0, rows, 64):
            part = slice(r, r + 64)
            act, slope = gelu_and_slope(pre_s[part])
            act_s[part] = act.astype(BF16)
            pg = (gw_s[part] * slope).astype(BF16)
            pg_s[part] = pg
            sums = sums + jnp.sum(pg.astype(F32), axis=0, keepdims=True)
        sm_o[pl.ds(8 + t, 1), :] = sums
        out_s[...] += dot(act_s[...], w2[t])
        dn_s[...] += dot_nt(pg_s[...], w1[t])
        g1 = dot(n2t_s[...], pg_s[...])
        for half in range(2):
            put_blocks(jfc, (half, lax.rem(t, 2), lax.div(t, 2)), g1[:, PIECE * half : PIECE * (half + 1)])
        g2 = dot(cott_s[...], act_s[...])
        if cut:
            for b in range(8):
                for s in range(2):
                    piece = g2[96 * b : 96 * (b + 1), PIECE * s : PIECE * (s + 1)].astype(BF16)
                    jfc[2 + b % 2, b // 2 % 2, b // 4, s, lax.rem(t, 2), lax.div(t, 2)] = piece
        else:
            for half in range(2):
                jfc[2 + half, lax.rem(t, 2), lax.div(t, 2)] = g2[:, PIECE * half : PIECE * (half + 1)].astype(BF16)

    j_copy = pltpu.make_async_copy(jfc, jfc_o, j_sem)
    j_copy.start()
    sums = [jnp.zeros((1, width), F32)] * 3
    for r in range(0, rows, step):
        part = slice(r, r + step)
        layer_o[part] = out_s[part].astype(BF16)
        _, unit, rstd = norm2(part)
        dn = dn_s[part]
        e = dn * gain
        inner = e - jnp.mean(e, axis=1, keepdims=True) - unit * jnp.mean(e * unit, axis=1, keepdims=True)
        mg = cot[part].astype(F32) + rstd * inner
        mg_o[part] = mg
        proj = mg.astype(BF16)
        proj_s[part] = proj
        for k, term in enumerate((proj.astype(F32), dn * unit, dn)):
            sums[k] = sums[k] + jnp.sum(term, axis=0, keepdims=True)
    for k in range(3):
        sm_o[4 + k : 5 + k, :] = sums[k]
    attg = dot_nt(proj_s[...], wout[...])
    for i in range(HEADS):
        attg_o[i] = halves_to_lanes(attg[:, HEAD_DIM * i : HEAD_DIM * (i + 1)]).astype(BF16)
    gout = dot_tn(att[...], proj_s[...])
    for k in range(2):
        put_blocks(gout_o, (k,), gout[:, PIECE * k : PIECE * (k + 1)])
    j_copy.wait()


def middle(cut, att, mixed, cot, small, wout, w1, w2):
    rows, width = cot.shape
    vmem = pl.BlockSpec(memory_space=pltpu.VMEM)
    hbm = pl.BlockSpec(memory_space=pl.ANY)
    dma = pltpu.SemaphoreType.DMA
    shape = jax.ShapeDtypeStruct
    ff = w1.shape[1]
    jfc_dims = (4, 2, 2, 2, 2, 2, 96, PIECE) if cut else (4, 2, 2, width, PIECE)
    gout_dims = (2, 2, 2, 2, 96, PIECE) if cut else (2, width, PIECE)
    full = lambda kind: pltpu.VMEM((rows, width), kind)
    tile = lambda kind: pltpu.VMEM((rows, FC_TILE), kind)
    return pl.pallas_call(
        functools.partial(middle_kernel, cut),
        out_shape=(
            shape((rows, width), BF16),
            shape((HEADS, rows // 2, 128), BF16),
            shape((rows, width), F32),
            shape(jfc_dims, BF16),
            shape(gout_dims, BF16),
            shape((16, width), F32),
        ),
        in_specs=[vmem] * 8 + [hbm] * 3,
        out_specs=(vmem, vmem, vmem, hbm, vmem, vmem),
        scratch_shapes=[
            pltpu.VMEM((width, width), BF16),
            pltpu.VMEM((ff // FC_TILE, width, FC_TILE), BF16),
            pltpu.VMEM((ff // FC_TILE, FC_TILE, width), BF16),
            full(F32), full(BF16),
            pltpu.VMEM((width, rows), BF16), pltpu.VMEM((width, rows), BF16),
            full(F32), full(F32), tile(F32), tile(F32), tile(BF16), tile(BF16), full(BF16), pltpu.VMEM((8, FC_TILE), F32),
            pltpu.VMEM(jfc_dims, BF16),
            dma((3, 4)), dma,
        ],
        compiler_params=pltpu.CompilerParams(vmem_limit_bytes=60 * MiB),
        cost_estimate=pl.CostEstimate(flops=2 * 8 * 10**9, bytes_accessed=3 * 10**7, transcendentals=4 * 10**6),
        name="middle",
    )(att, mixed, cot, *small, wout, w1, w2)


class Reduction:
    AXES = ("x", "y", "lo", "hi")

    def __init__(self, acc, received, fin, send_sem, recv_sem, bits, peers, order):
        self.acc, self.received, self.fin = acc, received, fin
        self.send_sem, self.recv_sem = send_sem, recv_sem
        self.bits, self.peers, self.order = bits, peers, order

    def remote(self, k, src, dst, axis):
        return pltpu.make_async_remote_copy(
            src_ref=src, dst_ref=dst, send_sem=self.send_sem.at[k], recv_sem=self.recv_sem.at[k],
            device_id=self.peers[axis], device_id_type=MESH,
        )

    def add(self, into, received, lead, free):
        count = 1 << len(free)

        def one(i):
            place = [(i >> (len(free) - 1 - n)) & 1 if isinstance(i, int) else lax.rem(lax.div(i, 1 << (len(free) - 1 - n)), 2) for n in range(len(free))]
            index = list(lead)
            for axis, p in zip(free, place):
                index[self.AXES.index(axis)] = p
            index, place = tuple(index), tuple(place)
            into[index] = (into[index].astype(F32) + received[place].astype(F32)).astype(BF16)

        if count > 2:
            pl.loop(0, count)(one)
        else:
            for i in range(count):
                one(i)

    def steps(self, source, core_half):
        copy = self.remote(0, source, self.received[0], "core")
        copy.start()
        if core_half is not None:
            core_half.start()
        yield
        copy.wait()
        if core_half is not None:
            core_half.wait()
        self.add(self.acc, self.received[0], [None] * 4, list(self.AXES))
        lead = [slice(None)] * 4
        free = list(self.AXES)
        for k, axis in enumerate(self.order):
            at = self.AXES.index(axis)
            lead[at] = 1 - self.bits[axis]
            copy = self.remote(1 + k, self.acc.at[tuple(lead)], self.received[1 + k], axis)
            copy.start()
            lead[at] = self.bits[axis]
            free.remove(axis)
            yield
            copy.wait()
            self.add(self.acc, self.received[1 + k], lead, free)
        bc, bx = self.bits["core"], self.bits["x"]
        mine = pltpu.make_async_copy(self.acc.at[tuple(lead)], self.fin.at[bc, bx], self.send_sem.at[7])
        mine.start()
        mine.wait()
        copy = self.remote(5, self.fin.at[bc, bx], self.fin.at[bc, bx], "x")
        copy.start()
        yield
        copy.wait()
        copy = self.remote(6, self.fin.at[bc], self.fin.at[bc], "core")
        copy.start()
        yield
        copy.wait()


def tick(*jobs):
    for job in jobs:
        next(job, None)


def back_kernel(
    n_crop, n_head, cut,
    attg, grp_h, own, lse, jfc_h, gout, wqkv_h, normed_h, mixed_h, mg_h, mixw_r, prow_r, crop, gain_r, sm_in,
    *rest,
):
    (
        grad_o, fin_o, sm_o,
        grp, wqkv, normed, mixed, mg_s, dor, q_s, k_s, v_s, do_s, kt_s, qt_s, dot_s, dqt_s, p_s, ds_s, dz_s, zq_s, dkv_s, dq_s, di_s, msg, ret, dn_s, sent_s, back_s,
        ja, jb, load_sem, do_send, do_recv, dq_send, dq_recv, own_sem, far_sem,
        *reduce_refs,
    ) = rest
    rows, width = mixed.shape
    group = rows * n_head
    local = HEADS // n_head
    c, h = lax.axis_index("crop"), lax.axis_index("head")
    far = lax.rem(c + n_crop // 2, n_crop)
    others = [lax.rem(h + o, n_head) for o in range(1, n_head)]
    peers = [(far, h)] + [(c, other) for other in others]
    if cut:
        bits = {"core": lax.rem(h, 2), "x": lax.div(h, 2), "y": lax.rem(c, 2), "lo": lax.rem(lax.div(c, 2), 2), "hi": lax.div(c, 4)}
        near = {
            "core": (c, h + 1 - 2 * bits["core"]),
            "x": (c, h + 2 - 4 * bits["x"]),
            "y": (c + 1 - 2 * bits["y"], h),
            "lo": (c + 2 - 4 * bits["lo"], h),
            "hi": (far, h),
        }
        peers += [near["y"], near["lo"]]
    greet(peers)

    def spread(j, source, target, send_sem, recv_sem):
        copies = [pltpu.make_async_copy(source(h), target(h), own_sem.at[j])]
        for o, other in enumerate(others):
            copies.append(
                pltpu.make_async_remote_copy(
                    src_ref=source(other), dst_ref=target(h), send_sem=send_sem.at[j, o], recv_sem=recv_sem.at[j, o],
                    device_id=(c, other), device_id_type=MESH,
                )
            )
        for copy in copies:
            copy.start()
        return copies

    do_copies = [
        spread(j, lambda d, j=j: attg.at[d * local + j], lambda s, j=j: dor.at[j, s], do_send, do_recv) for j in range(local)
    ]
    loads = [
        pltpu.make_async_copy(a, b, load_sem.at[k])
        for k, (a, b) in enumerate([(grp_h, grp), (normed_h, normed), (wqkv_h, wqkv), (mixed_h, mixed), (mg_h, mg_s)])
    ]
    loads += [pltpu.make_async_copy(gout.at[k], ja.at[k, 0], load_sem.at[5 + k]) for k in range(2)]
    for load in loads:
        load.start()
    jobs, plan = [], {}
    if cut:
        send_sem, recv_sem, half_sem, sm_send, sm_recv, sm_r, acc_s, *received = reduce_refs
        orders = [("y", "lo", "x", "hi"), ("lo", "y", "x", "hi")] * 2 + [("y", "lo", "x", "hi"), ("y", "x", "lo", "hi")]
        for k in range(6):
            acc = acc_s.at[k] if k < 4 else (ja, jb)[k - 4].at[bits["core"]]
            red = Reduction(acc, [r.at[k] for r in received], fin_o.at[k], send_sem.at[k], recv_sem.at[k], bits, near, orders[k])
            if k < 4:
                keep = pltpu.make_async_copy(jfc_h.at[k, bits["core"]], acc, half_sem.at[k])
                jobs.append(red.steps(jfc_h.at[k, 1 - bits["core"]], keep))
            else:
                jobs.append(red.steps((ja, jb)[k - 4].at[1 - bits["core"]], None))
        fc1, fc2, fc3, fc4, joba, jobb = jobs
        tick(fc1, fc2, fc3, fc4)
        plan = {
            (0, "first"): (fc1, fc2),
            (0, 5): (fc1, fc2, fc3, fc4),
            (1, "end"): (joba,),
            (1, 5): (fc1, fc2),
            (2, 0): (fc1, fc2),
            (2, 3): (fc1, fc2, fc3, fc4),
            (2, 5): (joba,),
            "last": (fc3, fc4, jobb, fc1, fc2),
        }

    bound = crop[0, 0]
    first_case = bound < group // 2
    quarter = rows // 4
    short, long0 = 3 * quarter, 4 * quarter
    in_col = either_in_long(first_case, bound, (quarter, 1), 0, group) > 0.5
    in_row = either_in_long(first_case, bound, (1, quarter), 1, group) > 0.5
    col_long, col_short = jnp.where(in_col, 0.0, NEG), jnp.where(in_col, NEG, 0.0)
    row_long, row_short = jnp.where(in_row, 0.0, NEG), jnp.where(in_row, NEG, 0.0)
    lane = lax.broadcasted_iota(jnp.int32, (8, 128), 1) // HEAD_DIM
    ones = (lane == lax.broadcasted_iota(jnp.int32, (8, 128), 0)).astype(F32).astype(BF16)
    sums_q, sums_v = [None] * HEADS, [None] * HEADS
    dn_s[...] = jnp.zeros_like(dn_s)
    dq_copies = []

    def head_grads(j):
        for copy in dq_copies[j]:
            copy.wait()
        for pair in range(n_head // 2):
            packs = []
            for d in (2 * pair, 2 * pair + 1):
                i = d * local + j
                vk = ret[i, 0:rows]
                dq = lanes_to_halves(ret[i, rows : rows + rows // 2])
                dk, dv = vk[:, HEAD_DIM:], vk[:, :HEAD_DIM]
                sums_q[i] = jnp.sum(dq.astype(F32), axis=0, keepdims=True)
                sums_v[i] = jnp.sum(dv.astype(F32), axis=0, keepdims=True)
                odd = i % 2
                base = 3 * HEAD_DIM * i - HEAD_DIM * odd
                none = jnp.zeros_like(dq)
                wide = jnp.concatenate([none, dq, dk, dv] if odd else [dq, dk, dv, none], axis=1)
                dn_s[...] += dot_nt(wide, wqkv[:, base : base + 4 * HEAD_DIM])
                packs += [dq, dk, dv]
            grad = dot_tn(normed[...], jnp.concatenate(packs, axis=1))
            if j == 0:
                put_blocks(ja, (pair, 1), grad)
            else:
                put_blocks(jb, (pair, j - 1), grad)

    for j in range(local):
        for copy in do_copies[j]:
            copy.wait()
        if j == 0:
            loads[0].wait()
            tick(*plan.get((0, "first"), ()))
        rowd = []
        for s in range(n_head):
            prod = dor[j, s].astype(F32) * own[j, s].astype(F32)
            hi = prod.astype(BF16)
            d8 = dot_nt(ones, hi) + dot_nt(ones, (prod - hi.astype(F32)).astype(BF16))
            rowd.append(jnp.concatenate([d8[0:1], d8[1:2]], axis=1))
        end = lax.select(first_case, rowd[0], rowd[3])
        full = lax.select(first_case, rowd[3], rowd[0])
        ends = [end[:, quarter * k : quarter * (k + 1)] for k in range(4)]
        first, last = lax.select(first_case, ends[0], ends[3]), lax.select(first_case, ends[3], ends[0])
        di_s[0:1, :] = jnp.concatenate([first, ends[1], ends[2], last, full, rowd[1], rowd[2]], axis=1)
        qk = sorted_blocks(first_case, [grp[j, s, 0:rows] for s in range(n_head)])
        vv = sorted_blocks(first_case, [lanes_to_halves(grp[j, s, rows : rows + rows // 2]) for s in range(n_head)])
        dd = sorted_blocks(first_case, [lanes_to_halves(dor[j, s]) for s in range(n_head)])
        at = 0
        for a, b, d in zip(qk, vv, dd):
            n = a.shape[0]
            q = a[:, :HEAD_DIM] * BF16(HEAD_DIM**-0.5)
            q_s[at : at + n] = q
            k_s[at : at + n] = a[:, HEAD_DIM:]
            v_s[at : at + n] = b
            do_s[at : at + n] = d
            dz_s[at : at + n] = jnp.concatenate([d, jnp.zeros_like(d)], axis=1)
            zq_s[at : at + n] = jnp.concatenate([jnp.zeros_like(q), q], axis=1)
            at += n
        kt_s[...] = jnp.transpose(k_s[...])
        qt_s[...] = jnp.transpose(q_s[...])
        dot_s[...] = jnp.transpose(do_s[...])
        dkv_s[...] = jnp.zeros_like(dkv_s)

        def area(slot, q0, count, tile, k0, k1, masks):
            for at in range(0, count, tile):
                lanes = slice(q0 + at, q0 + at + tile)
                queries, grads = qt_s[:, lanes], dot_s[:, lanes]
                lse_row, di_row = lse[j : j + 1, lanes], di_s[0:1, lanes]
                for k in range(k0, k1, KEYS):
                    keys = slice(k, k + KEYS)
                    score = dot(k_s[keys], queries)
                    if k in masks:
                        score = score + masks[k]
                    p = jnp.exp(score - lse_row)
                    ds = p * (dot(v_s[keys], grads) - di_row)
                    place = (slot, slice(k - k0, k - k0 + KEYS), slice(at, at + tile))
                    p_s[place] = p.astype(BF16)
                    ds_s[place] = ds.astype(BF16)
            queries, number = slice(q0, q0 + count), k1 - k0
            dkv_s[k0:k1] += dot(p_s[slot, :number, :count], dz_s[queries]) + dot(ds_s[slot, :number, :count], zq_s[queries])
            dqt_s[:, queries] = dot(kt_s[:, k0:k1], ds_s[slot, :number, :count])

        tile = rows // 2
        area(0, 0, tile, tile, 0, long0, {short: col_short})
        area(1, tile, short - tile, short - tile, 0, long0, {short: col_short})
        either = {k: row_short for k in range(0, short, KEYS)}
        either[short] = jnp.where(in_row, col_long, col_short)
        either.update({k: row_long for k in range(long0, group, KEYS)})
        area(0, short, quarter, quarter, 0, group, either)
        tick(*plan.get((j, "near"), ()))
        for t in range(n_head - 1):
            for half in range(2):
                area(1 - half, long0 + t * rows + half * tile, tile, tile, short, group, {short: col_long})
                tick(*plan.get((j, 2 * t + half), ()))
        dq_s[...] = jnp.transpose(dqt_s[...] * HEAD_DIM**-0.5).astype(BF16)

        dkv = unsorted_blocks(first_case, dkv_s[...])
        dqu = unsorted_blocks(first_case, dq_s[...])
        for s in range(n_head):
            msg[j, s, 0:rows] = dkv[s].astype(BF16)
            msg[j, s, rows : rows + rows // 2] = halves_to_lanes(dqu[s])
        dq_copies.append(spread(j, lambda d, j=j: msg.at[j, d], lambda s, j=j: ret.at[s * local + j], dq_send, dq_recv))
        if j == 0:
            for load in loads[1:]:
                load.wait()
        else:
            head_grads(j - 1)
        tick(*plan.get((j, "end"), ()))

    head_grads(local - 1)
    tick(*plan.get("last", ()))
    share = as_column(as_line(mixw_r))
    gain = as_line(gain_r).astype(F32)
    sums = [jnp.zeros((1, width), F32)] * 2
    scaled = []
    step = 128
    for r in range(0, rows, step):
        part = slice(r, r + step)
        mix = mixed[part]
        mean = jnp.mean(mix, axis=1, keepdims=True)
        centered = mix - mean
        rstd = lax.rsqrt(jnp.mean(centered * centered, axis=1, keepdims=True) + EPS)
        unit = centered * rstd
        dn = dn_s[part]
        e = dn * gain
        inner = e - jnp.mean(e, axis=1, keepdims=True) - unit * jnp.mean(e * unit, axis=1, keepdims=True)
        grad = mg_s[part] + rstd * inner
        sums[0] = sums[0] + jnp.sum(dn * unit, axis=0, keepdims=True)
        sums[1] = sums[1] + jnp.sum(dn, axis=0, keepdims=True)
        mixed[part] = share[part] * grad
        dn_s[part] = (1.0 - share[part]) * grad
    chosen = lax.broadcasted_iota(jnp.int32, (rows, rows), 0) == as_line(prow_r)
    chosen = chosen.astype(F32).astype(BF16)
    given = dn_s[...]
    high = given.astype(BF16)
    low = (given - high.astype(F32)).astype(BF16)
    sent_s[...] = (dot(chosen, high) + dot(chosen, low)).astype(BF16)
    far_copy = pltpu.make_async_remote_copy(
        src_ref=sent_s, dst_ref=back_s, send_sem=far_sem.at[0], recv_sem=far_sem.at[1], device_id=(far, h), device_id_type=MESH
    )
    far_copy.start()
    sm_o[...] = sm_in[...]
    sm_o[0:1, :] = sums[0]
    sm_o[1:2, :] = sums[1]
    sm_o[2:3, :] = jnp.concatenate(sums_q, axis=1)
    sm_o[3:4, :] = jnp.concatenate(sums_v, axis=1)
    if cut:
        def small_sum():
            for k, axis in enumerate(("core", "x", "y", "lo", "hi")):
                copy = pltpu.make_async_remote_copy(
                    src_ref=sm_o, dst_ref=sm_r.at[k], send_sem=sm_send.at[k], recv_sem=sm_recv.at[k],
                    device_id=near[axis], device_id_type=MESH,
                )
                copy.start()
                yield
                copy.wait()
                sm_o[...] += sm_r[k]

        small = small_sum()
        tick(small, jobb, fc3, fc4, fc1, fc2, small, joba, small)
        tick(fc3, fc4, joba, small, jobb, joba, fc3, fc4, small, jobb, joba, fc3, fc4, small, jobb, joba, jobb, joba, jobb, jobb)
    else:
        fin_o[0] = ja[...]
        fin_o[1] = jb[...]
    far_copy.wait()
    for r in range(0, rows, step):
        part = slice(r, r + step)
        grad_o[part] = (mixed[part] + back_s[part].astype(F32)).astype(BF16)


def back(n_crop, n_head, cut, attg, grp, own, lse, jfc, gout, wqkv, normed, mixed, mg, mixw, prow, crop, gain, sm):
    rows, width = mixed.shape
    group, local = rows * n_head, HEADS // n_head
    vmem = pl.BlockSpec(memory_space=pltpu.VMEM)
    hbm = pl.BlockSpec(memory_space=pl.ANY)
    smem = pl.BlockSpec(memory_space=pltpu.SMEM)
    dma = pltpu.SemaphoreType.DMA
    shape = jax.ShapeDtypeStruct
    block = rows + rows // 2
    jq_dims = (2, 2, 2, 2, 2, 96, PIECE) if cut else (2, 2, width, PIECE)
    finals = (6, 2, 2, 96, PIECE) if cut else (2, *jq_dims)
    square = lambda n, kind: pltpu.VMEM((group, n), kind)
    scratch = [
        pltpu.VMEM((local, n_head, block, 128), BF16),
        pltpu.VMEM(wqkv.shape, BF16),
        pltpu.VMEM((rows, width), BF16),
        pltpu.VMEM((rows, width), F32),
        pltpu.VMEM((rows, width), F32),
        pltpu.VMEM((local, n_head, rows // 2, 128), BF16),
        square(HEAD_DIM, BF16), square(HEAD_DIM, BF16), square(HEAD_DIM, BF16), square(HEAD_DIM, BF16),
        pltpu.VMEM((HEAD_DIM, group), BF16), pltpu.VMEM((HEAD_DIM, group), BF16), pltpu.VMEM((HEAD_DIM, group), BF16),
        pltpu.VMEM((HEAD_DIM, group), F32), pltpu.VMEM((2, group, rows // 2), BF16), pltpu.VMEM((2, group, rows // 2), BF16),
        square(128, BF16), square(128, BF16), square(128, F32), square(HEAD_DIM, BF16),
        pltpu.VMEM((8, group), F32),
        pltpu.VMEM((local, n_head, block, 128), BF16),
        pltpu.VMEM((HEADS, block, 128), BF16),
        pltpu.VMEM((rows, width), F32),
        pltpu.VMEM((rows, width), BF16),
        pltpu.VMEM((rows, width), BF16),
        pltpu.VMEM(jq_dims, BF16),
        pltpu.VMEM(jq_dims, BF16),
        dma((7,)),
        dma((local, n_head - 1)), dma((local, n_head - 1)), dma((local, n_head - 1)), dma((local, n_head - 1)),
        dma((local,)),
        dma((2,)),
    ]
    if cut:
        scratch += [dma((6, 8)), dma((6, 8)), dma((4,)), dma((5,)), dma((5,)), pltpu.VMEM((5, 16, width), F32)]
        scratch.append(pltpu.VMEM((4, 2, 2, 2, 2, 96, PIECE), BF16))
        scratch += [pltpu.VMEM((6,) + (2,) * n + (96, PIECE), BF16) for n in (4, 3, 2, 1, 0)]
    return pl.pallas_call(
        functools.partial(back_kernel, n_crop, n_head, cut),
        out_shape=(shape((rows, width), BF16), shape(finals, BF16), shape((16, width), F32)),
        in_specs=[hbm, hbm, vmem, vmem, hbm, hbm, hbm, hbm, hbm, hbm, vmem, vmem, smem, vmem, vmem],
        out_specs=(vmem,) * 3,
        scratch_shapes=scratch,
        compiler_params=pltpu.CompilerParams(collective_id=2, has_side_effects=True, vmem_limit_bytes=60 * MiB),
        cost_estimate=pl.CostEstimate(flops=2 * 10**10, bytes_accessed=3 * 10**7, transcendentals=10**7),
        name="back",
    )(attg, grp, own, lse, jfc, gout, wqkv, normed, mixed, mg, mixw, prow, crop, gain, sm)


def finish_kernel(n_crop, n_head, grad, fin, sm, *outs):
    grad_o, g1_o, b1_o, gq_o, bq_o, bv_o, go_o, bo_o, g2_o, b2_o, gf1_o, bf1_o, gf2_o, bf2_o = outs
    c = lax.axis_index("crop")
    local = HEADS // n_head
    grad_o[...] = grad[...]
    parts = []
    for k in range(4):
        core, x = k % 2, k // 2
        for half in range(2):
            at = FC_TILE * k + PIECE * half
            gf1_o[:, at : at + PIECE] = fin[half, core, x].astype(F32)
        both = jnp.concatenate([fin[2, core, x], fin[3, core, x]], axis=0)
        parts.append(jnp.transpose(both.astype(F32)))
    gf2_o[...] = jnp.concatenate(parts, axis=1)
    for k in range(2):
        go_o[:, PIECE * k : PIECE * (k + 1)] = fin[4, k, 0].astype(F32)
    parts = []
    for i in range(HEADS):
        d, j = i // local, i % local
        piece = fin[4, d // 2, 1] if j == 0 else fin[5, d // 2, j - 1]
        parts.append(piece[:, 192 * (d % 2) : 192 * (d % 2 + 1)].astype(F32))
    gq_o[...] = jnp.concatenate(parts, axis=1)
    piece = jnp.zeros((16, 96), F32)
    wide = jnp.zeros((1, PIECE), F32)
    for k in range(n_crop):
        piece = lax.select(c == k, sm[:, 96 * k : 96 * (k + 1)], piece)
        wide = lax.select(c == k, sm[8 + k // 2 : 9 + k // 2, PIECE * (k % 2) : PIECE * (k % 2 + 1)], wide)
    for row, out in ((0, g1_o), (1, b1_o), (2, bq_o), (3, bv_o), (4, bo_o), (5, g2_o), (6, b2_o), (7, bf2_o)):
        out[...] = piece[row : row + 1].reshape(96)
    bf1_o[...] = wide.reshape(PIECE)


def finish(n_crop, n_head, grad, fin, sm):
    rows, width = grad.shape
    vmem = pl.BlockSpec(memory_space=pltpu.VMEM)
    shape = jax.ShapeDtypeStruct
    short = shape((96,), F32)
    outs = (
        shape((rows, width), BF16), short, short, shape((96, 3 * width), F32), short, short, shape((96, width), F32), short,
        short, short, shape((96, 4 * width), F32), shape((PIECE,), F32), shape((PIECE, width), F32), short,
    )
    return pl.pallas_call(
        functools.partial(finish_kernel, n_crop, n_head),
        out_shape=outs,
        in_specs=[vmem] * 3,
        out_specs=(vmem,) * len(outs),
        compiler_params=pltpu.CompilerParams(vmem_limit_bytes=60 * MiB),
        name="finish",
    )(grad, fin, sm)


def sum_everywhere(grads, small, n_crop, n_head):
    c = lax.axis_index("crop")

    def scatter(value):
        part = lax.psum_scatter(value.astype(F32), "crop", scatter_dimension=0, tiled=True)
        return lax.psum(part.astype(BF16), "head").astype(F32)

    jfc, ja, jb = grads
    width = jfc.shape[3]
    local = HEADS // n_head
    g1 = jnp.concatenate([jfc[half, t % 2, t // 2] for t in range(4) for half in range(2)], axis=1)
    g2 = jnp.concatenate([jfc[2 + half, t % 2, t // 2] for t in range(4) for half in range(2)], axis=1).T
    go = jnp.concatenate([ja[0, 0], ja[1, 0]], axis=1)
    parts = []
    for i in range(HEADS):
        d, j = i // local, i % local
        piece = ja[d // 2, 1] if j == 0 else jb[d // 2, j - 1]
        parts.append(piece[:, 192 * (d % 2) : 192 * (d % 2 + 1)])
    gq = jnp.concatenate(parts, axis=1)
    total = lax.psum(small, ("crop", "head"))

    def mine(vector):
        count = vector.shape[0] // n_crop
        return lax.dynamic_slice_in_dim(vector, c * count, count, 0)

    rows = [mine(total[k]) for k in range(8)]
    return [
        rows[0], rows[1], scatter(gq), rows[2], rows[3], scatter(go), rows[4], rows[5], rows[6],
        scatter(g1), mine(total[8:12].reshape(4 * width)), scatter(g2), rows[7],
    ]


def shards(
    tokens, mix_weight, partner_row, crop_lengths, ln1_gain, ln1_bias, w_qkv, b_query, b_value, w_out, b_out,
    ln2_gain, ln2_bias, w_fc1, b_fc1, w_fc2, b_fc2, cotangent,
):
    n_crop, n_head = lax.axis_size("crop"), lax.axis_size("head")
    cut = n_crop == 8 and n_head == 4
    small1, small2 = (ln1_gain, ln1_bias, b_query, b_value), (b_out, ln2_gain, ln2_bias, b_fc2, b_fc1)
    mixed, normed, grp, att, own, lse = front(n_crop, n_head, tokens, mix_weight, partner_row, crop_lengths, small1, w_qkv)
    layer_out, attg, mg, jfc, gout, sm = middle(cut, att, mixed, cotangent, small2, w_out, w_fc1, w_fc2)
    grad, fin, sm = back(
        n_crop, n_head, cut, attg, grp, own, lse, jfc, gout, w_qkv, normed, mixed, mg, mix_weight, partner_row, crop_lengths, ln1_gain, sm
    )
    if not cut:
        return (layer_out, grad, *sum_everywhere((jfc, fin[0], fin[1]), sm, n_crop, n_head))
    outs = finish(n_crop, n_head, grad, fin, sm)
    return (layer_out, *outs)


def solution(mesh):
    rows, one = P(("crop", "head"), None), P(("crop", "head"))
    in_specs = (rows, one, one, P("crop", None)) + (P(),) * 13 + (rows,)
    vector, matrix = P("crop"), P("crop", None)
    out_specs = (
        rows, rows, vector, vector, matrix, vector, vector, matrix, vector, vector, vector, matrix, vector, matrix, vector,
    )
    return jax.shard_map(shards, mesh=mesh, in_specs=in_specs, out_specs=out_specs, check_vma=False)
```

```python
import functools

import jax
import jax.numpy as jnp
from jax import lax
from jax.experimental import pallas as pl
from jax.experimental.pallas import tpu as pltpu
from jax.sharding import PartitionSpec as P

HEADS = 12
HEAD_DIM = 64
EPS = 1e-06
NEG = -1e30
KEYS = 64
LANES = 256
MESH = pl.DeviceIdType.MESH
F32 = jnp.float32
BF16 = jnp.bfloat16
MiB = 1 << 20


def dot(left, right):
    return jnp.dot(left, right, preferred_element_type=F32)


def dot_nt(left, right):
    return lax.dot_general(left, right, (((1,), (1,)), ((), ())), preferred_element_type=F32)


def dot_tn(left, right):
    return lax.dot_general(left, right, (((0,), (0,)), ((), ())), preferred_element_type=F32)


def as_line(ref):
    return ref[...].reshape(1, ref.shape[0])


def as_column(row):
    return jnp.transpose(jnp.broadcast_to(row, (8, row.shape[1])))[:, 0:1]


def as_row(column):
    return jnp.transpose(jnp.broadcast_to(column, (column.shape[0], 128)))[0:8]


def halves_to_lanes(block):
    half = block.shape[0] // 2
    return jnp.concatenate([block[:half], block[half:]], axis=1)


def lanes_to_halves(block):
    return jnp.concatenate([block[:, :HEAD_DIM], block[:, HEAD_DIM:]], axis=0)


def greet(peers):
    barrier = pltpu.get_barrier_semaphore()
    for peer in peers:
        pl.semaphore_signal(barrier, inc=1, device_id=peer, device_id_type=MESH)
    pl.semaphore_wait(barrier, len(peers))


def sorted_blocks(first_case, parts):
    end = lax.select(first_case, parts[0], parts[3])
    full = lax.select(first_case, parts[3], parts[0])
    q = end.shape[0] // 4
    near = lax.select(first_case, end[:q], end[3 * q :])
    either = lax.select(first_case, end[3 * q :], end[:q])
    return [near, end[q : 3 * q], either, full, parts[1], parts[2]]


def unsorted_blocks(first_case, block):
    n = block.shape[0] // 4
    q = n // 4
    low, mid, top = block[:q], block[q : 3 * q], block[3 * q : n]
    head = lax.select(first_case, low, top)
    tail = lax.select(first_case, top, low)
    end = jnp.concatenate([head, mid, tail], axis=0)
    full = block[n : 2 * n]
    return [
        lax.select(first_case, end, full),
        block[2 * n : 3 * n],
        block[3 * n :],
        lax.select(first_case, full, end),
    ]


def either_in_long(first_case, bound, shape, axis, group):
    place = lax.broadcasted_iota(jnp.int32, shape, axis)
    row = place + jnp.where(first_case, group // 4 - 128, group - group // 4)
    past = row >= bound
    return jnp.where(first_case, past.astype(F32), 1.0 - past.astype(F32))


def front_kernel(
    n_crop,
    n_head,
    tokens, mixw_r, prow_r, crop, gain_r, bias_r, bq_r, bv_r, wqkv,
    mixed_o, normed_o, grp_o, att_o, own_o, lse_o,
    prt, mixed_s, normed_s, msg, grp, q_s, k_s, v_s, o_s, qt_s, vt_s, ot_s, s_s, p_s, tot_s, own_s, att_r,
    prt_sem, qkv_send, qkv_recv, att_send, att_recv, own_sem, out_sem,
):
    rows, width = tokens.shape
    group = rows * n_head
    local = HEADS // n_head
    c, h = lax.axis_index("crop"), lax.axis_index("head")
    far = lax.rem(c + n_crop // 2, n_crop)
    others = [lax.rem(h + o, n_head) for o in range(1, n_head)]
    greet([(far, h)] + [(c, other) for other in others])

    partner_copy = pltpu.make_async_remote_copy(
        src_ref=tokens, dst_ref=prt, send_sem=prt_sem.at[0], recv_sem=prt_sem.at[1], device_id=(far, h), device_id_type=MESH
    )
    partner_copy.start()
    mixw, prow = as_line(mixw_r), as_line(prow_r)
    gain, bias, query_bias, value_bias = [as_line(r).astype(F32) for r in (gain_r, bias_r, bq_r, bv_r)]
    share = as_column(mixw)
    chosen = lax.broadcasted_iota(jnp.int32, (rows, rows), 0) == prow
    chosen = chosen.astype(F32).astype(BF16)
    partner_copy.wait()
    step = 128
    for r in range(0, rows, step):
        part = slice(r, r + step)
        gathered = dot_tn(chosen[:, part], prt[...])
        mix = share[part] * tokens[part].astype(F32) + (1.0 - share[part]) * gathered
        mixed_s[part] = mix
        mean = jnp.mean(mix, axis=1, keepdims=True)
        centered = mix - mean
        variance = jnp.mean(centered * centered, axis=1, keepdims=True)
        normed = centered * lax.rsqrt(variance + EPS) * gain + bias
        normed_s[part] = normed.astype(BF16)
    outs = [
        pltpu.make_async_copy(mixed_s, mixed_o, out_sem.at[0]),
        pltpu.make_async_copy(normed_s, normed_o, out_sem.at[1]),
    ]
    for out in outs:
        out.start()

    qkv_copies = []
    for j in range(local):
        for d in range(n_head):
            i = d * local + j
            odd = i % 2
            base = 3 * HEAD_DIM * i - HEAD_DIM * odd
            res = dot(normed_s[...], wqkv[:, base : base + 4 * HEAD_DIM])
            res = res[:, HEAD_DIM * odd : HEAD_DIM * odd + 3 * HEAD_DIM]
            bq = query_bias[:, HEAD_DIM * i : HEAD_DIM * (i + 1)]
            bv = value_bias[:, HEAD_DIM * i : HEAD_DIM * (i + 1)]
            res = res + jnp.concatenate([bq, jnp.zeros_like(bq), bv], axis=1)
            msg[i, 0:rows] = res[:, : 2 * HEAD_DIM].astype(BF16)
            msg[i, rows : rows + rows // 2] = halves_to_lanes(res[:, 2 * HEAD_DIM :]).astype(BF16)
        batch = [pltpu.make_async_copy(msg.at[h * local + j], grp.at[j, h], own_sem.at[j])]
        for o, other in enumerate(others):
            batch.append(
                pltpu.make_async_remote_copy(
                    src_ref=msg.at[other * local + j],
                    dst_ref=grp.at[j, h],
                    send_sem=qkv_send.at[j, o],
                    recv_sem=qkv_recv.at[j, o],
                    device_id=(c, other),
                    device_id_type=MESH,
                )
            )
        for copy in batch:
            copy.start()
        qkv_copies.append(batch)

    bound = crop[0, 0]
    first_case = bound < group // 2
    quarter = rows // 4
    short, long0 = 3 * quarter, 4 * quarter
    in_col = either_in_long(first_case, bound, (quarter, 1), 0, group) > 0.5
    in_row = either_in_long(first_case, bound, (1, quarter), 1, group) > 0.5
    col_long, col_short = jnp.where(in_col, 0.0, NEG), jnp.where(in_col, NEG, 0.0)
    row_long, row_short = jnp.where(in_row, 0.0, NEG), jnp.where(in_row, NEG, 0.0)
    att_copies = []
    for j in range(local):
        for copy in qkv_copies[j]:
            copy.wait()
        qk = sorted_blocks(first_case, [grp[j, s, 0:rows] for s in range(n_head)])
        vv = sorted_blocks(first_case, [lanes_to_halves(grp[j, s, rows : rows + rows // 2]) for s in range(n_head)])
        at = 0
        for a, b in zip(qk, vv):
            n = a.shape[0]
            q_s[at : at + n] = a[:, :HEAD_DIM] * BF16(HEAD_DIM**-0.5)
            k_s[at : at + n] = a[:, HEAD_DIM:]
            v_s[at : at + n] = b
            at += n

        qt_s[...] = jnp.transpose(q_s[...])
        vt_s[...] = jnp.transpose(v_s[...])

        def area(slot, q0, count, k0, k1, masks):
            lanes, number = slice(q0, q0 + count), k1 - k0
            s_s[slot, :number, :count] = dot(k_s[k0:k1], qt_s[:, lanes])
            for k, mask in masks.items():
                s_s[slot, k - k0 : k - k0 + quarter, :count] += mask
            for at in range(0, count, LANES):
                wide = min(LANES, count - at)
                here = slice(at, at + wide)
                top = jnp.full((8, wide), NEG, F32)
                for k in range(0, number, KEYS):
                    top = jnp.maximum(top, jnp.max(s_s[slot, k : k + KEYS, here].reshape(KEYS // 8, 8, wide), axis=0))
                top = jnp.max(top, axis=0, keepdims=True)
                total = jnp.zeros((8, wide), F32)
                for k in range(0, number, KEYS):
                    p = jnp.exp(s_s[slot, k : k + KEYS, here] - top)
                    total = total + jnp.sum(p.reshape(KEYS // 8, 8, wide), axis=0)
                    p_s[slot, k : k + KEYS, here] = p.astype(BF16)
                total = jnp.sum(total, axis=0, keepdims=True)
                tot_s[slot : slot + 1, here] = 1.0 / total
                lse_o[j : j + 1, q0 + at : q0 + at + wide] = top + jnp.log(total)
            out = dot(vt_s[:, k0:k1], p_s[slot, :number, :count])
            ot_s[:, lanes] = out * tot_s[slot : slot + 1, :count]

        area(0, 0, short, 0, long0, {short: col_short})
        either = {k: row_short for k in range(0, short, quarter)}
        either[short] = jnp.where(in_row, col_long, col_short)
        either.update({k: row_long for k in range(long0, group, quarter)})
        area(1, short, quarter, 0, group, either)
        for t in range(n_head - 1):
            area(t % 2, long0 + t * rows, rows, short, group, {short: col_long})
        o_s[...] = jnp.transpose(ot_s[...]).astype(BF16)

        for s, block in enumerate(unsorted_blocks(first_case, o_s[...])):
            own_s[j, s] = halves_to_lanes(block)
        batch = [pltpu.make_async_copy(own_s.at[j, h], att_r.at[h * local + j], own_sem.at[j])]
        for o, other in enumerate(others):
            batch.append(
                pltpu.make_async_remote_copy(
                    src_ref=own_s.at[j, other],
                    dst_ref=att_r.at[h * local + j],
                    send_sem=att_send.at[j, o],
                    recv_sem=att_recv.at[j, o],
                    device_id=(c, other),
                    device_id_type=MESH,
                )
            )
        for copy in batch:
            copy.start()
        att_copies.append(batch)
    late = [pltpu.make_async_copy(grp, grp_o, out_sem.at[2]), pltpu.make_async_copy(own_s, own_o, out_sem.at[3])]
    for out in late:
        out.start()
    outs += late
    for batch in att_copies:
        for copy in batch:
            copy.wait()
    for p in range(HEADS // 2):
        even, odd = att_r[2 * p], att_r[2 * p + 1]
        top = jnp.concatenate([even[:, :HEAD_DIM], odd[:, :HEAD_DIM]], axis=1)
        low = jnp.concatenate([even[:, HEAD_DIM:], odd[:, HEAD_DIM:]], axis=1)
        att_o[:, 128 * p : 128 * (p + 1)] = jnp.concatenate([top, low], axis=0)
    for out in outs:
        out.wait()


def front(n_crop, n_head, tokens, mixw, prow, crop, small, wqkv):
    rows, width = tokens.shape
    group, local = rows * n_head, HEADS // n_head
    dma = pltpu.SemaphoreType.DMA
    vmem = pl.BlockSpec(memory_space=pltpu.VMEM)
    hbm = pl.BlockSpec(memory_space=pl.ANY)
    block = rows + rows // 2
    shape = jax.ShapeDtypeStruct
    return pl.pallas_call(
        functools.partial(front_kernel, n_crop, n_head),
        out_shape=(
            shape((rows, width), F32),
            shape((rows, width), BF16),
            shape((local, n_head, block, 128), BF16),
            shape((rows, width), BF16),
            shape((local, n_head, rows // 2, 128), BF16),
            shape((8, group), F32),
        ),
        in_specs=[vmem, vmem, vmem, pl.BlockSpec(memory_space=pltpu.SMEM), vmem, vmem, vmem, vmem, vmem],
        out_specs=(hbm, hbm, hbm, vmem, hbm, vmem),
        scratch_shapes=[
            pltpu.VMEM((rows, width), BF16),
            pltpu.VMEM((rows, width), F32),
            pltpu.VMEM((rows, width), BF16),
            pltpu.VMEM((HEADS, block, 128), BF16),
            pltpu.VMEM((local, n_head, block, 128), BF16),
            pltpu.VMEM((group, HEAD_DIM), BF16),
            pltpu.VMEM((group, HEAD_DIM), BF16),
            pltpu.VMEM((group, HEAD_DIM), BF16),
            pltpu.VMEM((group, HEAD_DIM), BF16),
            pltpu.VMEM((HEAD_DIM, group), BF16),
            pltpu.VMEM((HEAD_DIM, group), BF16),
            pltpu.VMEM((HEAD_DIM, group), F32),
            pltpu.VMEM((2, group, rows), F32),
            pltpu.VMEM((2, group, rows), BF16),
            pltpu.VMEM((8, rows), F32),
            pltpu.VMEM((local, n_head, rows // 2, 128), BF16),
            pltpu.VMEM((HEADS, rows // 2, 128), BF16),
            dma((2,)),
            dma((local, n_head - 1)),
            dma((local, n_head - 1)),
            dma((local, n_head - 1)),
            dma((local, n_head - 1)),
            dma((local,)),
            dma((4,)),
        ],
        compiler_params=pltpu.CompilerParams(collective_id=1, has_side_effects=True, vmem_limit_bytes=56 * MiB),
        cost_estimate=pl.CostEstimate(flops=10**10, bytes_accessed=2 * 10**7, transcendentals=10**7),
        name="front",
    )(tokens, mixw, prow, crop, *small, wqkv)


GELU_POLY = (0.254829592, -0.284496736, 1.421413741, -1.453152027, 1.061405429)
FC_TILE = 768
PIECE = 384


def gelu_and_slope(pre):
    bell = jnp.exp(-0.5 * pre * pre)
    t = 1.0 / (1.0 + (0.3275911 * 0.7071067811865476) * jnp.abs(pre))
    poly = GELU_POLY[4]
    for coefficient in GELU_POLY[3::-1]:
        poly = poly * t + coefficient
    tail = 0.5 * poly * t * bell
    phi = jnp.where(pre >= 0.0, 1.0 - tail, tail)
    return pre * phi, phi + pre * bell * 0.3989422804014327


def put_blocks(ref, lead, value):
    if len(ref.shape) == len(lead) + 5:
        rows = value.shape[0] // 8
        for c in range(8):
            ref[(*lead, c % 2, c // 2 % 2, c // 4)] = value[c * rows : (c + 1) * rows].astype(BF16)
    else:
        ref[lead] = value.astype(BF16)


def middle_kernel(
    cut,
    att, mixed, cot, bout_r, gain_r, bias_r, bfc2_r, bfc1_r, wout_h, w1_h, w2_h,
    layer_o, attg_o, mg_o, jfc_o, gout_o, sm_o,
    wout, w1, w2, mid_s, n2_s, n2t_s, cott_s, out_s, dn_s, pre_s, gw_s, act_s, pg_s, proj_s, b1_s, jfc,
    w_sem, j_sem,
):
    rows, width = cot.shape
    tiles = w1_h.shape[1] // FC_TILE
    wout_copy = pltpu.make_async_copy(wout_h, wout, w_sem.at[0, 0])
    wout_copy.start()
    w_copies = []
    for t in range(tiles):
        at = slice(t * FC_TILE, (t + 1) * FC_TILE)
        pair = (
            pltpu.make_async_copy(w1_h.at[:, at], w1.at[t], w_sem.at[1, t]),
            pltpu.make_async_copy(w2_h.at[at], w2.at[t], w_sem.at[2, t]),
        )
        for copy in pair:
            copy.start()
        w_copies.append(pair)
    sm_o[...] = jnp.zeros_like(sm_o)
    bout, gain, bias, bfc2, bfc1 = [as_line(r).astype(F32) for r in (bout_r, gain_r, bias_r, bfc2_r, bfc1_r)]
    for t in range(tiles):
        b1_s[t : t + 1, :] = bfc1[:, t * FC_TILE : (t + 1) * FC_TILE]
    cott_s[...] = jnp.transpose(cot[...])
    wout_copy.wait()
    step = 128
    mid_s[...] = mixed[...] + dot(att[...], wout[...]) + bout

    def norm2(part):
        mid = mid_s[part]
        mean = jnp.mean(mid, axis=1, keepdims=True)
        centered = mid - mean
        rstd = lax.rsqrt(jnp.mean(centered * centered, axis=1, keepdims=True) + EPS)
        return mid, centered * rstd, rstd

    total = jnp.zeros((1, width), F32)
    for r in range(0, rows, step):
        part = slice(r, r + step)
        mid, unit, _ = norm2(part)
        n2_s[part] = (unit * gain + bias).astype(BF16)
        out_s[part] = mid + bfc2
        dn_s[part] = jnp.zeros((step, width), F32)
        total = total + jnp.sum(cot[part].astype(F32), axis=0, keepdims=True)
    sm_o[7:8, :] = total
    n2t_s[...] = jnp.transpose(n2_s[...])

    @pl.loop(0, tiles)
    def _(t):
        pltpu.make_async_copy(w1.at[t], w1.at[t], w_sem.at[1, t]).wait()
        pltpu.make_async_copy(w2.at[t], w2.at[t], w_sem.at[2, t]).wait()
        pre_s[...] = dot(n2_s[...], w1[t]) + b1_s[pl.ds(t, 1), :]
        gw_s[...] = dot_nt(cot[...], w2[t])
        sums = jnp.zeros((1, FC_TILE), F32)
        for r in range(0, rows, 64):
            part = slice(r, r + 64)
            act, slope = gelu_and_slope(pre_s[part])
            act_s[part] = act.astype(BF16)
            pg = (gw_s[part] * slope).astype(BF16)
            pg_s[part] = pg
            sums = sums + jnp.sum(pg.astype(F32), axis=0, keepdims=True)
        sm_o[pl.ds(8 + t, 1), :] = sums
        out_s[...] += dot(act_s[...], w2[t])
        dn_s[...] += dot_nt(pg_s[...], w1[t])
        g1 = dot(n2t_s[...], pg_s[...])
        for half in range(2):
            put_blocks(jfc, (half, lax.rem(t, 2), lax.div(t, 2)), g1[:, PIECE * half : PIECE * (half + 1)])
        g2 = dot(cott_s[...], act_s[...])
        if cut:
            for b in range(8):
                for s in range(2):
                    piece = g2[96 * b : 96 * (b + 1), PIECE * s : PIECE * (s + 1)].astype(BF16)
                    jfc[2 + b % 2, b // 2 % 2, b // 4, s, lax.rem(t, 2), lax.div(t, 2)] = piece
        else:
            for half in range(2):
                jfc[2 + half, lax.rem(t, 2), lax.div(t, 2)] = g2[:, PIECE * half : PIECE * (half + 1)].astype(BF16)

    j_copy = pltpu.make_async_copy(jfc, jfc_o, j_sem)
    j_copy.start()
    sums = [jnp.zeros((1, width), F32)] * 3
    for r in range(0, rows, step):
        part = slice(r, r + step)
        layer_o[part] = out_s[part].astype(BF16)
        _, unit, rstd = norm2(part)
        dn = dn_s[part]
        e = dn * gain
        inner = e - jnp.mean(e, axis=1, keepdims=True) - unit * jnp.mean(e * unit, axis=1, keepdims=True)
        mg = cot[part].astype(F32) + rstd * inner
        mg_o[part] = mg
        proj = mg.astype(BF16)
        proj_s[part] = proj
        for k, term in enumerate((proj.astype(F32), dn * unit, dn)):
            sums[k] = sums[k] + jnp.sum(term, axis=0, keepdims=True)
    for k in range(3):
        sm_o[4 + k : 5 + k, :] = sums[k]
    attg = dot_nt(proj_s[...], wout[...])
    for i in range(HEADS):
        attg_o[i] = halves_to_lanes(attg[:, HEAD_DIM * i : HEAD_DIM * (i + 1)]).astype(BF16)
    gout = dot_tn(att[...], proj_s[...])
    for k in range(2):
        put_blocks(gout_o, (k,), gout[:, PIECE * k : PIECE * (k + 1)])
    j_copy.wait()


def middle(cut, att, mixed, cot, small, wout, w1, w2):
    rows, width = cot.shape
    vmem = pl.BlockSpec(memory_space=pltpu.VMEM)
    hbm = pl.BlockSpec(memory_space=pl.ANY)
    dma = pltpu.SemaphoreType.DMA
    shape = jax.ShapeDtypeStruct
    ff = w1.shape[1]
    jfc_dims = (4, 2, 2, 2, 2, 2, 96, PIECE) if cut else (4, 2, 2, width, PIECE)
    gout_dims = (2, 2, 2, 2, 96, PIECE) if cut else (2, width, PIECE)
    full = lambda kind: pltpu.VMEM((rows, width), kind)
    tile = lambda kind: pltpu.VMEM((rows, FC_TILE), kind)
    return pl.pallas_call(
        functools.partial(middle_kernel, cut),
        out_shape=(
            shape((rows, width), BF16),
            shape((HEADS, rows // 2, 128), BF16),
            shape((rows, width), F32),
            shape(jfc_dims, BF16),
            shape(gout_dims, BF16),
            shape((16, width), F32),
        ),
        in_specs=[vmem] * 8 + [hbm] * 3,
        out_specs=(vmem, vmem, vmem, hbm, vmem, vmem),
        scratch_shapes=[
            pltpu.VMEM((width, width), BF16),
            pltpu.VMEM((ff // FC_TILE, width, FC_TILE), BF16),
            pltpu.VMEM((ff // FC_TILE, FC_TILE, width), BF16),
            full(F32), full(BF16),
            pltpu.VMEM((width, rows), BF16), pltpu.VMEM((width, rows), BF16),
            full(F32), full(F32), tile(F32), tile(F32), tile(BF16), tile(BF16), full(BF16), pltpu.VMEM((8, FC_TILE), F32),
            pltpu.VMEM(jfc_dims, BF16),
            dma((3, 4)), dma,
        ],
        compiler_params=pltpu.CompilerParams(vmem_limit_bytes=60 * MiB),
        cost_estimate=pl.CostEstimate(flops=2 * 8 * 10**9, bytes_accessed=3 * 10**7, transcendentals=4 * 10**6),
        name="middle",
    )(att, mixed, cot, *small, wout, w1, w2)


class Reduction:
    AXES = ("x", "y", "lo", "hi")

    def __init__(self, acc, received, fin, send_sem, recv_sem, bits, peers, order):
        self.acc, self.received, self.fin = acc, received, fin
        self.send_sem, self.recv_sem = send_sem, recv_sem
        self.bits, self.peers, self.order = bits, peers, order

    def remote(self, k, src, dst, axis):
        return pltpu.make_async_remote_copy(
            src_ref=src, dst_ref=dst, send_sem=self.send_sem.at[k], recv_sem=self.recv_sem.at[k],
            device_id=self.peers[axis], device_id_type=MESH,
        )

    def add(self, into, received, lead, free):
        count = 1 << len(free)

        def one(i):
            place = [(i >> (len(free) - 1 - n)) & 1 if isinstance(i, int) else lax.rem(lax.div(i, 1 << (len(free) - 1 - n)), 2) for n in range(len(free))]
            index = list(lead)
            for axis, p in zip(free, place):
                index[self.AXES.index(axis)] = p
            index, place = tuple(index), tuple(place)
            into[index] = (into[index].astype(F32) + received[place].astype(F32)).astype(BF16)

        if count > 2:
            pl.loop(0, count)(one)
        else:
            for i in range(count):
                one(i)

    def steps(self, source, core_half):
        copy = self.remote(0, source, self.received[0], "core")
        copy.start()
        if core_half is not None:
            core_half.start()
        yield
        copy.wait()
        if core_half is not None:
            core_half.wait()
        self.add(self.acc, self.received[0], [None] * 4, list(self.AXES))
        lead = [slice(None)] * 4
        free = list(self.AXES)
        for k, axis in enumerate(self.order):
            at = self.AXES.index(axis)
            lead[at] = 1 - self.bits[axis]
            copy = self.remote(1 + k, self.acc.at[tuple(lead)], self.received[1 + k], axis)
            copy.start()
            lead[at] = self.bits[axis]
            free.remove(axis)
            yield
            copy.wait()
            self.add(self.acc, self.received[1 + k], lead, free)
        bc, bx = self.bits["core"], self.bits["x"]
        mine = pltpu.make_async_copy(self.acc.at[tuple(lead)], self.fin.at[bc, bx], self.send_sem.at[7])
        mine.start()
        mine.wait()
        copy = self.remote(5, self.fin.at[bc, bx], self.fin.at[bc, bx], "x")
        copy.start()
        yield
        copy.wait()
        copy = self.remote(6, self.fin.at[bc], self.fin.at[bc], "core")
        copy.start()
        yield
        copy.wait()


def tick(*jobs):
    for job in jobs:
        next(job, None)


def back_kernel(
    n_crop, n_head, cut,
    attg, grp_h, own, lse, jfc_h, gout, wqkv_h, normed_h, mixed_h, mg_h, mixw_r, prow_r, crop, gain_r, sm_in,
    *rest,
):
    (
        grad_o, fin_o, sm_o,
        grp, wqkv, normed, mixed, mg_s, dor, k_s, v_s, kt_s, qt_s, dot_s, dqt_s, s_s, dp_s, pds_s, dzq_s, dkv_s, dq_s, di_s, msg, ret, dn_s, sent_s, back_s,
        ja, jb, load_sem, do_send, do_recv, dq_send, dq_recv, own_sem, far_sem,
        *reduce_refs,
    ) = rest
    rows, width = mixed.shape
    group = rows * n_head
    local = HEADS // n_head
    c, h = lax.axis_index("crop"), lax.axis_index("head")
    far = lax.rem(c + n_crop // 2, n_crop)
    others = [lax.rem(h + o, n_head) for o in range(1, n_head)]
    peers = [(far, h)] + [(c, other) for other in others]
    if cut:
        bits = {"core": lax.rem(h, 2), "x": lax.div(h, 2), "y": lax.rem(c, 2), "lo": lax.rem(lax.div(c, 2), 2), "hi": lax.div(c, 4)}
        near = {
            "core": (c, h + 1 - 2 * bits["core"]),
            "x": (c, h + 2 - 4 * bits["x"]),
            "y": (c + 1 - 2 * bits["y"], h),
            "lo": (c + 2 - 4 * bits["lo"], h),
            "hi": (far, h),
        }
        peers += [near["y"], near["lo"]]
    greet(peers)

    def spread(j, source, target, send_sem, recv_sem):
        copies = [pltpu.make_async_copy(source(h), target(h), own_sem.at[j])]
        for o, other in enumerate(others):
            copies.append(
                pltpu.make_async_remote_copy(
                    src_ref=source(other), dst_ref=target(h), send_sem=send_sem.at[j, o], recv_sem=recv_sem.at[j, o],
                    device_id=(c, other), device_id_type=MESH,
                )
            )
        for copy in copies:
            copy.start()
        return copies

    do_copies = [
        spread(j, lambda d, j=j: attg.at[d * local + j], lambda s, j=j: dor.at[j, s], do_send, do_recv) for j in range(local)
    ]
    loads = [
        pltpu.make_async_copy(a, b, load_sem.at[k])
        for k, (a, b) in enumerate([(grp_h, grp), (normed_h, normed), (wqkv_h, wqkv), (mixed_h, mixed), (mg_h, mg_s)])
    ]
    loads += [pltpu.make_async_copy(gout.at[k], ja.at[k, 0], load_sem.at[5 + k]) for k in range(2)]
    for load in loads:
        load.start()
    jobs, plan = [], {}
    if cut:
        send_sem, recv_sem, half_sem, sm_send, sm_recv, sm_r, acc_s, *received = reduce_refs
        orders = [("y", "lo", "x", "hi"), ("lo", "y", "x", "hi")] * 2 + [("y", "lo", "x", "hi"), ("y", "x", "lo", "hi")]
        for k in range(6):
            acc = acc_s.at[k] if k < 4 else (ja, jb)[k - 4].at[bits["core"]]
            red = Reduction(acc, [r.at[k] for r in received], fin_o.at[k], send_sem.at[k], recv_sem.at[k], bits, near, orders[k])
            if k < 4:
                keep = pltpu.make_async_copy(jfc_h.at[k, bits["core"]], acc, half_sem.at[k])
                jobs.append(red.steps(jfc_h.at[k, 1 - bits["core"]], keep))
            else:
                jobs.append(red.steps((ja, jb)[k - 4].at[1 - bits["core"]], None))
        fc1, fc2, fc3, fc4, joba, jobb = jobs
        tick(fc1, fc2, fc3, fc4)
        plan = {
            (0, "first"): (fc1, fc2),
            (0, 5): (fc1, fc2, fc3, fc4),
            (1, "end"): (joba,),
            (1, 5): (fc1, fc2),
            (2, 0): (fc1, fc2),
            (2, 3): (fc1, fc2, fc3, fc4),
            (2, 5): (joba,),
            "last": (fc3, fc4, jobb, fc1, fc2),
        }

    bound = crop[0, 0]
    first_case = bound < group // 2
    quarter = rows // 4
    short, long0 = 3 * quarter, 4 * quarter
    in_col = either_in_long(first_case, bound, (quarter, 1), 0, group) > 0.5
    in_row = either_in_long(first_case, bound, (1, quarter), 1, group) > 0.5
    col_long, col_short = jnp.where(in_col, 0.0, NEG), jnp.where(in_col, NEG, 0.0)
    row_long, row_short = jnp.where(in_row, 0.0, NEG), jnp.where(in_row, NEG, 0.0)
    lane = lax.broadcasted_iota(jnp.int32, (8, 128), 1) // HEAD_DIM
    ones = (lane == lax.broadcasted_iota(jnp.int32, (8, 128), 0)).astype(F32).astype(BF16)
    sums_q, sums_v = [None] * HEADS, [None] * HEADS
    dn_s[...] = jnp.zeros_like(dn_s)
    dq_copies = []

    def head_grads(j):
        for copy in dq_copies[j]:
            copy.wait()
        for pair in range(n_head // 2):
            packs = []
            for d in (2 * pair, 2 * pair + 1):
                i = d * local + j
                vk = ret[i, 0:rows]
                dq = lanes_to_halves(ret[i, rows : rows + rows // 2])
                dk, dv = vk[:, HEAD_DIM:], vk[:, :HEAD_DIM]
                sums_q[i] = jnp.sum(dq.astype(F32), axis=0, keepdims=True)
                sums_v[i] = jnp.sum(dv.astype(F32), axis=0, keepdims=True)
                odd = i % 2
                base = 3 * HEAD_DIM * i - HEAD_DIM * odd
                none = jnp.zeros_like(dq)
                wide = jnp.concatenate([none, dq, dk, dv] if odd else [dq, dk, dv, none], axis=1)
                dn_s[...] += dot_nt(wide, wqkv[:, base : base + 4 * HEAD_DIM])
                packs += [dq, dk, dv]
            grad = dot_tn(normed[...], jnp.concatenate(packs, axis=1))
            if j == 0:
                put_blocks(ja, (pair, 1), grad)
            else:
                put_blocks(jb, (pair, j - 1), grad)

    for j in range(local):
        for copy in do_copies[j]:
            copy.wait()
        if j == 0:
            loads[0].wait()
            tick(*plan.get((0, "first"), ()))
        rowd = []
        for s in range(n_head):
            prod = dor[j, s].astype(F32) * own[j, s].astype(F32)
            hi = prod.astype(BF16)
            d8 = dot_nt(ones, hi) + dot_nt(ones, (prod - hi.astype(F32)).astype(BF16))
            rowd.append(jnp.concatenate([d8[0:1], d8[1:2]], axis=1))
        end = lax.select(first_case, rowd[0], rowd[3])
        full = lax.select(first_case, rowd[3], rowd[0])
        ends = [end[:, quarter * k : quarter * (k + 1)] for k in range(4)]
        first, last = lax.select(first_case, ends[0], ends[3]), lax.select(first_case, ends[3], ends[0])
        di_s[0:1, :] = jnp.concatenate([first, ends[1], ends[2], last, full, rowd[1], rowd[2]], axis=1)
        qk = sorted_blocks(first_case, [grp[j, s, 0:rows] for s in range(n_head)])
        vv = sorted_blocks(first_case, [lanes_to_halves(grp[j, s, rows : rows + rows // 2]) for s in range(n_head)])
        dd = sorted_blocks(first_case, [lanes_to_halves(dor[j, s]) for s in range(n_head)])
        at = 0
        for a, b, d in zip(qk, vv, dd):
            n = a.shape[0]
            q = a[:, :HEAD_DIM] * BF16(HEAD_DIM**-0.5)
            k_s[at : at + n] = a[:, HEAD_DIM:]
            v_s[at : at + n] = b
            qt_s[:, at : at + n] = jnp.transpose(q)
            dot_s[:, at : at + n] = jnp.transpose(d)
            block, inner = at // rows, at % rows
            dzq_s[block, inner : inner + n] = jnp.concatenate([d, jnp.zeros_like(d)], axis=1)
            dzq_s[block, rows + inner : rows + inner + n] = jnp.concatenate([jnp.zeros_like(q), q], axis=1)
            at += n
        kt_s[...] = jnp.transpose(k_s[...])
        dqt_s[...] = jnp.zeros_like(dqt_s)
        dkv_s[...] = jnp.zeros_like(dkv_s)

        def area(q0, count, k0, k1, masks):
            lanes, number = slice(q0, q0 + count), k1 - k0
            s_s[:number, :count] = dot(k_s[k0:k1], qt_s[:, lanes])
            dp_s[:number, :count] = dot(v_s[k0:k1], dot_s[:, lanes])
            for k, mask in masks.items():
                if k0 <= k < k1:
                    s_s[k - k0 : k - k0 + quarter, :count] += mask
            for at in range(0, count, LANES):
                wide = min(LANES, count - at)
                here, place = slice(at, at + wide), slice(q0 + at, q0 + at + wide)
                lse_row, di_row = lse[j : j + 1, place], di_s[0:1, place]
                for k in range(0, number, KEYS):
                    keys = slice(k, k + KEYS)
                    p = jnp.exp(s_s[keys, here] - lse_row)
                    ds = p * (dp_s[keys, here] - di_row)
                    pds_s[keys, here] = p.astype(BF16)
                    pds_s[keys, rows + at : rows + at + wide] = ds.astype(BF16)
            block, inner = q0 // rows, q0 % rows
            if count == rows:
                add = dot(pds_s[:number], dzq_s[block])
            else:
                add = dot(pds_s[:number, :count], dzq_s[block, inner : inner + count])
                add = add + dot(pds_s[:number, rows : rows + count], dzq_s[block, rows + inner : rows + inner + count])
            dkv_s[k0:k1] += add
            dqt_s[:, lanes] += dot(kt_s[:, k0:k1], pds_s[:number, rows : rows + count])

        area(0, short, 0, long0, {short: col_short})
        either = {k: row_short for k in range(0, short, quarter)}
        either[short] = jnp.where(in_row, col_long, col_short)
        either.update({k: row_long for k in range(long0, group, quarter)})
        for k in range(0, group, rows):
            area(short, quarter, k, k + rows, either)
        tick(*plan.get((j, "near"), ()))
        half_keys = (group - short) // 2
        for t in range(n_head - 1):
            for half in range(2):
                k = short + half * half_keys
                area(long0 + t * rows, rows, k, k + half_keys, {short: col_long})
                tick(*plan.get((j, 2 * t + half), ()))
        dq_s[...] = jnp.transpose(dqt_s[...] * HEAD_DIM**-0.5).astype(BF16)

        dkv = unsorted_blocks(first_case, dkv_s[...])
        dqu = unsorted_blocks(first_case, dq_s[...])
        for s in range(n_head):
            msg[j, s, 0:rows] = dkv[s].astype(BF16)
            msg[j, s, rows : rows + rows // 2] = halves_to_lanes(dqu[s])
        dq_copies.append(spread(j, lambda d, j=j: msg.at[j, d], lambda s, j=j: ret.at[s * local + j], dq_send, dq_recv))
        if j == 0:
            for load in loads[1:]:
                load.wait()
        else:
            head_grads(j - 1)
        tick(*plan.get((j, "end"), ()))

    head_grads(local - 1)
    tick(*plan.get("last", ()))
    share = as_column(as_line(mixw_r))
    gain = as_line(gain_r).astype(F32)
    sums = [jnp.zeros((1, width), F32)] * 2
    scaled = []
    step = 128
    for r in range(0, rows, step):
        part = slice(r, r + step)
        mix = mixed[part]
        mean = jnp.mean(mix, axis=1, keepdims=True)
        centered = mix - mean
        rstd = lax.rsqrt(jnp.mean(centered * centered, axis=1, keepdims=True) + EPS)
        unit = centered * rstd
        dn = dn_s[part]
        e = dn * gain
        inner = e - jnp.mean(e, axis=1, keepdims=True) - unit * jnp.mean(e * unit, axis=1, keepdims=True)
        grad = mg_s[part] + rstd * inner
        sums[0] = sums[0] + jnp.sum(dn * unit, axis=0, keepdims=True)
        sums[1] = sums[1] + jnp.sum(dn, axis=0, keepdims=True)
        mixed[part] = share[part] * grad
        dn_s[part] = (1.0 - share[part]) * grad
    chosen = lax.broadcasted_iota(jnp.int32, (rows, rows), 0) == as_line(prow_r)
    chosen = chosen.astype(F32).astype(BF16)
    given = dn_s[...]
    high = given.astype(BF16)
    low = (given - high.astype(F32)).astype(BF16)
    sent_s[...] = (dot(chosen, high) + dot(chosen, low)).astype(BF16)
    far_copy = pltpu.make_async_remote_copy(
        src_ref=sent_s, dst_ref=back_s, send_sem=far_sem.at[0], recv_sem=far_sem.at[1], device_id=(far, h), device_id_type=MESH
    )
    far_copy.start()
    sm_o[...] = sm_in[...]
    sm_o[0:1, :] = sums[0]
    sm_o[1:2, :] = sums[1]
    sm_o[2:3, :] = jnp.concatenate(sums_q, axis=1)
    sm_o[3:4, :] = jnp.concatenate(sums_v, axis=1)
    if cut:
        def small_sum():
            for k, axis in enumerate(("core", "x", "y", "lo", "hi")):
                copy = pltpu.make_async_remote_copy(
                    src_ref=sm_o, dst_ref=sm_r.at[k], send_sem=sm_send.at[k], recv_sem=sm_recv.at[k],
                    device_id=near[axis], device_id_type=MESH,
                )
                copy.start()
                yield
                copy.wait()
                sm_o[...] += sm_r[k]

        small = small_sum()
        tick(small, jobb, fc3, fc4, fc1, fc2, small, joba, small)
        tick(fc3, fc4, joba, small, jobb, joba, fc3, fc4, small, jobb, joba, fc3, fc4, small, jobb, joba, jobb, joba, jobb, jobb)
    else:
        fin_o[0] = ja[...]
        fin_o[1] = jb[...]
    far_copy.wait()
    for r in range(0, rows, step):
        part = slice(r, r + step)
        grad_o[part] = (mixed[part] + back_s[part].astype(F32)).astype(BF16)


def back(n_crop, n_head, cut, attg, grp, own, lse, jfc, gout, wqkv, normed, mixed, mg, mixw, prow, crop, gain, sm):
    rows, width = mixed.shape
    group, local = rows * n_head, HEADS // n_head
    vmem = pl.BlockSpec(memory_space=pltpu.VMEM)
    hbm = pl.BlockSpec(memory_space=pl.ANY)
    smem = pl.BlockSpec(memory_space=pltpu.SMEM)
    dma = pltpu.SemaphoreType.DMA
    shape = jax.ShapeDtypeStruct
    block = rows + rows // 2
    jq_dims = (2, 2, 2, 2, 2, 96, PIECE) if cut else (2, 2, width, PIECE)
    finals = (6, 2, 2, 96, PIECE) if cut else (2, *jq_dims)
    square = lambda n, kind: pltpu.VMEM((group, n), kind)
    scratch = [
        pltpu.VMEM((local, n_head, block, 128), BF16),
        pltpu.VMEM(wqkv.shape, BF16),
        pltpu.VMEM((rows, width), BF16),
        pltpu.VMEM((rows, width), F32),
        pltpu.VMEM((rows, width), F32),
        pltpu.VMEM((local, n_head, rows // 2, 128), BF16),
        square(HEAD_DIM, BF16), square(HEAD_DIM, BF16),
        pltpu.VMEM((HEAD_DIM, group), BF16), pltpu.VMEM((HEAD_DIM, group), BF16), pltpu.VMEM((HEAD_DIM, group), BF16),
        pltpu.VMEM((HEAD_DIM, group), F32),
        pltpu.VMEM((832, rows), F32), pltpu.VMEM((832, rows), F32), pltpu.VMEM((832, 2 * rows), BF16),
        pltpu.VMEM((n_head, 2 * rows, 128), BF16), square(128, F32), square(HEAD_DIM, BF16),
        pltpu.VMEM((8, group), F32),
        pltpu.VMEM((local, n_head, block, 128), BF16),
        pltpu.VMEM((HEADS, block, 128), BF16),
        pltpu.VMEM((rows, width), F32),
        pltpu.VMEM((rows, width), BF16),
        pltpu.VMEM((rows, width), BF16),
        pltpu.VMEM(jq_dims, BF16),
        pltpu.VMEM(jq_dims, BF16),
        dma((7,)),
        dma((local, n_head - 1)), dma((local, n_head - 1)), dma((local, n_head - 1)), dma((local, n_head - 1)),
        dma((local,)),
        dma((2,)),
    ]
    if cut:
        scratch += [dma((6, 8)), dma((6, 8)), dma((4,)), dma((5,)), dma((5,)), pltpu.VMEM((5, 16, width), F32)]
        scratch.append(pltpu.VMEM((4, 2, 2, 2, 2, 96, PIECE), BF16))
        scratch += [pltpu.VMEM((6,) + (2,) * n + (96, PIECE), BF16) for n in (4, 3, 2, 1, 0)]
    return pl.pallas_call(
        functools.partial(back_kernel, n_crop, n_head, cut),
        out_shape=(shape((rows, width), BF16), shape(finals, BF16), shape((16, width), F32)),
        in_specs=[hbm, hbm, vmem, vmem, hbm, hbm, hbm, hbm, hbm, hbm, vmem, vmem, smem, vmem, vmem],
        out_specs=(vmem,) * 3,
        scratch_shapes=scratch,
        compiler_params=pltpu.CompilerParams(collective_id=2, has_side_effects=True, vmem_limit_bytes=60 * MiB),
        cost_estimate=pl.CostEstimate(flops=2 * 10**10, bytes_accessed=3 * 10**7, transcendentals=10**7),
        name="back",
    )(attg, grp, own, lse, jfc, gout, wqkv, normed, mixed, mg, mixw, prow, crop, gain, sm)


def finish_kernel(n_crop, n_head, grad, fin, sm, *outs):
    grad_o, g1_o, b1_o, gq_o, bq_o, bv_o, go_o, bo_o, g2_o, b2_o, gf1_o, bf1_o, gf2_o, bf2_o = outs
    c = lax.axis_index("crop")
    local = HEADS // n_head
    grad_o[...] = grad[...]
    parts = []
    for k in range(4):
        core, x = k % 2, k // 2
        for half in range(2):
            at = FC_TILE * k + PIECE * half
            gf1_o[:, at : at + PIECE] = fin[half, core, x].astype(F32)
        both = jnp.concatenate([fin[2, core, x], fin[3, core, x]], axis=0)
        parts.append(jnp.transpose(both.astype(F32)))
    gf2_o[...] = jnp.concatenate(parts, axis=1)
    for k in range(2):
        go_o[:, PIECE * k : PIECE * (k + 1)] = fin[4, k, 0].astype(F32)
    parts = []
    for i in range(HEADS):
        d, j = i // local, i % local
        piece = fin[4, d // 2, 1] if j == 0 else fin[5, d // 2, j - 1]
        parts.append(piece[:, 192 * (d % 2) : 192 * (d % 2 + 1)].astype(F32))
    gq_o[...] = jnp.concatenate(parts, axis=1)
    piece = jnp.zeros((16, 96), F32)
    wide = jnp.zeros((1, PIECE), F32)
    for k in range(n_crop):
        piece = lax.select(c == k, sm[:, 96 * k : 96 * (k + 1)], piece)
        wide = lax.select(c == k, sm[8 + k // 2 : 9 + k // 2, PIECE * (k % 2) : PIECE * (k % 2 + 1)], wide)
    for row, out in ((0, g1_o), (1, b1_o), (2, bq_o), (3, bv_o), (4, bo_o), (5, g2_o), (6, b2_o), (7, bf2_o)):
        out[...] = piece[row : row + 1].reshape(96)
    bf1_o[...] = wide.reshape(PIECE)


def finish(n_crop, n_head, grad, fin, sm):
    rows, width = grad.shape
    vmem = pl.BlockSpec(memory_space=pltpu.VMEM)
    shape = jax.ShapeDtypeStruct
    short = shape((96,), F32)
    outs = (
        shape((rows, width), BF16), short, short, shape((96, 3 * width), F32), short, short, shape((96, width), F32), short,
        short, short, shape((96, 4 * width), F32), shape((PIECE,), F32), shape((PIECE, width), F32), short,
    )
    return pl.pallas_call(
        functools.partial(finish_kernel, n_crop, n_head),
        out_shape=outs,
        in_specs=[vmem] * 3,
        out_specs=(vmem,) * len(outs),
        compiler_params=pltpu.CompilerParams(vmem_limit_bytes=60 * MiB),
        name="finish",
    )(grad, fin, sm)


def sum_everywhere(grads, small, n_crop, n_head):
    c = lax.axis_index("crop")

    def scatter(value):
        part = lax.psum_scatter(value.astype(F32), "crop", scatter_dimension=0, tiled=True)
        return lax.psum(part.astype(BF16), "head").astype(F32)

    jfc, ja, jb = grads
    width = jfc.shape[3]
    local = HEADS // n_head
    g1 = jnp.concatenate([jfc[half, t % 2, t // 2] for t in range(4) for half in range(2)], axis=1)
    g2 = jnp.concatenate([jfc[2 + half, t % 2, t // 2] for t in range(4) for half in range(2)], axis=1).T
    go = jnp.concatenate([ja[0, 0], ja[1, 0]], axis=1)
    parts = []
    for i in range(HEADS):
        d, j = i // local, i % local
        piece = ja[d // 2, 1] if j == 0 else jb[d // 2, j - 1]
        parts.append(piece[:, 192 * (d % 2) : 192 * (d % 2 + 1)])
    gq = jnp.concatenate(parts, axis=1)
    total = lax.psum(small, ("crop", "head"))

    def mine(vector):
        count = vector.shape[0] // n_crop
        return lax.dynamic_slice_in_dim(vector, c * count, count, 0)

    rows = [mine(total[k]) for k in range(8)]
    return [
        rows[0], rows[1], scatter(gq), rows[2], rows[3], scatter(go), rows[4], rows[5], rows[6],
        scatter(g1), mine(total[8:12].reshape(4 * width)), scatter(g2), rows[7],
    ]


def shards(
    tokens, mix_weight, partner_row, crop_lengths, ln1_gain, ln1_bias, w_qkv, b_query, b_value, w_out, b_out,
    ln2_gain, ln2_bias, w_fc1, b_fc1, w_fc2, b_fc2, cotangent,
):
    n_crop, n_head = lax.axis_size("crop"), lax.axis_size("head")
    cut = n_crop == 8 and n_head == 4
    small1, small2 = (ln1_gain, ln1_bias, b_query, b_value), (b_out, ln2_gain, ln2_bias, b_fc2, b_fc1)
    mixed, normed, grp, att, own, lse = front(n_crop, n_head, tokens, mix_weight, partner_row, crop_lengths, small1, w_qkv)
    layer_out, attg, mg, jfc, gout, sm = middle(cut, att, mixed, cotangent, small2, w_out, w_fc1, w_fc2)
    grad, fin, sm = back(
        n_crop, n_head, cut, attg, grp, own, lse, jfc, gout, w_qkv, normed, mixed, mg, mix_weight, partner_row, crop_lengths, ln1_gain, sm
    )
    if not cut:
        return (layer_out, grad, *sum_everywhere((jfc, fin[0], fin[1]), sm, n_crop, n_head))
    outs = finish(n_crop, n_head, grad, fin, sm)
    return (layer_out, *outs)


def solution(mesh):
    rows, one = P(("crop", "head"), None), P(("crop", "head"))
    in_specs = (rows, one, one, P("crop", None)) + (P(),) * 13 + (rows,)
    vector, matrix = P("crop"), P("crop", None)
    out_specs = (
        rows, rows, vector, vector, matrix, vector, vector, matrix, vector, vector, vector, matrix, vector, matrix, vector,
    )
    return jax.shard_map(shards, mesh=mesh, in_specs=in_specs, out_specs=out_specs, check_vma=False)
```

```python
import functools
import itertools

import jax
import jax.numpy as jnp
from jax import lax
from jax.experimental import pallas as pl
from jax.experimental.pallas import tpu as pltpu
from jax.sharding import PartitionSpec as P

HEADS = 12
HEAD_DIM = 64
EPS = 1e-06
NEG = -1e30
KEYS = 64
LANES = 256
MESH = pl.DeviceIdType.MESH
F32 = jnp.float32
BF16 = jnp.bfloat16
MiB = 1 << 20


def dot(left, right):
    return jnp.dot(left, right, preferred_element_type=F32)


def dot_nt(left, right):
    return lax.dot_general(left, right, (((1,), (1,)), ((), ())), preferred_element_type=F32)


def dot_tn(left, right):
    return lax.dot_general(left, right, (((0,), (0,)), ((), ())), preferred_element_type=F32)


def as_line(ref):
    return ref[...].reshape(1, ref.shape[0])


def as_column(row):
    return jnp.transpose(jnp.broadcast_to(row, (8, row.shape[1])))[:, 0:1]


def as_row(column):
    return jnp.transpose(jnp.broadcast_to(column, (column.shape[0], 128)))[0:8]


def halves_to_lanes(block):
    half = block.shape[0] // 2
    return jnp.concatenate([block[:half], block[half:]], axis=1)


def lanes_to_halves(block):
    return jnp.concatenate([block[:, :HEAD_DIM], block[:, HEAD_DIM:]], axis=0)


def greet(peers):
    barrier = pltpu.get_barrier_semaphore()
    for peer in peers:
        pl.semaphore_signal(barrier, inc=1, device_id=peer, device_id_type=MESH)
    pl.semaphore_wait(barrier, len(peers))


def sorted_blocks(first_case, parts):
    end = lax.select(first_case, parts[0], parts[3])
    full = lax.select(first_case, parts[3], parts[0])
    q = end.shape[0] // 4
    near = lax.select(first_case, end[:q], end[3 * q :])
    either = lax.select(first_case, end[3 * q :], end[:q])
    return [near, end[q : 3 * q], either, full, parts[1], parts[2]]


def unsorted_blocks(first_case, block):
    n = block.shape[0] // 4
    q = n // 4
    low, mid, top = block[:q], block[q : 3 * q], block[3 * q : n]
    head = lax.select(first_case, low, top)
    tail = lax.select(first_case, top, low)
    end = jnp.concatenate([head, mid, tail], axis=0)
    full = block[n : 2 * n]
    return [
        lax.select(first_case, end, full),
        block[2 * n : 3 * n],
        block[3 * n :],
        lax.select(first_case, full, end),
    ]


def either_in_long(first_case, bound, shape, axis, group):
    place = lax.broadcasted_iota(jnp.int32, shape, axis)
    row = place + jnp.where(first_case, group // 4 - 128, group - group // 4)
    past = row >= bound
    return jnp.where(first_case, past.astype(F32), 1.0 - past.astype(F32))


def front_kernel(
    n_crop,
    n_head,
    tokens, mixw_r, prow_r, crop, gain_r, bias_r, bq_r, bv_r, wqkv,
    mixed_o, normed_o, grp_o, att_o, own_o, lse_o,
    prt, mixed_s, normed_s, msg, grp, q_s, k_s, v_s, o_s, qt_s, vt_s, ot_s, s_s, p_s, tot_s, own_s, att_r,
    prt_sem, qkv_send, qkv_recv, att_send, att_recv, own_sem, out_sem,
):
    rows, width = tokens.shape
    group = rows * n_head
    local = HEADS // n_head
    c, h = lax.axis_index("crop"), lax.axis_index("head")
    far = lax.rem(c + n_crop // 2, n_crop)
    others = [lax.rem(h + o, n_head) for o in range(1, n_head)]
    greet([(far, h)] + [(c, other) for other in others])

    partner_copy = pltpu.make_async_remote_copy(
        src_ref=tokens, dst_ref=prt, send_sem=prt_sem.at[0], recv_sem=prt_sem.at[1], device_id=(far, h), device_id_type=MESH
    )
    partner_copy.start()
    mixw, prow = as_line(mixw_r), as_line(prow_r)
    gain, bias, query_bias, value_bias = [as_line(r).astype(F32) for r in (gain_r, bias_r, bq_r, bv_r)]
    share = as_column(mixw)
    chosen = lax.broadcasted_iota(jnp.int32, (rows, rows), 0) == prow
    chosen = chosen.astype(F32).astype(BF16)
    partner_copy.wait()
    step = 128
    for r in range(0, rows, step):
        part = slice(r, r + step)
        gathered = dot_tn(chosen[:, part], prt[...])
        mix = share[part] * tokens[part].astype(F32) + (1.0 - share[part]) * gathered
        mixed_s[part] = mix
        mean = jnp.mean(mix, axis=1, keepdims=True)
        centered = mix - mean
        variance = jnp.mean(centered * centered, axis=1, keepdims=True)
        normed = centered * lax.rsqrt(variance + EPS) * gain + bias
        normed_s[part] = normed.astype(BF16)
    outs = [
        pltpu.make_async_copy(mixed_s, mixed_o, out_sem.at[0]),
        pltpu.make_async_copy(normed_s, normed_o, out_sem.at[1]),
    ]
    for out in outs:
        out.start()

    qkv_copies = []
    for j in range(local):
        for d in range(n_head):
            i = d * local + j
            odd = i % 2
            base = 3 * HEAD_DIM * i - HEAD_DIM * odd
            res = dot(normed_s[...], wqkv[:, base : base + 4 * HEAD_DIM])
            res = res[:, HEAD_DIM * odd : HEAD_DIM * odd + 3 * HEAD_DIM]
            bq = query_bias[:, HEAD_DIM * i : HEAD_DIM * (i + 1)]
            bv = value_bias[:, HEAD_DIM * i : HEAD_DIM * (i + 1)]
            res = res + jnp.concatenate([bq, jnp.zeros_like(bq), bv], axis=1)
            msg[i, 0:rows] = res[:, : 2 * HEAD_DIM].astype(BF16)
            msg[i, rows : rows + rows // 2] = halves_to_lanes(res[:, 2 * HEAD_DIM :]).astype(BF16)
        batch = [pltpu.make_async_copy(msg.at[h * local + j], grp.at[j, h], own_sem.at[j])]
        for o, other in enumerate(others):
            batch.append(
                pltpu.make_async_remote_copy(
                    src_ref=msg.at[other * local + j],
                    dst_ref=grp.at[j, h],
                    send_sem=qkv_send.at[j, o],
                    recv_sem=qkv_recv.at[j, o],
                    device_id=(c, other),
                    device_id_type=MESH,
                )
            )
        for copy in batch:
            copy.start()
        qkv_copies.append(batch)

    bound = crop[0, 0]
    first_case = bound < group // 2
    quarter = rows // 4
    short, long0 = 3 * quarter, 4 * quarter
    in_col = either_in_long(first_case, bound, (quarter, 1), 0, group) > 0.5
    in_row = either_in_long(first_case, bound, (1, quarter), 1, group) > 0.5
    col_long, col_short = jnp.where(in_col, 0.0, NEG), jnp.where(in_col, NEG, 0.0)
    row_long, row_short = jnp.where(in_row, 0.0, NEG), jnp.where(in_row, NEG, 0.0)
    att_copies = []
    for j in range(local):
        for copy in qkv_copies[j]:
            copy.wait()
        qk = sorted_blocks(first_case, [grp[j, s, 0:rows] for s in range(n_head)])
        vv = sorted_blocks(first_case, [lanes_to_halves(grp[j, s, rows : rows + rows // 2]) for s in range(n_head)])
        at = 0
        for a, b in zip(qk, vv):
            n = a.shape[0]
            q_s[at : at + n] = a[:, :HEAD_DIM] * BF16(HEAD_DIM**-0.5)
            k_s[at : at + n] = a[:, HEAD_DIM:]
            v_s[at : at + n] = b
            at += n

        qt_s[...] = jnp.transpose(q_s[...])
        vt_s[...] = jnp.transpose(v_s[...])

        def area(slot, q0, count, k0, k1, masks):
            lanes, number = slice(q0, q0 + count), k1 - k0
            s_s[slot, :number, :count] = dot(k_s[k0:k1], qt_s[:, lanes])
            for k, mask in masks.items():
                s_s[slot, k - k0 : k - k0 + quarter, :count] += mask
            for at in range(0, count, LANES):
                wide = min(LANES, count - at)
                here = slice(at, at + wide)
                top = jnp.full((8, wide), NEG, F32)
                for k in range(0, number, KEYS):
                    top = jnp.maximum(top, jnp.max(s_s[slot, k : k + KEYS, here].reshape(KEYS // 8, 8, wide), axis=0))
                top = jnp.max(top, axis=0, keepdims=True)
                total = jnp.zeros((8, wide), F32)
                for k in range(0, number, KEYS):
                    p = jnp.exp(s_s[slot, k : k + KEYS, here] - top)
                    total = total + jnp.sum(p.reshape(KEYS // 8, 8, wide), axis=0)
                    p_s[slot, k : k + KEYS, here] = p.astype(BF16)
                total = jnp.sum(total, axis=0, keepdims=True)
                tot_s[slot : slot + 1, here] = 1.0 / total
                lse_o[j : j + 1, q0 + at : q0 + at + wide] = top + jnp.log(total)
            out = dot(vt_s[:, k0:k1], p_s[slot, :number, :count])
            ot_s[:, lanes] = out * tot_s[slot : slot + 1, :count]

        area(0, 0, short, 0, long0, {short: col_short})
        either = {k: row_short for k in range(0, short, quarter)}
        either[short] = jnp.where(in_row, col_long, col_short)
        either.update({k: row_long for k in range(long0, group, quarter)})
        area(1, short, quarter, 0, group, either)
        for t in range(n_head - 1):
            area(t % 2, long0 + t * rows, rows, short, group, {short: col_long})
        o_s[...] = jnp.transpose(ot_s[...]).astype(BF16)

        for s, block in enumerate(unsorted_blocks(first_case, o_s[...])):
            own_s[j, s] = halves_to_lanes(block)
        batch = [pltpu.make_async_copy(own_s.at[j, h], att_r.at[h * local + j], own_sem.at[j])]
        for o, other in enumerate(others):
            batch.append(
                pltpu.make_async_remote_copy(
                    src_ref=own_s.at[j, other],
                    dst_ref=att_r.at[h * local + j],
                    send_sem=att_send.at[j, o],
                    recv_sem=att_recv.at[j, o],
                    device_id=(c, other),
                    device_id_type=MESH,
                )
            )
        for copy in batch:
            copy.start()
        att_copies.append(batch)
    late = [pltpu.make_async_copy(grp, grp_o, out_sem.at[2]), pltpu.make_async_copy(own_s, own_o, out_sem.at[3])]
    for out in late:
        out.start()
    outs += late
    for batch in att_copies:
        for copy in batch:
            copy.wait()
    for p in range(HEADS // 2):
        even, odd = att_r[2 * p], att_r[2 * p + 1]
        top = jnp.concatenate([even[:, :HEAD_DIM], odd[:, :HEAD_DIM]], axis=1)
        low = jnp.concatenate([even[:, HEAD_DIM:], odd[:, HEAD_DIM:]], axis=1)
        att_o[:, 128 * p : 128 * (p + 1)] = jnp.concatenate([top, low], axis=0)
    for out in outs:
        out.wait()


def front(n_crop, n_head, tokens, mixw, prow, crop, small, wqkv):
    rows, width = tokens.shape
    group, local = rows * n_head, HEADS // n_head
    dma = pltpu.SemaphoreType.DMA
    vmem = pl.BlockSpec(memory_space=pltpu.VMEM)
    hbm = pl.BlockSpec(memory_space=pl.ANY)
    block = rows + rows // 2
    shape = jax.ShapeDtypeStruct
    return pl.pallas_call(
        functools.partial(front_kernel, n_crop, n_head),
        out_shape=(
            shape((rows, width), F32),
            shape((rows, width), BF16),
            shape((local, n_head, block, 128), BF16),
            shape((rows, width), BF16),
            shape((local, n_head, rows // 2, 128), BF16),
            shape((8, group), F32),
        ),
        in_specs=[vmem, vmem, vmem, pl.BlockSpec(memory_space=pltpu.SMEM), vmem, vmem, vmem, vmem, vmem],
        out_specs=(hbm, hbm, hbm, vmem, hbm, vmem),
        scratch_shapes=[
            pltpu.VMEM((rows, width), BF16),
            pltpu.VMEM((rows, width), F32),
            pltpu.VMEM((rows, width), BF16),
            pltpu.VMEM((HEADS, block, 128), BF16),
            pltpu.VMEM((local, n_head, block, 128), BF16),
            pltpu.VMEM((group, HEAD_DIM), BF16),
            pltpu.VMEM((group, HEAD_DIM), BF16),
            pltpu.VMEM((group, HEAD_DIM), BF16),
            pltpu.VMEM((group, HEAD_DIM), BF16),
            pltpu.VMEM((HEAD_DIM, group), BF16),
            pltpu.VMEM((HEAD_DIM, group), BF16),
            pltpu.VMEM((HEAD_DIM, group), F32),
            pltpu.VMEM((2, group, rows), F32),
            pltpu.VMEM((2, group, rows), BF16),
            pltpu.VMEM((8, rows), F32),
            pltpu.VMEM((local, n_head, rows // 2, 128), BF16),
            pltpu.VMEM((HEADS, rows // 2, 128), BF16),
            dma((2,)),
            dma((local, n_head - 1)),
            dma((local, n_head - 1)),
            dma((local, n_head - 1)),
            dma((local, n_head - 1)),
            dma((local,)),
            dma((4,)),
        ],
        compiler_params=pltpu.CompilerParams(collective_id=1, has_side_effects=True, vmem_limit_bytes=56 * MiB),
        cost_estimate=pl.CostEstimate(flops=10**10, bytes_accessed=2 * 10**7, transcendentals=10**7),
        name="front",
    )(tokens, mixw, prow, crop, *small, wqkv)


GELU_POLY = (0.254829592, -0.284496736, 1.421413741, -1.453152027, 1.061405429)
FC_TILE = 768
PIECE = 384


def gelu_and_slope(pre):
    bell = jnp.exp(-0.5 * pre * pre)
    t = 1.0 / (1.0 + (0.3275911 * 0.7071067811865476) * jnp.abs(pre))
    poly = GELU_POLY[4]
    for coefficient in GELU_POLY[3::-1]:
        poly = poly * t + coefficient
    tail = 0.5 * poly * t * bell
    phi = jnp.where(pre >= 0.0, 1.0 - tail, tail)
    return pre * phi, phi + pre * bell * 0.3989422804014327


def put_blocks(ref, lead, value):
    if len(ref.shape) == len(lead) + 5:
        rows = value.shape[0] // 8
        for c in range(8):
            ref[(*lead, c % 2, c // 2 % 2, c // 4)] = value[c * rows : (c + 1) * rows].astype(BF16)
    else:
        ref[lead] = value.astype(BF16)


def middle_kernel(
    cut,
    att, mixed, cot, bout_r, gain_r, bias_r, bfc2_r, bfc1_r, wout_h, w1_h, w2_h,
    layer_o, attg_o, mg_o, jfc_o, gout_o, sm_o,
    wout, w1, w2, mid_s, n2_s, n2t_s, cott_s, out_s, dn_s, pre_s, gw_s, act_s, pg_s, proj_s, jfc,
    w_sem, j_sem,
):
    rows, width = cot.shape
    tiles = w1_h.shape[1] // FC_TILE
    wout_copy = pltpu.make_async_copy(wout_h, wout, w_sem.at[0, 0])
    wout_copy.start()
    w_copies = []
    for t in range(tiles):
        at = slice(t * FC_TILE, (t + 1) * FC_TILE)
        pair = (
            pltpu.make_async_copy(w1_h.at[:, at], w1.at[t], w_sem.at[1, t]),
            pltpu.make_async_copy(w2_h.at[at], w2.at[t], w_sem.at[2, t]),
        )
        for copy in pair:
            copy.start()
        w_copies.append(pair)
    sm_o[...] = jnp.zeros_like(sm_o)
    bout, gain, bias, bfc2, bfc1 = [as_line(r).astype(F32) for r in (bout_r, gain_r, bias_r, bfc2_r, bfc1_r)]
    cott_s[...] = jnp.transpose(cot[...])
    wout_copy.wait()
    step = 128
    mid_s[...] = mixed[...] + dot(att[...], wout[...]) + bout

    def norm2(part):
        mid = mid_s[part]
        mean = jnp.mean(mid, axis=1, keepdims=True)
        centered = mid - mean
        rstd = lax.rsqrt(jnp.mean(centered * centered, axis=1, keepdims=True) + EPS)
        return mid, centered * rstd, rstd

    total = jnp.zeros((1, width), F32)
    for r in range(0, rows, step):
        part = slice(r, r + step)
        mid, unit, _ = norm2(part)
        n2_s[part] = (unit * gain + bias).astype(BF16)
        out_s[part] = mid + bfc2
        dn_s[part] = jnp.zeros((step, width), F32)
        total = total + jnp.sum(cot[part].astype(F32), axis=0, keepdims=True)
    sm_o[7:8, :] = total
    n2t_s[...] = jnp.transpose(n2_s[...])

    def first_products(t):
        for copy in w_copies[t]:
            copy.wait()
        pre_s[t % 2] = dot(n2_s[...], w1[t]) + bfc1[:, t * FC_TILE : (t + 1) * FC_TILE]
        gw_s[t % 2] = dot_nt(cot[...], w2[t])

    j_copies = []
    first_products(0)
    for t in range(tiles):
        now, core, x = t % 2, t % 2, t // 2
        if t + 1 < tiles:
            first_products(t + 1)
        sums = jnp.zeros((1, FC_TILE), F32)
        for r in range(0, rows, 32):
            part = slice(r, r + 32)
            act, slope = gelu_and_slope(pre_s[now, part])
            act_s[now, part] = act.astype(BF16)
            pg = (gw_s[now, part] * slope).astype(BF16)
            pg_s[now, part] = pg
            sums = sums + jnp.sum(pg.astype(F32), axis=0, keepdims=True)
        sm_o[8 + t : 9 + t, :] = sums
        out_s[...] += dot(act_s[now], w2[t])
        dn_s[...] += dot_nt(pg_s[now], w1[t])
        g1 = dot(n2t_s[...], pg_s[now])
        for half in range(2):
            put_blocks(jfc, (half, core, x), g1[:, PIECE * half : PIECE * (half + 1)])
        g2 = dot(cott_s[...], act_s[now])
        places = [(0, core, x), (1, core, x)]
        if cut:
            for b in range(8):
                for s in range(2):
                    piece = g2[96 * b : 96 * (b + 1), PIECE * s : PIECE * (s + 1)].astype(BF16)
                    jfc[2 + b % 2, b // 2 % 2, b // 4, s, core, x] = piece
            places.append((slice(2, 4), slice(0, 2), slice(0, 2), slice(0, 2), core, x))
        else:
            for half in range(2):
                jfc[2 + half, core, x] = g2[:, PIECE * half : PIECE * (half + 1)].astype(BF16)
            places += [(2, core, x), (3, core, x)]
        for n, place in enumerate(places):
            j_copies.append(pltpu.make_async_copy(jfc.at[place], jfc_o.at[place], j_sem.at[t, n]))
            j_copies[-1].start()

    sums = [jnp.zeros((1, width), F32)] * 3
    for r in range(0, rows, step):
        part = slice(r, r + step)
        layer_o[part] = out_s[part].astype(BF16)
        _, unit, rstd = norm2(part)
        dn = dn_s[part]
        e = dn * gain
        inner = e - jnp.mean(e, axis=1, keepdims=True) - unit * jnp.mean(e * unit, axis=1, keepdims=True)
        mg = cot[part].astype(F32) + rstd * inner
        mg_o[part] = mg
        proj = mg.astype(BF16)
        proj_s[part] = proj
        for k, term in enumerate((proj.astype(F32), dn * unit, dn)):
            sums[k] = sums[k] + jnp.sum(term, axis=0, keepdims=True)
    for k in range(3):
        sm_o[4 + k : 5 + k, :] = sums[k]
    attg = dot_nt(proj_s[...], wout[...])
    for i in range(HEADS):
        attg_o[i] = halves_to_lanes(attg[:, HEAD_DIM * i : HEAD_DIM * (i + 1)]).astype(BF16)
    gout = dot_tn(att[...], proj_s[...])
    for k in range(2):
        put_blocks(gout_o, (k,), gout[:, PIECE * k : PIECE * (k + 1)])
    for copy in j_copies:
        copy.wait()


def middle(cut, att, mixed, cot, small, wout, w1, w2):
    rows, width = cot.shape
    vmem = pl.BlockSpec(memory_space=pltpu.VMEM)
    hbm = pl.BlockSpec(memory_space=pl.ANY)
    dma = pltpu.SemaphoreType.DMA
    shape = jax.ShapeDtypeStruct
    ff = w1.shape[1]
    jfc_dims = (4, 2, 2, 2, 2, 2, 96, PIECE) if cut else (4, 2, 2, width, PIECE)
    gout_dims = (2, 2, 2, 2, 96, PIECE) if cut else (2, width, PIECE)
    full = lambda kind: pltpu.VMEM((rows, width), kind)
    tile = lambda kind: pltpu.VMEM((2, rows, FC_TILE), kind)
    return pl.pallas_call(
        functools.partial(middle_kernel, cut),
        out_shape=(
            shape((rows, width), BF16),
            shape((HEADS, rows // 2, 128), BF16),
            shape((rows, width), F32),
            shape(jfc_dims, BF16),
            shape(gout_dims, BF16),
            shape((16, width), F32),
        ),
        in_specs=[vmem] * 8 + [hbm] * 3,
        out_specs=(vmem, vmem, vmem, hbm, vmem, vmem),
        scratch_shapes=[
            pltpu.VMEM((width, width), BF16),
            pltpu.VMEM((ff // FC_TILE, width, FC_TILE), BF16),
            pltpu.VMEM((ff // FC_TILE, FC_TILE, width), BF16),
            full(F32), full(BF16),
            pltpu.VMEM((width, rows), BF16), pltpu.VMEM((width, rows), BF16),
            full(F32), full(F32), tile(F32), tile(F32), tile(BF16), tile(BF16), full(BF16),
            pltpu.VMEM(jfc_dims, BF16),
            dma((3, 4)), dma((4, 4)),
        ],
        compiler_params=pltpu.CompilerParams(vmem_limit_bytes=60 * MiB),
        cost_estimate=pl.CostEstimate(flops=2 * 8 * 10**9, bytes_accessed=3 * 10**7, transcendentals=4 * 10**6),
        name="middle",
    )(att, mixed, cot, *small, wout, w1, w2)


class Reduction:
    AXES = ("x", "y", "lo", "hi")

    def __init__(self, acc, received, fin, send_sem, recv_sem, bits, peers, others, order):
        self.acc, self.received, self.fin = acc, received, fin
        self.send_sem, self.recv_sem = send_sem, recv_sem
        self.bits, self.peers, self.others, self.order = bits, peers, others, order

    def remote(self, k, src, dst, axis, peer=None):
        return pltpu.make_async_remote_copy(
            src_ref=src, dst_ref=dst, send_sem=self.send_sem.at[k], recv_sem=self.recv_sem.at[k],
            device_id=peer or self.peers[axis], device_id_type=MESH,
        )

    def add(self, into, received, lead, free):
        for place in itertools.product((0, 1), repeat=len(free)):
            index = list(lead)
            for axis, p in zip(free, place):
                index[self.AXES.index(axis)] = p
            index = tuple(index)
            into[index] = into[index] + received[place]

    def steps(self, source, core_half):
        copy = self.remote(0, source, self.received[0], "core")
        copy.start()
        if core_half is not None:
            core_half.start()
        yield
        copy.wait()
        if core_half is not None:
            core_half.wait()
        self.add(self.acc, self.received[0], [None] * 4, list(self.AXES))
        lead = [slice(None)] * 4
        free = list(self.AXES)
        for k, axis in enumerate(self.order):
            at = self.AXES.index(axis)
            lead[at] = 1 - self.bits[axis]
            copy = self.remote(1 + k, self.acc.at[tuple(lead)], self.received[1 + k], axis)
            copy.start()
            lead[at] = self.bits[axis]
            free.remove(axis)
            yield
            copy.wait()
            self.add(self.acc, self.received[1 + k], lead, free)
        bc, bx = self.bits["core"], self.bits["x"]
        mine = pltpu.make_async_copy(self.acc.at[tuple(lead)], self.fin.at[bc, bx], self.send_sem.at[8])
        mine.start()
        mine.wait()
        copies = [
            self.remote(5 + n, self.fin.at[bc, bx], self.fin.at[bc, bx], None, other) for n, other in enumerate(self.others)
        ]
        for copy in copies:
            copy.start()
        yield
        for copy in copies:
            copy.wait()


def tick(*jobs):
    for job in jobs:
        next(job, None)


def back_kernel(
    n_crop, n_head, cut,
    attg, grp_h, own, lse, jfc_h, gout, wqkv_h, normed_h, mixed_h, mg_h, mixw_r, prow_r, crop, gain_r, sm_in,
    *rest,
):
    (
        grad_o, fin_o, sm_o,
        grp, wqkv, normt, mixed, mg_s, dor, k_s, v_s, kt_s, qt_s, dot_s, dqt_s, s_s, dp_s, pds_s, dzq_s, dkv_s, dq_s, di_s, msg, ret, dn_s, sent_s, back_s,
        ja, jb, load_sem, do_send, do_recv, dq_send, dq_recv, own_sem, far_sem,
        *reduce_refs,
    ) = rest
    rows, width = mixed.shape
    group = rows * n_head
    local = HEADS // n_head
    c, h = lax.axis_index("crop"), lax.axis_index("head")
    far = lax.rem(c + n_crop // 2, n_crop)
    others = [lax.rem(h + o, n_head) for o in range(1, n_head)]
    peers = [(far, h)] + [(c, other) for other in others]
    if cut:
        bits = {"core": lax.rem(h, 2), "x": lax.div(h, 2), "y": lax.rem(c, 2), "lo": lax.rem(lax.div(c, 2), 2), "hi": lax.div(c, 4)}
        near = {
            "core": (c, h + 1 - 2 * bits["core"]),
            "x": (c, h + 2 - 4 * bits["x"]),
            "y": (c + 1 - 2 * bits["y"], h),
            "lo": (c + 2 - 4 * bits["lo"], h),
            "hi": (far, h),
        }
        peers += [near["y"], near["lo"]]
    greet(peers)

    def spread(j, source, target, send_sem, recv_sem):
        copies = [pltpu.make_async_copy(source(h), target(h), own_sem.at[j])]
        for o, other in enumerate(others):
            copies.append(
                pltpu.make_async_remote_copy(
                    src_ref=source(other), dst_ref=target(h), send_sem=send_sem.at[j, o], recv_sem=recv_sem.at[j, o],
                    device_id=(c, other), device_id_type=MESH,
                )
            )
        for copy in copies:
            copy.start()
        return copies

    do_copies = [
        spread(j, lambda d, j=j: attg.at[d * local + j], lambda s, j=j: dor.at[j, s], do_send, do_recv) for j in range(local)
    ]
    loads = [
        pltpu.make_async_copy(a, b, load_sem.at[k])
        for k, (a, b) in enumerate([(grp_h, grp), (normed_h, sent_s), (wqkv_h, wqkv), (mixed_h, mixed), (mg_h, mg_s)])
    ]
    loads += [pltpu.make_async_copy(gout.at[k], ja.at[k, 0], load_sem.at[5 + k]) for k in range(2)]
    for load in loads:
        load.start()
    jobs, plan = [], {}
    if cut:
        send_sem, recv_sem, half_sem, sm_send, sm_recv, sm_r, acc_s, *received = reduce_refs
        orders = [
            ("y", "hi", "lo", "x"), ("lo", "y", "hi", "x"), ("y", "lo", "hi", "x"), ("lo", "y", "hi", "x"),
            ("lo", "x", "y", "hi"), ("y", "x", "lo", "hi"),
        ]
        for k in range(6):
            acc = acc_s.at[k] if k < 4 else (ja, jb)[k - 4].at[bits["core"]]
            red = Reduction(acc, [r.at[k] for r in received], fin_o.at[k], send_sem.at[k], recv_sem.at[k], bits, near, peers[1:n_head], orders[k])
            if k < 4:
                keep = pltpu.make_async_copy(jfc_h.at[k, bits["core"]], acc, half_sem.at[k])
                jobs.append(red.steps(jfc_h.at[k, 1 - bits["core"]], keep))
            else:
                jobs.append(red.steps((ja, jb)[k - 4].at[1 - bits["core"]], None))
        fc1, fc2, fc3, fc4, joba, jobb = jobs
        plan = {
            (0, "first"): (fc1, fc2),
            (0, 2): (fc1, fc2, fc3, fc4),
            (1, 2): (fc1, fc2, fc3, fc4),
            (1, "end"): (joba,),
            (2, 2): (fc1, fc2, fc4),
            (2, 5): (fc3, joba, fc1),
            (2, "end"): (fc2, fc4),
            "last": (jobb, fc3, fc1, fc4, fc2),
        }

    bound = crop[0, 0]
    first_case = bound < group // 2
    quarter = rows // 4
    short, long0 = 3 * quarter, 4 * quarter
    in_col = either_in_long(first_case, bound, (quarter, 1), 0, group) > 0.5
    in_row = either_in_long(first_case, bound, (1, quarter), 1, group) > 0.5
    col_long, col_short = jnp.where(in_col, 0.0, NEG), jnp.where(in_col, NEG, 0.0)
    row_long, row_short = jnp.where(in_row, 0.0, NEG), jnp.where(in_row, NEG, 0.0)
    lane = lax.broadcasted_iota(jnp.int32, (8, 128), 1) // HEAD_DIM
    ones = (lane == lax.broadcasted_iota(jnp.int32, (8, 128), 0)).astype(F32).astype(BF16)
    sums_q, sums_v = [None] * HEADS, [None] * HEADS
    dq_copies = []

    def head_grads(j):
        for copy in dq_copies[j]:
            copy.wait()
        total = dn_s[...] if j else 0.0
        for pair in range(n_head // 2):
            packs = []
            for d in (2 * pair, 2 * pair + 1):
                i = d * local + j
                vk = ret[i, 0:rows]
                dq = lanes_to_halves(ret[i, rows : rows + rows // 2])
                dk, dv = vk[:, HEAD_DIM:], vk[:, :HEAD_DIM]
                sums_q[i] = jnp.sum(dq.astype(F32), axis=0, keepdims=True)
                sums_v[i] = jnp.sum(dv.astype(F32), axis=0, keepdims=True)
                odd = i % 2
                base = 3 * HEAD_DIM * i - HEAD_DIM * odd
                none = jnp.zeros_like(dq)
                wide = jnp.concatenate([none, dq, dk, dv] if odd else [dq, dk, dv, none], axis=1)
                total = total + dot_nt(wide, wqkv[:, base : base + 4 * HEAD_DIM])
                packs += [dq, dk, dv]
            grad = dot(normt[...], jnp.concatenate(packs, axis=1))
            if j == 0:
                put_blocks(ja, (pair, 1), grad)
            else:
                put_blocks(jb, (pair, j - 1), grad)
        dn_s[...] = total

    for j in range(local):
        for copy in do_copies[j]:
            copy.wait()
        if j == 0:
            loads[0].wait()
            tick(*plan.get((0, "first"), ()))
        rowd = []
        for s in range(n_head):
            prod = dor[j, s].astype(F32) * own[j, s].astype(F32)
            hi = prod.astype(BF16)
            d8 = dot_nt(ones, hi) + dot_nt(ones, (prod - hi.astype(F32)).astype(BF16))
            rowd.append(jnp.concatenate([d8[0:1], d8[1:2]], axis=1))
        end = lax.select(first_case, rowd[0], rowd[3])
        full = lax.select(first_case, rowd[3], rowd[0])
        ends = [end[:, quarter * k : quarter * (k + 1)] for k in range(4)]
        first, last = lax.select(first_case, ends[0], ends[3]), lax.select(first_case, ends[3], ends[0])
        di_s[0:1, :] = jnp.concatenate([first, ends[1], ends[2], last, full, rowd[1], rowd[2]], axis=1)
        qk = sorted_blocks(first_case, [grp[j, s, 0:rows] for s in range(n_head)])
        vv = sorted_blocks(first_case, [lanes_to_halves(grp[j, s, rows : rows + rows // 2]) for s in range(n_head)])
        dd = sorted_blocks(first_case, [lanes_to_halves(dor[j, s]) for s in range(n_head)])
        at = 0
        for a, b, d in zip(qk, vv, dd):
            n = a.shape[0]
            q = a[:, :HEAD_DIM] * BF16(HEAD_DIM**-0.5)
            k_s[at : at + n] = a[:, HEAD_DIM:]
            v_s[at : at + n] = b
            qt_s[:, at : at + n] = jnp.transpose(q)
            dot_s[:, at : at + n] = jnp.transpose(d)
            block, inner = at // rows, at % rows
            dzq_s[block, inner : inner + n] = jnp.concatenate([d, jnp.zeros_like(d)], axis=1)
            dzq_s[block, rows + inner : rows + inner + n] = jnp.concatenate([jnp.zeros_like(q), q], axis=1)
            at += n
        kt_s[...] = jnp.transpose(k_s[...])
        dqt_s[...] = jnp.zeros_like(dqt_s)
        dkv_s[...] = jnp.zeros_like(dkv_s)

        def area(q0, count, k0, k1, masks):
            lanes, number = slice(q0, q0 + count), k1 - k0
            s_s[:number, :count] = dot(k_s[k0:k1], qt_s[:, lanes])
            dp_s[:number, :count] = dot(v_s[k0:k1], dot_s[:, lanes])
            for k, mask in masks.items():
                if k0 <= k < k1:
                    s_s[k - k0 : k - k0 + quarter, :count] += mask
            for at in range(0, count, LANES):
                wide = min(LANES, count - at)
                here, place = slice(at, at + wide), slice(q0 + at, q0 + at + wide)
                lse_row, di_row = lse[j : j + 1, place], di_s[0:1, place]
                for k in range(0, number, KEYS):
                    keys = slice(k, k + KEYS)
                    p = jnp.exp(s_s[keys, here] - lse_row)
                    ds = p * (dp_s[keys, here] - di_row)
                    pds_s[keys, here] = p.astype(BF16)
                    pds_s[keys, rows + at : rows + at + wide] = ds.astype(BF16)
            block, inner = q0 // rows, q0 % rows
            if count == rows:
                add = dot(pds_s[:number], dzq_s[block])
            else:
                add = dot(pds_s[:number, :count], dzq_s[block, inner : inner + count])
                add = add + dot(pds_s[:number, rows : rows + count], dzq_s[block, rows + inner : rows + inner + count])
            dkv_s[k0:k1] += add
            dqt_s[:, lanes] += dot(kt_s[:, k0:k1], pds_s[:number, rows : rows + count])

        area(0, short, 0, long0, {short: col_short})
        either = {k: row_short for k in range(0, short, quarter)}
        either[short] = jnp.where(in_row, col_long, col_short)
        either.update({k: row_long for k in range(long0, group, quarter)})
        for k in range(0, group, rows):
            area(short, quarter, k, k + rows, either)
        tick(*plan.get((j, "near"), ()))
        half_keys = (group - short) // 2
        for t in range(n_head - 1):
            for half in range(2):
                k = short + half * half_keys
                area(long0 + t * rows, rows, k, k + half_keys, {short: col_long})
                tick(*plan.get((j, 2 * t + half), ()))
        dq_s[...] = jnp.transpose(dqt_s[...] * HEAD_DIM**-0.5).astype(BF16)

        dkv = unsorted_blocks(first_case, dkv_s[...])
        dqu = unsorted_blocks(first_case, dq_s[...])
        for s in range(n_head):
            msg[j, s, 0:rows] = dkv[s].astype(BF16)
            msg[j, s, rows : rows + rows // 2] = halves_to_lanes(dqu[s])
        dq_copies.append(spread(j, lambda d, j=j: msg.at[j, d], lambda s, j=j: ret.at[s * local + j], dq_send, dq_recv))
        if j == 0:
            for load in loads[1:]:
                load.wait()
            normt[...] = jnp.transpose(sent_s[...])
        else:
            head_grads(j - 1)
        tick(*plan.get((j, "end"), ()))

    head_grads(local - 1)
    tick(*plan.get("last", ()))
    share = as_column(as_line(mixw_r))
    gain = as_line(gain_r).astype(F32)
    sums = [jnp.zeros((1, width), F32)] * 2
    scaled = []
    step = 128
    for r in range(0, rows, step):
        part = slice(r, r + step)
        mix = mixed[part]
        mean = jnp.mean(mix, axis=1, keepdims=True)
        centered = mix - mean
        rstd = lax.rsqrt(jnp.mean(centered * centered, axis=1, keepdims=True) + EPS)
        unit = centered * rstd
        dn = dn_s[part]
        e = dn * gain
        inner = e - jnp.mean(e, axis=1, keepdims=True) - unit * jnp.mean(e * unit, axis=1, keepdims=True)
        grad = mg_s[part] + rstd * inner
        sums[0] = sums[0] + jnp.sum(dn * unit, axis=0, keepdims=True)
        sums[1] = sums[1] + jnp.sum(dn, axis=0, keepdims=True)
        mixed[part] = share[part] * grad
        dn_s[part] = (1.0 - share[part]) * grad
    chosen = lax.broadcasted_iota(jnp.int32, (rows, rows), 0) == as_line(prow_r)
    chosen = chosen.astype(F32).astype(BF16)
    given = dn_s[...]
    high = given.astype(BF16)
    low = (given - high.astype(F32)).astype(BF16)
    sent_s[...] = (dot(chosen, high) + dot(chosen, low)).astype(BF16)
    far_copy = pltpu.make_async_remote_copy(
        src_ref=sent_s, dst_ref=back_s, send_sem=far_sem.at[0], recv_sem=far_sem.at[1], device_id=(far, h), device_id_type=MESH
    )
    far_copy.start()
    sm_o[...] = sm_in[...]
    sm_o[0:1, :] = sums[0]
    sm_o[1:2, :] = sums[1]
    sm_o[2:3, :] = jnp.concatenate(sums_q, axis=1)
    sm_o[3:4, :] = jnp.concatenate(sums_v, axis=1)
    if cut:
        def small_sum():
            for k, axis in enumerate(("core", "x", "y", "lo", "hi")):
                copy = pltpu.make_async_remote_copy(
                    src_ref=sm_o, dst_ref=sm_r.at[k], send_sem=sm_send.at[k], recv_sem=sm_recv.at[k],
                    device_id=near[axis], device_id_type=MESH,
                )
                copy.start()
                yield
                copy.wait()
                sm_o[...] += sm_r[k]

        small = small_sum()
        tick(small, jobb, fc3, fc4, joba, fc1, fc2, small, fc3, fc4, joba, small, fc3, joba, jobb, small, jobb, small, jobb)
    else:
        fin_o[0] = ja[...]
        fin_o[1] = jb[...]
    far_copy.wait()
    for r in range(0, rows, step):
        part = slice(r, r + step)
        grad_o[part] = (mixed[part] + back_s[part].astype(F32)).astype(BF16)
    if cut:
        tick(small, joba, jobb, joba, jobb)


def back(n_crop, n_head, cut, attg, grp, own, lse, jfc, gout, wqkv, normed, mixed, mg, mixw, prow, crop, gain, sm):
    rows, width = mixed.shape
    group, local = rows * n_head, HEADS // n_head
    vmem = pl.BlockSpec(memory_space=pltpu.VMEM)
    hbm = pl.BlockSpec(memory_space=pl.ANY)
    smem = pl.BlockSpec(memory_space=pltpu.SMEM)
    dma = pltpu.SemaphoreType.DMA
    shape = jax.ShapeDtypeStruct
    block = rows + rows // 2
    jq_dims = (2, 2, 2, 2, 2, 96, PIECE) if cut else (2, 2, width, PIECE)
    finals = (6, 2, 2, 96, PIECE) if cut else (2, *jq_dims)
    square = lambda n, kind: pltpu.VMEM((group, n), kind)
    scratch = [
        pltpu.VMEM((local, n_head, block, 128), BF16),
        pltpu.VMEM(wqkv.shape, BF16),
        pltpu.VMEM((width, rows), BF16),
        pltpu.VMEM((rows, width), F32),
        pltpu.VMEM((rows, width), F32),
        pltpu.VMEM((local, n_head, rows // 2, 128), BF16),
        square(HEAD_DIM, BF16), square(HEAD_DIM, BF16),
        pltpu.VMEM((HEAD_DIM, group), BF16), pltpu.VMEM((HEAD_DIM, group), BF16), pltpu.VMEM((HEAD_DIM, group), BF16),
        pltpu.VMEM((HEAD_DIM, group), F32),
        pltpu.VMEM((832, rows), F32), pltpu.VMEM((832, rows), F32), pltpu.VMEM((832, 2 * rows), BF16),
        pltpu.VMEM((n_head, 2 * rows, 128), BF16), square(128, F32), square(HEAD_DIM, BF16),
        pltpu.VMEM((8, group), F32),
        pltpu.VMEM((local, n_head, block, 128), BF16),
        pltpu.VMEM((HEADS, block, 128), BF16),
        pltpu.VMEM((rows, width), F32),
        pltpu.VMEM((rows, width), BF16),
        pltpu.VMEM((rows, width), BF16),
        pltpu.VMEM(jq_dims, BF16),
        pltpu.VMEM(jq_dims, BF16),
        dma((7,)),
        dma((local, n_head - 1)), dma((local, n_head - 1)), dma((local, n_head - 1)), dma((local, n_head - 1)),
        dma((local,)),
        dma((2,)),
    ]
    if cut:
        scratch += [dma((6, 9)), dma((6, 9)), dma((4,)), dma((5,)), dma((5,)), pltpu.VMEM((5, 16, width), F32)]
        scratch.append(pltpu.VMEM((4, 2, 2, 2, 2, 96, PIECE), BF16))
        scratch += [pltpu.VMEM((6,) + (2,) * n + (96, PIECE), BF16) for n in (4, 3, 2, 1, 0)]
    return pl.pallas_call(
        functools.partial(back_kernel, n_crop, n_head, cut),
        out_shape=(shape((rows, width), BF16), shape(finals, BF16), shape((16, width), F32)),
        in_specs=[hbm, hbm, vmem, vmem, hbm, hbm, hbm, hbm, hbm, hbm, vmem, vmem, smem, vmem, vmem],
        out_specs=(vmem,) * 3,
        scratch_shapes=scratch,
        compiler_params=pltpu.CompilerParams(collective_id=2, has_side_effects=True, vmem_limit_bytes=60 * MiB),
        cost_estimate=pl.CostEstimate(flops=2 * 10**10, bytes_accessed=3 * 10**7, transcendentals=10**7),
        name="back",
    )(attg, grp, own, lse, jfc, gout, wqkv, normed, mixed, mg, mixw, prow, crop, gain, sm)


def finish_kernel(n_crop, n_head, grad, fin, sm, *outs):
    grad_o, g1_o, b1_o, gq_o, bq_o, bv_o, go_o, bo_o, g2_o, b2_o, gf1_o, bf1_o, gf2_o, bf2_o = outs
    c = lax.axis_index("crop")
    local = HEADS // n_head
    grad_o[...] = grad[...]
    parts = []
    for k in range(4):
        core, x = k % 2, k // 2
        for half in range(2):
            at = FC_TILE * k + PIECE * half
            gf1_o[:, at : at + PIECE] = fin[half, core, x].astype(F32)
        both = jnp.concatenate([fin[2, core, x], fin[3, core, x]], axis=0)
        parts.append(jnp.transpose(both.astype(F32)))
    gf2_o[...] = jnp.concatenate(parts, axis=1)
    for k in range(2):
        go_o[:, PIECE * k : PIECE * (k + 1)] = fin[4, k, 0].astype(F32)
    parts = []
    for i in range(HEADS):
        d, j = i // local, i % local
        piece = fin[4, d // 2, 1] if j == 0 else fin[5, d // 2, j - 1]
        parts.append(piece[:, 192 * (d % 2) : 192 * (d % 2 + 1)].astype(F32))
    gq_o[...] = jnp.concatenate(parts, axis=1)
    piece = jnp.zeros((16, 96), F32)
    wide = jnp.zeros((1, PIECE), F32)
    for k in range(n_crop):
        piece = lax.select(c == k, sm[:, 96 * k : 96 * (k + 1)], piece)
        wide = lax.select(c == k, sm[8 + k // 2 : 9 + k // 2, PIECE * (k % 2) : PIECE * (k % 2 + 1)], wide)
    for row, out in ((0, g1_o), (1, b1_o), (2, bq_o), (3, bv_o), (4, bo_o), (5, g2_o), (6, b2_o), (7, bf2_o)):
        out[...] = piece[row : row + 1].reshape(96)
    bf1_o[...] = wide.reshape(PIECE)


def finish(n_crop, n_head, grad, fin, sm):
    rows, width = grad.shape
    vmem = pl.BlockSpec(memory_space=pltpu.VMEM)
    shape = jax.ShapeDtypeStruct
    short = shape((96,), F32)
    outs = (
        shape((rows, width), BF16), short, short, shape((96, 3 * width), F32), short, short, shape((96, width), F32), short,
        short, short, shape((96, 4 * width), F32), shape((PIECE,), F32), shape((PIECE, width), F32), short,
    )
    return pl.pallas_call(
        functools.partial(finish_kernel, n_crop, n_head),
        out_shape=outs,
        in_specs=[vmem] * 3,
        out_specs=(vmem,) * len(outs),
        compiler_params=pltpu.CompilerParams(vmem_limit_bytes=60 * MiB),
        name="finish",
    )(grad, fin, sm)


def sum_everywhere(grads, small, n_crop, n_head):
    c = lax.axis_index("crop")

    def scatter(value):
        part = lax.psum_scatter(value.astype(F32), "crop", scatter_dimension=0, tiled=True)
        return lax.psum(part.astype(BF16), "head").astype(F32)

    jfc, ja, jb = grads
    width = jfc.shape[3]
    local = HEADS // n_head
    g1 = jnp.concatenate([jfc[half, t % 2, t // 2] for t in range(4) for half in range(2)], axis=1)
    g2 = jnp.concatenate([jfc[2 + half, t % 2, t // 2] for t in range(4) for half in range(2)], axis=1).T
    go = jnp.concatenate([ja[0, 0], ja[1, 0]], axis=1)
    parts = []
    for i in range(HEADS):
        d, j = i // local, i % local
        piece = ja[d // 2, 1] if j == 0 else jb[d // 2, j - 1]
        parts.append(piece[:, 192 * (d % 2) : 192 * (d % 2 + 1)])
    gq = jnp.concatenate(parts, axis=1)
    total = lax.psum(small, ("crop", "head"))

    def mine(vector):
        count = vector.shape[0] // n_crop
        return lax.dynamic_slice_in_dim(vector, c * count, count, 0)

    rows = [mine(total[k]) for k in range(8)]
    return [
        rows[0], rows[1], scatter(gq), rows[2], rows[3], scatter(go), rows[4], rows[5], rows[6],
        scatter(g1), mine(total[8:12].reshape(4 * width)), scatter(g2), rows[7],
    ]


def shards(
    tokens, mix_weight, partner_row, crop_lengths, ln1_gain, ln1_bias, w_qkv, b_query, b_value, w_out, b_out,
    ln2_gain, ln2_bias, w_fc1, b_fc1, w_fc2, b_fc2, cotangent,
):
    n_crop, n_head = lax.axis_size("crop"), lax.axis_size("head")
    cut = n_crop == 8 and n_head == 4
    small1, small2 = (ln1_gain, ln1_bias, b_query, b_value), (b_out, ln2_gain, ln2_bias, b_fc2, b_fc1)
    mixed, normed, grp, att, own, lse = front(n_crop, n_head, tokens, mix_weight, partner_row, crop_lengths, small1, w_qkv)
    layer_out, attg, mg, jfc, gout, sm = middle(cut, att, mixed, cotangent, small2, w_out, w_fc1, w_fc2)
    grad, fin, sm = back(
        n_crop, n_head, cut, attg, grp, own, lse, jfc, gout, w_qkv, normed, mixed, mg, mix_weight, partner_row, crop_lengths, ln1_gain, sm
    )
    if not cut:
        return (layer_out, grad, *sum_everywhere((jfc, fin[0], fin[1]), sm, n_crop, n_head))
    outs = finish(n_crop, n_head, grad, fin, sm)
    return (layer_out, *outs)


def solution(mesh):
    rows, one = P(("crop", "head"), None), P(("crop", "head"))
    in_specs = (rows, one, one, P("crop", None)) + (P(),) * 13 + (rows,)
    vector, matrix = P("crop"), P("crop", None)
    out_specs = (
        rows, rows, vector, vector, matrix, vector, vector, matrix, vector, vector, vector, matrix, vector, matrix, vector,
    )
    return jax.shard_map(shards, mesh=mesh, in_specs=in_specs, out_specs=out_specs, check_vma=False)
```

```python
import functools
import itertools

import jax
import jax.numpy as jnp
from jax import lax
from jax.experimental import pallas as pl
from jax.experimental.pallas import tpu as pltpu
from jax.sharding import PartitionSpec as P

HEADS = 12
HEAD_DIM = 64
EPS = 1e-06
NEG = -1e30
KEYS = 64
LANES = 256
FC_TILE = 768
MESH = pl.DeviceIdType.MESH
F32 = jnp.float32
BF16 = jnp.bfloat16
MiB = 1 << 20


def dot(left, right):
    return jnp.dot(left, right, preferred_element_type=F32)


def dot_nt(left, right):
    return lax.dot_general(left, right, (((1,), (1,)), ((), ())), preferred_element_type=F32)


def dot_tn(left, right):
    return lax.dot_general(left, right, (((0,), (0,)), ((), ())), preferred_element_type=F32)


def as_line(ref):
    return ref[...].reshape(1, ref.shape[0])


def as_column(row):
    return jnp.transpose(jnp.broadcast_to(row, (8, row.shape[1])))[:, 0:1]


def as_row(column):
    return jnp.transpose(jnp.broadcast_to(column, (column.shape[0], 128)))[0:8]


def halves_to_lanes(block):
    half = block.shape[0] // 2
    return jnp.concatenate([block[:half], block[half:]], axis=1)


def lanes_to_halves(block):
    return jnp.concatenate([block[:, :HEAD_DIM], block[:, HEAD_DIM:]], axis=0)


def greet(peers):
    barrier = pltpu.get_barrier_semaphore()
    for peer in peers:
        pl.semaphore_signal(barrier, inc=1, device_id=peer, device_id_type=MESH)
    pl.semaphore_wait(barrier, len(peers))


def sorted_blocks(first_case, parts):
    end = lax.select(first_case, parts[0], parts[3])
    full = lax.select(first_case, parts[3], parts[0])
    q = end.shape[0] // 4
    near = lax.select(first_case, end[:q], end[3 * q :])
    either = lax.select(first_case, end[3 * q :], end[:q])
    return [near, end[q : 3 * q], either, full, parts[1], parts[2]]


def unsorted_blocks(first_case, block):
    n = block.shape[0] // 4
    q = n // 4
    low, mid, top = block[:q], block[q : 3 * q], block[3 * q : n]
    head = lax.select(first_case, low, top)
    tail = lax.select(first_case, top, low)
    end = jnp.concatenate([head, mid, tail], axis=0)
    full = block[n : 2 * n]
    return [
        lax.select(first_case, end, full),
        block[2 * n : 3 * n],
        block[3 * n :],
        lax.select(first_case, full, end),
    ]


def either_in_long(first_case, bound, shape, axis, group):
    place = lax.broadcasted_iota(jnp.int32, shape, axis)
    row = place + jnp.where(first_case, group // 4 - 128, group - group // 4)
    past = row >= bound
    return jnp.where(first_case, past.astype(F32), 1.0 - past.astype(F32))


def front_kernel(
    n_crop,
    n_head,
    tokens, mixw_r, prow_r, crop, gain_r, bias_r, bq_r, bv_r, wqkv, cot, w2_h,
    mixed_o, normed_o, grp_o, att_o, own_o, lse_o, gw_o, cott_o, gsum_o,
    prt, mixed_s, normed_s, msg, grp, q_s, k_s, v_s, o_s, qt_s, vt_s, ot_s, s_s, p_s, tot_s, own_s, att_r, w2, gw_s, cott_s,
    prt_sem, qkv_send, qkv_recv, att_send, att_recv, own_sem, out_sem, w2_sem, gw_sem,
):
    rows, width = tokens.shape
    group = rows * n_head
    local = HEADS // n_head
    c, h = lax.axis_index("crop"), lax.axis_index("head")
    far = lax.rem(c + n_crop // 2, n_crop)
    others = [lax.rem(h + o, n_head) for o in range(1, n_head)]
    greet([(far, h)] + [(c, other) for other in others])

    partner_copy = pltpu.make_async_remote_copy(
        src_ref=tokens, dst_ref=prt, send_sem=prt_sem.at[0], recv_sem=prt_sem.at[1], device_id=(far, h), device_id_type=MESH
    )
    partner_copy.start()
    mixw, prow = as_line(mixw_r), as_line(prow_r)
    gain, bias, query_bias, value_bias = [as_line(r).astype(F32) for r in (gain_r, bias_r, bq_r, bv_r)]
    share = as_column(mixw)
    chosen = lax.broadcasted_iota(jnp.int32, (rows, rows), 0) == prow
    chosen = chosen.astype(F32).astype(BF16)
    tiles = w2.shape[0]
    w2_copies = [
        pltpu.make_async_copy(w2_h.at[t * w2.shape[1] : (t + 1) * w2.shape[1]], w2.at[t], w2_sem.at[t]) for t in range(tiles)
    ]
    for copy in w2_copies:
        copy.start()
    gsum_o[...] = jnp.broadcast_to(jnp.sum(cot[...].astype(F32), axis=0, keepdims=True), gsum_o.shape)
    cott_s[...] = jnp.transpose(cot[...])
    gw_copies = [pltpu.make_async_copy(cott_s, cott_o, gw_sem.at[tiles])]
    gw_copies[0].start()
    for t in range(tiles):
        w2_copies[t].wait()
        gw_s[t] = dot_nt(cot[...], w2[t])
        gw_copies.append(pltpu.make_async_copy(gw_s.at[t], gw_o.at[t], gw_sem.at[t]))
        gw_copies[-1].start()
    partner_copy.wait()
    step = 128
    for r in range(0, rows, step):
        part = slice(r, r + step)
        gathered = dot_tn(chosen[:, part], prt[...])
        mix = share[part] * tokens[part].astype(F32) + (1.0 - share[part]) * gathered
        mixed_s[part] = mix
        mean = jnp.mean(mix, axis=1, keepdims=True)
        centered = mix - mean
        variance = jnp.mean(centered * centered, axis=1, keepdims=True)
        normed = centered * lax.rsqrt(variance + EPS) * gain + bias
        normed_s[part] = normed.astype(BF16)
    outs = [
        pltpu.make_async_copy(mixed_s, mixed_o, out_sem.at[0]),
        pltpu.make_async_copy(normed_s, normed_o, out_sem.at[1]),
    ]
    for out in outs:
        out.start()

    qkv_copies = []
    for j in range(local):
        for d in range(n_head):
            i = d * local + j
            odd = i % 2
            base = 3 * HEAD_DIM * i - HEAD_DIM * odd
            res = dot(normed_s[...], wqkv[:, base : base + 4 * HEAD_DIM])
            res = res[:, HEAD_DIM * odd : HEAD_DIM * odd + 3 * HEAD_DIM]
            bq = query_bias[:, HEAD_DIM * i : HEAD_DIM * (i + 1)]
            bv = value_bias[:, HEAD_DIM * i : HEAD_DIM * (i + 1)]
            res = res + jnp.concatenate([bq, jnp.zeros_like(bq), bv], axis=1)
            msg[i, 0:rows] = res[:, : 2 * HEAD_DIM].astype(BF16)
            msg[i, rows : rows + rows // 2] = halves_to_lanes(res[:, 2 * HEAD_DIM :]).astype(BF16)
        batch = [pltpu.make_async_copy(msg.at[h * local + j], grp.at[j, h], own_sem.at[j])]
        for o, other in enumerate(others):
            batch.append(
                pltpu.make_async_remote_copy(
                    src_ref=msg.at[other * local + j],
                    dst_ref=grp.at[j, h],
                    send_sem=qkv_send.at[j, o],
                    recv_sem=qkv_recv.at[j, o],
                    device_id=(c, other),
                    device_id_type=MESH,
                )
            )
        qkv_copies.append(batch)
        if j == 0:
            for copy in batch:
                copy.start()

    bound = crop[0, 0]
    first_case = bound < group // 2
    quarter = rows // 4
    short, long0 = 3 * quarter, 4 * quarter
    in_col = either_in_long(first_case, bound, (quarter, 1), 0, group) > 0.5
    in_row = either_in_long(first_case, bound, (1, quarter), 1, group) > 0.5
    col_long, col_short = jnp.where(in_col, 0.0, NEG), jnp.where(in_col, NEG, 0.0)
    row_long, row_short = jnp.where(in_row, 0.0, NEG), jnp.where(in_row, NEG, 0.0)
    att_copies = []
    for j in range(local):
        for copy in qkv_copies[j]:
            copy.wait()
        if j + 1 < local:
            for copy in qkv_copies[j + 1]:
                copy.start()
        qk = sorted_blocks(first_case, [grp[j, s, 0:rows] for s in range(n_head)])
        vv = sorted_blocks(first_case, [lanes_to_halves(grp[j, s, rows : rows + rows // 2]) for s in range(n_head)])
        at = 0
        for a, b in zip(qk, vv):
            n = a.shape[0]
            q_s[at : at + n] = a[:, :HEAD_DIM] * BF16(HEAD_DIM**-0.5)
            k_s[at : at + n] = a[:, HEAD_DIM:]
            v_s[at : at + n] = b
            at += n

        qt_s[...] = jnp.transpose(q_s[...])
        vt_s[...] = jnp.transpose(v_s[...])

        def area(slot, q0, count, k0, k1, masks):
            lanes, number = slice(q0, q0 + count), k1 - k0
            s_s[slot, :number, :count] = dot(k_s[k0:k1], qt_s[:, lanes])
            for k, mask in masks.items():
                s_s[slot, k - k0 : k - k0 + quarter, :count] += mask
            for at in range(0, count, LANES):
                wide = min(LANES, count - at)
                here = slice(at, at + wide)
                top = jnp.full((8, wide), NEG, F32)
                for k in range(0, number, KEYS):
                    top = jnp.maximum(top, jnp.max(s_s[slot, k : k + KEYS, here].reshape(KEYS // 8, 8, wide), axis=0))
                top = jnp.max(top, axis=0, keepdims=True)
                total = jnp.zeros((8, wide), F32)
                for k in range(0, number, KEYS):
                    p = jnp.exp(s_s[slot, k : k + KEYS, here] - top)
                    total = total + jnp.sum(p.reshape(KEYS // 8, 8, wide), axis=0)
                    p_s[slot, k : k + KEYS, here] = p.astype(BF16)
                total = jnp.sum(total, axis=0, keepdims=True)
                tot_s[slot : slot + 1, here] = 1.0 / total
                lse_o[j : j + 1, q0 + at : q0 + at + wide] = top + jnp.log(total)
            out = dot(vt_s[:, k0:k1], p_s[slot, :number, :count])
            ot_s[:, lanes] = out * tot_s[slot : slot + 1, :count]

        area(0, 0, short, 0, long0, {short: col_short})
        either = {k: row_short for k in range(0, short, quarter)}
        either[short] = jnp.where(in_row, col_long, col_short)
        either.update({k: row_long for k in range(long0, group, quarter)})
        area(1, short, quarter, 0, group, either)
        for t in range(n_head - 1):
            area(t % 2, long0 + t * rows, rows, short, group, {short: col_long})
        o_s[...] = jnp.transpose(ot_s[...]).astype(BF16)

        for s, block in enumerate(unsorted_blocks(first_case, o_s[...])):
            own_s[j, s] = halves_to_lanes(block)
        batch = [pltpu.make_async_copy(own_s.at[j, h], att_r.at[h * local + j], own_sem.at[j])]
        for o, other in enumerate(others):
            batch.append(
                pltpu.make_async_remote_copy(
                    src_ref=own_s.at[j, other],
                    dst_ref=att_r.at[h * local + j],
                    send_sem=att_send.at[j, o],
                    recv_sem=att_recv.at[j, o],
                    device_id=(c, other),
                    device_id_type=MESH,
                )
            )
        for copy in batch:
            copy.start()
        att_copies.append(batch)
    late = [pltpu.make_async_copy(grp, grp_o, out_sem.at[2]), pltpu.make_async_copy(own_s, own_o, out_sem.at[3])]
    for out in late:
        out.start()
    outs += late
    for batch in att_copies:
        for copy in batch:
            copy.wait()
    for p in range(HEADS // 2):
        even, odd = att_r[2 * p], att_r[2 * p + 1]
        top = jnp.concatenate([even[:, :HEAD_DIM], odd[:, :HEAD_DIM]], axis=1)
        low = jnp.concatenate([even[:, HEAD_DIM:], odd[:, HEAD_DIM:]], axis=1)
        att_o[:, 128 * p : 128 * (p + 1)] = jnp.concatenate([top, low], axis=0)
    for out in outs + gw_copies:
        out.wait()


def front(n_crop, n_head, tokens, mixw, prow, crop, small, wqkv, cot, w2):
    rows, width = tokens.shape
    group, local = rows * n_head, HEADS // n_head
    dma = pltpu.SemaphoreType.DMA
    vmem = pl.BlockSpec(memory_space=pltpu.VMEM)
    hbm = pl.BlockSpec(memory_space=pl.ANY)
    block = rows + rows // 2
    shape = jax.ShapeDtypeStruct
    return pl.pallas_call(
        functools.partial(front_kernel, n_crop, n_head),
        out_shape=(
            shape((rows, width), F32),
            shape((rows, width), BF16),
            shape((local, n_head, block, 128), BF16),
            shape((rows, width), BF16),
            shape((local, n_head, rows // 2, 128), BF16),
            shape((8, group), F32),
            shape((w2.shape[0] // FC_TILE, rows, FC_TILE), F32),
            shape((width, rows), BF16),
            shape((8, width), F32),
        ),
        in_specs=[vmem, vmem, vmem, pl.BlockSpec(memory_space=pltpu.SMEM), vmem, vmem, vmem, vmem, vmem, vmem, hbm],
        out_specs=(hbm, hbm, hbm, vmem, hbm, vmem, hbm, hbm, vmem),
        scratch_shapes=[
            pltpu.VMEM((rows, width), BF16),
            pltpu.VMEM((rows, width), F32),
            pltpu.VMEM((rows, width), BF16),
            pltpu.VMEM((HEADS, block, 128), BF16),
            pltpu.VMEM((local, n_head, block, 128), BF16),
            pltpu.VMEM((group, HEAD_DIM), BF16),
            pltpu.VMEM((group, HEAD_DIM), BF16),
            pltpu.VMEM((group, HEAD_DIM), BF16),
            pltpu.VMEM((group, HEAD_DIM), BF16),
            pltpu.VMEM((HEAD_DIM, group), BF16),
            pltpu.VMEM((HEAD_DIM, group), BF16),
            pltpu.VMEM((HEAD_DIM, group), F32),
            pltpu.VMEM((2, group, rows), F32),
            pltpu.VMEM((2, group, rows), BF16),
            pltpu.VMEM((8, rows), F32),
            pltpu.VMEM((local, n_head, rows // 2, 128), BF16),
            pltpu.VMEM((HEADS, rows // 2, 128), BF16),
            pltpu.VMEM((w2.shape[0] // FC_TILE, FC_TILE, width), BF16),
            pltpu.VMEM((w2.shape[0] // FC_TILE, rows, FC_TILE), F32),
            pltpu.VMEM((width, rows), BF16),
            dma((2,)),
            dma((local, n_head - 1)),
            dma((local, n_head - 1)),
            dma((local, n_head - 1)),
            dma((local, n_head - 1)),
            dma((local,)),
            dma((4,)),
            dma((4,)),
            dma((5,)),
        ],
        compiler_params=pltpu.CompilerParams(collective_id=1, has_side_effects=True, vmem_limit_bytes=60 * MiB),
        cost_estimate=pl.CostEstimate(flops=10**10, bytes_accessed=2 * 10**7, transcendentals=10**7),
        name="front",
    )(tokens, mixw, prow, crop, *small, wqkv, cot, w2)


GELU_POLY = (0.254829592, -0.284496736, 1.421413741, -1.453152027, 1.061405429)
PIECE = 384


def gelu_and_slope(pre):
    bell = jnp.exp(-0.5 * pre * pre)
    t = 1.0 / (1.0 + (0.3275911 * 0.7071067811865476) * jnp.abs(pre))
    poly = GELU_POLY[4]
    for coefficient in GELU_POLY[3::-1]:
        poly = poly * t + coefficient
    tail = 0.5 * poly * t * bell
    phi = jnp.where(pre >= 0.0, 1.0 - tail, tail)
    return pre * phi, phi + pre * bell * 0.3989422804014327


def put_blocks(ref, lead, value):
    if len(ref.shape) == len(lead) + 5:
        rows = value.shape[0] // 8
        for c in range(8):
            ref[(*lead, c % 2, c // 2 % 2, c // 4)] = value[c * rows : (c + 1) * rows].astype(BF16)
    else:
        ref[lead] = value.astype(BF16)


def middle_kernel(
    cut,
    att, mixed, cot, cott, gsum, bout_r, gain_r, bias_r, bfc2_r, bfc1_r, wout_h, w1_h, w2_h, gw_h,
    layer_o, attg_o, mg_o, jfc_o, gout_o, sm_o,
    wout, w1, w2, mid_s, n2_s, n2t_s, out_s, dn_s, pre_s, gw_s, act_s, pg_s, proj_s, jfc,
    w_sem, j_sem,
):
    rows, width = cot.shape
    tiles = w1_h.shape[1] // FC_TILE
    wout_copy = pltpu.make_async_copy(wout_h, wout, w_sem.at[0, 0])
    wout_copy.start()
    w_copies = []
    for t in range(tiles):
        at = slice(t * FC_TILE, (t + 1) * FC_TILE)
        pair = (
            pltpu.make_async_copy(w1_h.at[:, at], w1.at[t], w_sem.at[1, t]),
            pltpu.make_async_copy(gw_h.at[t], gw_s.at[t], w_sem.at[3, t]),
            pltpu.make_async_copy(w2_h.at[at], w2.at[t], w_sem.at[2, t]),
        )
        for copy in pair:
            copy.start()
        w_copies.append(pair)
    sm_o[...] = jnp.zeros_like(sm_o)
    bout, gain, bias, bfc2, bfc1 = [as_line(r).astype(F32) for r in (bout_r, gain_r, bias_r, bfc2_r, bfc1_r)]
    wout_copy.wait()
    step = 128
    mid_s[...] = mixed[...] + dot(att[...], wout[...]) + bout

    def norm2(part):
        mid = mid_s[part]
        mean = jnp.mean(mid, axis=1, keepdims=True)
        centered = mid - mean
        rstd = lax.rsqrt(jnp.mean(centered * centered, axis=1, keepdims=True) + EPS)
        return mid, centered * rstd, rstd

    for r in range(0, rows, step):
        part = slice(r, r + step)
        mid, unit, _ = norm2(part)
        n2_s[part] = (unit * gain + bias).astype(BF16)
        out_s[part] = mid + bfc2
        dn_s[part] = jnp.zeros((step, width), F32)
    sm_o[7:8, :] = gsum[0:1, :]
    n2t_s[...] = jnp.transpose(n2_s[...])

    def first_products(t):
        for copy in w_copies[t]:
            copy.wait()
        pre_s[t % 2] = dot(n2_s[...], w1[t]) + bfc1[:, t * FC_TILE : (t + 1) * FC_TILE]

    j_copies = []
    first_products(0)
    for t in range(tiles):
        now, core, x = t % 2, t % 2, t // 2
        if t + 1 < tiles:
            first_products(t + 1)
        sums = jnp.zeros((1, FC_TILE), F32)
        for r in range(0, rows, 32):
            part = slice(r, r + 32)
            act, slope = gelu_and_slope(pre_s[now, part])
            act_s[now, part] = act.astype(BF16)
            pg = (gw_s[t, part] * slope).astype(BF16)
            pg_s[now, part] = pg
            sums = sums + jnp.sum(pg.astype(F32), axis=0, keepdims=True)
        sm_o[8 + t : 9 + t, :] = sums
        out_s[...] += dot(act_s[now], w2[t])
        dn_s[...] += dot_nt(pg_s[now], w1[t])
        g1 = dot(n2t_s[...], pg_s[now])
        for half in range(2):
            put_blocks(jfc, (half, core, x), g1[:, PIECE * half : PIECE * (half + 1)])
        g2 = dot(cott[...], act_s[now])
        places = [(0, core, x), (1, core, x)]
        if cut:
            for b in range(8):
                for s in range(2):
                    piece = g2[96 * b : 96 * (b + 1), PIECE * s : PIECE * (s + 1)].astype(BF16)
                    jfc[2 + b % 2, b // 2 % 2, b // 4, s, core, x] = piece
            places.append((slice(2, 4), slice(0, 2), slice(0, 2), slice(0, 2), core, x))
        else:
            for half in range(2):
                jfc[2 + half, core, x] = g2[:, PIECE * half : PIECE * (half + 1)].astype(BF16)
            places += [(2, core, x), (3, core, x)]
        for n, place in enumerate(places):
            j_copies.append(pltpu.make_async_copy(jfc.at[place], jfc_o.at[place], j_sem.at[t, n]))
            j_copies[-1].start()

    sums = [jnp.zeros((1, width), F32)] * 3
    for r in range(0, rows, step):
        part = slice(r, r + step)
        layer_o[part] = out_s[part].astype(BF16)
        _, unit, rstd = norm2(part)
        dn = dn_s[part]
        e = dn * gain
        inner = e - jnp.mean(e, axis=1, keepdims=True) - unit * jnp.mean(e * unit, axis=1, keepdims=True)
        mg = cot[part].astype(F32) + rstd * inner
        mg_o[part] = mg
        proj = mg.astype(BF16)
        proj_s[part] = proj
        for k, term in enumerate((proj.astype(F32), dn * unit, dn)):
            sums[k] = sums[k] + jnp.sum(term, axis=0, keepdims=True)
    for k in range(3):
        sm_o[4 + k : 5 + k, :] = sums[k]
    attg = dot_nt(proj_s[...], wout[...])
    for i in range(HEADS):
        attg_o[i] = halves_to_lanes(attg[:, HEAD_DIM * i : HEAD_DIM * (i + 1)]).astype(BF16)
    gout = dot_tn(att[...], proj_s[...])
    for k in range(2):
        put_blocks(gout_o, (k,), gout[:, PIECE * k : PIECE * (k + 1)])
    for copy in j_copies:
        copy.wait()


def middle(cut, att, mixed, cot, cott, gsum, small, wout, w1, w2, gw):
    rows, width = cot.shape
    vmem = pl.BlockSpec(memory_space=pltpu.VMEM)
    hbm = pl.BlockSpec(memory_space=pl.ANY)
    dma = pltpu.SemaphoreType.DMA
    shape = jax.ShapeDtypeStruct
    ff = w1.shape[1]
    jfc_dims = (4, 2, 2, 2, 2, 2, 96, PIECE) if cut else (4, 2, 2, width, PIECE)
    gout_dims = (2, 2, 2, 2, 96, PIECE) if cut else (2, width, PIECE)
    full = lambda kind: pltpu.VMEM((rows, width), kind)
    tile = lambda kind: pltpu.VMEM((2, rows, FC_TILE), kind)
    return pl.pallas_call(
        functools.partial(middle_kernel, cut),
        out_shape=(
            shape((rows, width), BF16),
            shape((HEADS, rows // 2, 128), BF16),
            shape((rows, width), F32),
            shape(jfc_dims, BF16),
            shape(gout_dims, BF16),
            shape((16, width), F32),
        ),
        in_specs=[vmem] * 10 + [hbm] * 4,
        out_specs=(vmem, vmem, vmem, hbm, vmem, vmem),
        scratch_shapes=[
            pltpu.VMEM((width, width), BF16),
            pltpu.VMEM((ff // FC_TILE, width, FC_TILE), BF16),
            pltpu.VMEM((ff // FC_TILE, FC_TILE, width), BF16),
            full(F32), full(BF16),
            pltpu.VMEM((width, rows), BF16),
            full(F32), full(F32), tile(F32), pltpu.VMEM(gw.shape, F32), tile(BF16), tile(BF16), full(BF16),
            pltpu.VMEM(jfc_dims, BF16),
            dma((4, 4)), dma((4, 4)),
        ],
        compiler_params=pltpu.CompilerParams(vmem_limit_bytes=60 * MiB),
        cost_estimate=pl.CostEstimate(flops=2 * 8 * 10**9, bytes_accessed=3 * 10**7, transcendentals=4 * 10**6),
        name="middle",
    )(att, mixed, cot, cott, gsum, *small, wout, w1, w2, gw)


class Reduction:
    AXES = ("x", "y", "lo", "hi")

    def __init__(self, acc, received, fin, send_sem, recv_sem, bits, peers, others, order):
        self.acc, self.received, self.fin = acc, received, fin
        self.send_sem, self.recv_sem = send_sem, recv_sem
        self.bits, self.peers, self.others, self.order = bits, peers, others, order

    def remote(self, k, src, dst, axis, peer=None):
        return pltpu.make_async_remote_copy(
            src_ref=src, dst_ref=dst, send_sem=self.send_sem.at[k], recv_sem=self.recv_sem.at[k],
            device_id=peer or self.peers[axis], device_id_type=MESH,
        )

    def add(self, into, received, lead, free):
        for place in itertools.product((0, 1), repeat=len(free)):
            index = list(lead)
            for axis, p in zip(free, place):
                index[self.AXES.index(axis)] = p
            index = tuple(index)
            into[index] = into[index] + received[place]

    def steps(self, source, core_half):
        copy = self.remote(0, source, self.received[0], "core")
        copy.start()
        if core_half is not None:
            core_half.start()
        yield
        copy.wait()
        if core_half is not None:
            core_half.wait()
        self.add(self.acc, self.received[0], [None] * 4, list(self.AXES))
        lead = [slice(None)] * 4
        free = list(self.AXES)
        for k, axis in enumerate(self.order):
            at = self.AXES.index(axis)
            lead[at] = 1 - self.bits[axis]
            copy = self.remote(1 + k, self.acc.at[tuple(lead)], self.received[1 + k], axis)
            copy.start()
            lead[at] = self.bits[axis]
            free.remove(axis)
            yield
            copy.wait()
            self.add(self.acc, self.received[1 + k], lead, free)
        bc, bx = self.bits["core"], self.bits["x"]
        mine = pltpu.make_async_copy(self.acc.at[tuple(lead)], self.fin.at[bc, bx], self.send_sem.at[8])
        mine.start()
        mine.wait()
        copies = [
            self.remote(5 + n, self.fin.at[bc, bx], self.fin.at[bc, bx], None, other) for n, other in enumerate(self.others)
        ]
        for copy in copies:
            copy.start()
        yield
        for copy in copies:
            copy.wait()


def tick(*jobs):
    for job in jobs:
        next(job, None)


def back_kernel(
    n_crop, n_head, cut,
    attg, grp_h, own, lse, jfc_h, gout, wqkv_h, normed_h, mixed_h, mg_h, mixw_r, prow_r, crop, gain_r, sm_in,
    *rest,
):
    (
        grad_o, fin_o, sm_o,
        grp, wqkv, normt, mixed, mg_s, dor, k_s, v_s, kt_s, qt_s, dot_s, dqt_s, s_s, dp_s, pds_s, dzq_s, dkv_s, dq_s, di_s, msg, ret, dn_s, sent_s, back_s,
        ja, jb, load_sem, do_send, do_recv, dq_send, dq_recv, own_sem, far_sem,
        *reduce_refs,
    ) = rest
    rows, width = mixed.shape
    group = rows * n_head
    local = HEADS // n_head
    c, h = lax.axis_index("crop"), lax.axis_index("head")
    far = lax.rem(c + n_crop // 2, n_crop)
    others = [lax.rem(h + o, n_head) for o in range(1, n_head)]
    peers = [(far, h)] + [(c, other) for other in others]
    if cut:
        bits = {"core": lax.rem(h, 2), "x": lax.div(h, 2), "y": lax.rem(c, 2), "lo": lax.rem(lax.div(c, 2), 2), "hi": lax.div(c, 4)}
        near = {
            "core": (c, h + 1 - 2 * bits["core"]),
            "x": (c, h + 2 - 4 * bits["x"]),
            "y": (c + 1 - 2 * bits["y"], h),
            "lo": (c + 2 - 4 * bits["lo"], h),
            "hi": (far, h),
        }
        peers += [near["y"], near["lo"]]
    greet(peers)

    def spread(j, source, target, send_sem, recv_sem):
        copies = [pltpu.make_async_copy(source(h), target(h), own_sem.at[j])]
        for o, other in enumerate(others):
            copies.append(
                pltpu.make_async_remote_copy(
                    src_ref=source(other), dst_ref=target(h), send_sem=send_sem.at[j, o], recv_sem=recv_sem.at[j, o],
                    device_id=(c, other), device_id_type=MESH,
                )
            )
        return copies

    def start(copies):
        for copy in copies:
            copy.start()

    do_copies = [
        spread(j, lambda d, j=j: attg.at[d * local + j], lambda s, j=j: dor.at[j, s], do_send, do_recv) for j in range(local)
    ]
    start(do_copies[0])
    loads = [
        pltpu.make_async_copy(a, b, load_sem.at[k])
        for k, (a, b) in enumerate([(grp_h, grp), (normed_h, sent_s), (wqkv_h, wqkv), (mixed_h, mixed), (mg_h, mg_s)])
    ]
    loads += [pltpu.make_async_copy(gout.at[k], ja.at[k, 0], load_sem.at[5 + k]) for k in range(2)]
    for load in loads:
        load.start()
    jobs, plan = [], {}
    if cut:
        send_sem, recv_sem, half_sem, sm_send, sm_recv, sm_r, acc_s, *received = reduce_refs
        orders = [
            ("y", "hi", "lo", "x"), ("lo", "y", "hi", "x"), ("y", "lo", "hi", "x"), ("lo", "y", "hi", "x"),
            ("lo", "x", "y", "hi"), ("y", "x", "lo", "hi"),
        ]
        for k in range(6):
            acc = acc_s.at[k] if k < 4 else (ja, jb)[k - 4].at[bits["core"]]
            red = Reduction(acc, [r.at[k] for r in received], fin_o.at[k], send_sem.at[k], recv_sem.at[k], bits, near, peers[1:n_head], orders[k])
            if k < 4:
                keep = pltpu.make_async_copy(jfc_h.at[k, bits["core"]], acc, half_sem.at[k])
                jobs.append(red.steps(jfc_h.at[k, 1 - bits["core"]], keep))
            else:
                jobs.append(red.steps((ja, jb)[k - 4].at[1 - bits["core"]], None))
        fc1, fc2, fc3, fc4, joba, jobb = jobs
        plan = {
            (0, "first"): (fc1, fc2),
            (0, 2): (fc1, fc2, fc3, fc4),
            (1, 2): (fc1, fc2, fc3, fc4),
            (1, "end"): (joba,),
            (2, 2): (fc1, fc2, fc4),
            (2, 5): (fc3, joba, fc1),
            (2, "end"): (fc2, fc4),
            "last": (jobb, fc3, fc1, fc4, fc2),
        }

    bound = crop[0, 0]
    first_case = bound < group // 2
    quarter = rows // 4
    short, long0 = 3 * quarter, 4 * quarter
    in_col = either_in_long(first_case, bound, (quarter, 1), 0, group) > 0.5
    in_row = either_in_long(first_case, bound, (1, quarter), 1, group) > 0.5
    col_long, col_short = jnp.where(in_col, 0.0, NEG), jnp.where(in_col, NEG, 0.0)
    row_long, row_short = jnp.where(in_row, 0.0, NEG), jnp.where(in_row, NEG, 0.0)
    lane = lax.broadcasted_iota(jnp.int32, (8, 128), 1) // HEAD_DIM
    ones = (lane == lax.broadcasted_iota(jnp.int32, (8, 128), 0)).astype(F32).astype(BF16)
    sums_q, sums_v = [None] * HEADS, [None] * HEADS
    dq_copies = []

    def head_grads(j):
        for copy in dq_copies[j]:
            copy.wait()
        total = dn_s[...] if j else 0.0
        for pair in range(n_head // 2):
            packs = []
            for d in (2 * pair, 2 * pair + 1):
                i = d * local + j
                vk = ret[i, 0:rows]
                dq = lanes_to_halves(ret[i, rows : rows + rows // 2])
                dk, dv = vk[:, HEAD_DIM:], vk[:, :HEAD_DIM]
                sums_q[i] = jnp.sum(dq.astype(F32), axis=0, keepdims=True)
                sums_v[i] = jnp.sum(dv.astype(F32), axis=0, keepdims=True)
                odd = i % 2
                base = 3 * HEAD_DIM * i - HEAD_DIM * odd
                none = jnp.zeros_like(dq)
                wide = jnp.concatenate([none, dq, dk, dv] if odd else [dq, dk, dv, none], axis=1)
                total = total + dot_nt(wide, wqkv[:, base : base + 4 * HEAD_DIM])
                packs += [dq, dk, dv]
            grad = dot(normt[...], jnp.concatenate(packs, axis=1))
            if j == 0:
                put_blocks(ja, (pair, 1), grad)
            else:
                put_blocks(jb, (pair, j - 1), grad)
        dn_s[...] = total

    for j in range(local):
        for copy in do_copies[j]:
            copy.wait()
        if j + 1 < local:
            start(do_copies[j + 1])
        if j == 0:
            loads[0].wait()
            tick(*plan.get((0, "first"), ()))
        rowd = []
        for s in range(n_head):
            prod = dor[j, s].astype(F32) * own[j, s].astype(F32)
            hi = prod.astype(BF16)
            d8 = dot_nt(ones, hi) + dot_nt(ones, (prod - hi.astype(F32)).astype(BF16))
            rowd.append(jnp.concatenate([d8[0:1], d8[1:2]], axis=1))
        end = lax.select(first_case, rowd[0], rowd[3])
        full = lax.select(first_case, rowd[3], rowd[0])
        ends = [end[:, quarter * k : quarter * (k + 1)] for k in range(4)]
        first, last = lax.select(first_case, ends[0], ends[3]), lax.select(first_case, ends[3], ends[0])
        di_s[0:1, :] = jnp.concatenate([first, ends[1], ends[2], last, full, rowd[1], rowd[2]], axis=1)
        qk = sorted_blocks(first_case, [grp[j, s, 0:rows] for s in range(n_head)])
        vv = sorted_blocks(first_case, [lanes_to_halves(grp[j, s, rows : rows + rows // 2]) for s in range(n_head)])
        dd = sorted_blocks(first_case, [lanes_to_halves(dor[j, s]) for s in range(n_head)])
        at = 0
        for a, b, d in zip(qk, vv, dd):
            n = a.shape[0]
            q = a[:, :HEAD_DIM] * BF16(HEAD_DIM**-0.5)
            k_s[at : at + n] = a[:, HEAD_DIM:]
            v_s[at : at + n] = b
            qt_s[:, at : at + n] = jnp.transpose(q)
            dot_s[:, at : at + n] = jnp.transpose(d)
            block, inner = at // rows, at % rows
            dzq_s[block, inner : inner + n] = jnp.concatenate([d, jnp.zeros_like(d)], axis=1)
            dzq_s[block, rows + inner : rows + inner + n] = jnp.concatenate([jnp.zeros_like(q), q], axis=1)
            at += n
        kt_s[...] = jnp.transpose(k_s[...])
        dqt_s[...] = jnp.zeros_like(dqt_s)
        dkv_s[...] = jnp.zeros_like(dkv_s)

        def area(q0, count, k0, k1, masks):
            lanes, number = slice(q0, q0 + count), k1 - k0
            s_s[:number, :count] = dot(k_s[k0:k1], qt_s[:, lanes])
            dp_s[:number, :count] = dot(v_s[k0:k1], dot_s[:, lanes])
            for k, mask in masks.items():
                if k0 <= k < k1:
                    s_s[k - k0 : k - k0 + quarter, :count] += mask
            for at in range(0, count, LANES):
                wide = min(LANES, count - at)
                here, place = slice(at, at + wide), slice(q0 + at, q0 + at + wide)
                lse_row, di_row = lse[j : j + 1, place], di_s[0:1, place]
                for k in range(0, number, KEYS):
                    keys = slice(k, k + KEYS)
                    p = jnp.exp(s_s[keys, here] - lse_row)
                    ds = p * (dp_s[keys, here] - di_row)
                    pds_s[keys, here] = p.astype(BF16)
                    pds_s[keys, rows + at : rows + at + wide] = ds.astype(BF16)
            block, inner = q0 // rows, q0 % rows
            if count == rows:
                add = dot(pds_s[:number], dzq_s[block])
            else:
                add = dot(pds_s[:number, :count], dzq_s[block, inner : inner + count])
                add = add + dot(pds_s[:number, rows : rows + count], dzq_s[block, rows + inner : rows + inner + count])
            dkv_s[k0:k1] += add
            dqt_s[:, lanes] += dot(kt_s[:, k0:k1], pds_s[:number, rows : rows + count])

        area(0, short, 0, long0, {short: col_short})
        either = {k: row_short for k in range(0, short, quarter)}
        either[short] = jnp.where(in_row, col_long, col_short)
        either.update({k: row_long for k in range(long0, group, quarter)})
        for k in range(0, group, rows):
            area(short, quarter, k, k + rows, either)
        tick(*plan.get((j, "near"), ()))
        half_keys = (group - short) // 2
        for t in range(n_head - 1):
            for half in range(2):
                k = short + half * half_keys
                area(long0 + t * rows, rows, k, k + half_keys, {short: col_long})
                tick(*plan.get((j, 2 * t + half), ()))
        dq_s[...] = jnp.transpose(dqt_s[...] * HEAD_DIM**-0.5).astype(BF16)

        dkv = unsorted_blocks(first_case, dkv_s[...])
        dqu = unsorted_blocks(first_case, dq_s[...])
        for s in range(n_head):
            msg[j, s, 0:rows] = dkv[s].astype(BF16)
            msg[j, s, rows : rows + rows // 2] = halves_to_lanes(dqu[s])
        dq_copies.append(spread(j, lambda d, j=j: msg.at[j, d], lambda s, j=j: ret.at[s * local + j], dq_send, dq_recv))
        start(dq_copies[j])
        if j == 0:
            for load in loads[1:]:
                load.wait()
            normt[...] = jnp.transpose(sent_s[...])
        else:
            head_grads(j - 1)
        tick(*plan.get((j, "end"), ()))

    head_grads(local - 1)
    tick(*plan.get("last", ()))
    share = as_column(as_line(mixw_r))
    gain = as_line(gain_r).astype(F32)
    sums = [jnp.zeros((1, width), F32)] * 2
    scaled = []
    step = 128
    for r in range(0, rows, step):
        part = slice(r, r + step)
        mix = mixed[part]
        mean = jnp.mean(mix, axis=1, keepdims=True)
        centered = mix - mean
        rstd = lax.rsqrt(jnp.mean(centered * centered, axis=1, keepdims=True) + EPS)
        unit = centered * rstd
        dn = dn_s[part]
        e = dn * gain
        inner = e - jnp.mean(e, axis=1, keepdims=True) - unit * jnp.mean(e * unit, axis=1, keepdims=True)
        grad = mg_s[part] + rstd * inner
        sums[0] = sums[0] + jnp.sum(dn * unit, axis=0, keepdims=True)
        sums[1] = sums[1] + jnp.sum(dn, axis=0, keepdims=True)
        mixed[part] = share[part] * grad
        dn_s[part] = (1.0 - share[part]) * grad
    chosen = lax.broadcasted_iota(jnp.int32, (rows, rows), 0) == as_line(prow_r)
    chosen = chosen.astype(F32).astype(BF16)
    given = dn_s[...]
    high = given.astype(BF16)
    low = (given - high.astype(F32)).astype(BF16)
    sent_s[...] = (dot(chosen, high) + dot(chosen, low)).astype(BF16)
    far_copy = pltpu.make_async_remote_copy(
        src_ref=sent_s, dst_ref=back_s, send_sem=far_sem.at[0], recv_sem=far_sem.at[1], device_id=(far, h), device_id_type=MESH
    )
    far_copy.start()
    sm_o[...] = sm_in[...]
    sm_o[0:1, :] = sums[0]
    sm_o[1:2, :] = sums[1]
    sm_o[2:3, :] = jnp.concatenate(sums_q, axis=1)
    sm_o[3:4, :] = jnp.concatenate(sums_v, axis=1)
    if cut:
        def small_sum():
            for k, axis in enumerate(("core", "x", "y", "lo", "hi")):
                copy = pltpu.make_async_remote_copy(
                    src_ref=sm_o, dst_ref=sm_r.at[k], send_sem=sm_send.at[k], recv_sem=sm_recv.at[k],
                    device_id=near[axis], device_id_type=MESH,
                )
                copy.start()
                yield
                copy.wait()
                sm_o[...] += sm_r[k]

        small = small_sum()
        tick(small, jobb, fc3, fc4, joba, fc1, fc2, small, fc3, fc4, joba, small, fc3, joba, jobb, small, jobb, small, jobb)
    else:
        fin_o[0] = ja[...]
        fin_o[1] = jb[...]
    far_copy.wait()
    for r in range(0, rows, step):
        part = slice(r, r + step)
        grad_o[part] = (mixed[part] + back_s[part].astype(F32)).astype(BF16)
    if cut:
        tick(small, joba, jobb, joba, jobb)


def back(n_crop, n_head, cut, attg, grp, own, lse, jfc, gout, wqkv, normed, mixed, mg, mixw, prow, crop, gain, sm):
    rows, width = mixed.shape
    group, local = rows * n_head, HEADS // n_head
    vmem = pl.BlockSpec(memory_space=pltpu.VMEM)
    hbm = pl.BlockSpec(memory_space=pl.ANY)
    smem = pl.BlockSpec(memory_space=pltpu.SMEM)
    dma = pltpu.SemaphoreType.DMA
    shape = jax.ShapeDtypeStruct
    block = rows + rows // 2
    jq_dims = (2, 2, 2, 2, 2, 96, PIECE) if cut else (2, 2, width, PIECE)
    finals = (6, 2, 2, 96, PIECE) if cut else (2, *jq_dims)
    square = lambda n, kind: pltpu.VMEM((group, n), kind)
    scratch = [
        pltpu.VMEM((local, n_head, block, 128), BF16),
        pltpu.VMEM(wqkv.shape, BF16),
        pltpu.VMEM((width, rows), BF16),
        pltpu.VMEM((rows, width), F32),
        pltpu.VMEM((rows, width), F32),
        pltpu.VMEM((local, n_head, rows // 2, 128), BF16),
        square(HEAD_DIM, BF16), square(HEAD_DIM, BF16),
        pltpu.VMEM((HEAD_DIM, group), BF16), pltpu.VMEM((HEAD_DIM, group), BF16), pltpu.VMEM((HEAD_DIM, group), BF16),
        pltpu.VMEM((HEAD_DIM, group), F32),
        pltpu.VMEM((832, rows), F32), pltpu.VMEM((832, rows), F32), pltpu.VMEM((832, 2 * rows), BF16),
        pltpu.VMEM((n_head, 2 * rows, 128), BF16), square(128, F32), square(HEAD_DIM, BF16),
        pltpu.VMEM((8, group), F32),
        pltpu.VMEM((local, n_head, block, 128), BF16),
        pltpu.VMEM((HEADS, block, 128), BF16),
        pltpu.VMEM((rows, width), F32),
        pltpu.VMEM((rows, width), BF16),
        pltpu.VMEM((rows, width), BF16),
        pltpu.VMEM(jq_dims, BF16),
        pltpu.VMEM(jq_dims, BF16),
        dma((7,)),
        dma((local, n_head - 1)), dma((local, n_head - 1)), dma((local, n_head - 1)), dma((local, n_head - 1)),
        dma((local,)),
        dma((2,)),
    ]
    if cut:
        scratch += [dma((6, 9)), dma((6, 9)), dma((4,)), dma((5,)), dma((5,)), pltpu.VMEM((5, 16, width), F32)]
        scratch.append(pltpu.VMEM((4, 2, 2, 2, 2, 96, PIECE), BF16))
        scratch += [pltpu.VMEM((6,) + (2,) * n + (96, PIECE), BF16) for n in (4, 3, 2, 1, 0)]
    return pl.pallas_call(
        functools.partial(back_kernel, n_crop, n_head, cut),
        out_shape=(shape((rows, width), BF16), shape(finals, BF16), shape((16, width), F32)),
        in_specs=[hbm, hbm, vmem, vmem, hbm, hbm, hbm, hbm, hbm, hbm, vmem, vmem, smem, vmem, vmem],
        out_specs=(vmem,) * 3,
        scratch_shapes=scratch,
        compiler_params=pltpu.CompilerParams(collective_id=2, has_side_effects=True, vmem_limit_bytes=60 * MiB),
        cost_estimate=pl.CostEstimate(flops=2 * 10**10, bytes_accessed=3 * 10**7, transcendentals=10**7),
        name="back",
    )(attg, grp, own, lse, jfc, gout, wqkv, normed, mixed, mg, mixw, prow, crop, gain, sm)


def finish_kernel(n_crop, n_head, grad, fin, sm, *outs):
    grad_o, g1_o, b1_o, gq_o, bq_o, bv_o, go_o, bo_o, g2_o, b2_o, gf1_o, bf1_o, gf2_o, bf2_o = outs
    c = lax.axis_index("crop")
    local = HEADS // n_head
    grad_o[...] = grad[...]
    parts = []
    for k in range(4):
        core, x = k % 2, k // 2
        for half in range(2):
            at = FC_TILE * k + PIECE * half
            gf1_o[:, at : at + PIECE] = fin[half, core, x].astype(F32)
        both = jnp.concatenate([fin[2, core, x], fin[3, core, x]], axis=0)
        parts.append(jnp.transpose(both.astype(F32)))
    gf2_o[...] = jnp.concatenate(parts, axis=1)
    for k in range(2):
        go_o[:, PIECE * k : PIECE * (k + 1)] = fin[4, k, 0].astype(F32)
    parts = []
    for i in range(HEADS):
        d, j = i // local, i % local
        piece = fin[4, d // 2, 1] if j == 0 else fin[5, d // 2, j - 1]
        parts.append(piece[:, 192 * (d % 2) : 192 * (d % 2 + 1)].astype(F32))
    gq_o[...] = jnp.concatenate(parts, axis=1)
    piece = jnp.zeros((16, 96), F32)
    wide = jnp.zeros((1, PIECE), F32)
    for k in range(n_crop):
        piece = lax.select(c == k, sm[:, 96 * k : 96 * (k + 1)], piece)
        wide = lax.select(c == k, sm[8 + k // 2 : 9 + k // 2, PIECE * (k % 2) : PIECE * (k % 2 + 1)], wide)
    for row, out in ((0, g1_o), (1, b1_o), (2, bq_o), (3, bv_o), (4, bo_o), (5, g2_o), (6, b2_o), (7, bf2_o)):
        out[...] = piece[row : row + 1].reshape(96)
    bf1_o[...] = wide.reshape(PIECE)


def finish(n_crop, n_head, grad, fin, sm):
    rows, width = grad.shape
    vmem = pl.BlockSpec(memory_space=pltpu.VMEM)
    shape = jax.ShapeDtypeStruct
    short = shape((96,), F32)
    outs = (
        shape((rows, width), BF16), short, short, shape((96, 3 * width), F32), short, short, shape((96, width), F32), short,
        short, short, shape((96, 4 * width), F32), shape((PIECE,), F32), shape((PIECE, width), F32), short,
    )
    return pl.pallas_call(
        functools.partial(finish_kernel, n_crop, n_head),
        out_shape=outs,
        in_specs=[vmem] * 3,
        out_specs=(vmem,) * len(outs),
        compiler_params=pltpu.CompilerParams(vmem_limit_bytes=60 * MiB),
        name="finish",
    )(grad, fin, sm)


def sum_everywhere(grads, small, n_crop, n_head):
    c = lax.axis_index("crop")

    def scatter(value):
        part = lax.psum_scatter(value.astype(F32), "crop", scatter_dimension=0, tiled=True)
        return lax.psum(part.astype(BF16), "head").astype(F32)

    jfc, ja, jb = grads
    width = jfc.shape[3]
    local = HEADS // n_head
    g1 = jnp.concatenate([jfc[half, t % 2, t // 2] for t in range(4) for half in range(2)], axis=1)
    g2 = jnp.concatenate([jfc[2 + half, t % 2, t // 2] for t in range(4) for half in range(2)], axis=1).T
    go = jnp.concatenate([ja[0, 0], ja[1, 0]], axis=1)
    parts = []
    for i in range(HEADS):
        d, j = i // local, i % local
        piece = ja[d // 2, 1] if j == 0 else jb[d // 2, j - 1]
        parts.append(piece[:, 192 * (d % 2) : 192 * (d % 2 + 1)])
    gq = jnp.concatenate(parts, axis=1)
    total = lax.psum(small, ("crop", "head"))

    def mine(vector):
        count = vector.shape[0] // n_crop
        return lax.dynamic_slice_in_dim(vector, c * count, count, 0)

    rows = [mine(total[k]) for k in range(8)]
    return [
        rows[0], rows[1], scatter(gq), rows[2], rows[3], scatter(go), rows[4], rows[5], rows[6],
        scatter(g1), mine(total[8:12].reshape(4 * width)), scatter(g2), rows[7],
    ]


def shards(
    tokens, mix_weight, partner_row, crop_lengths, ln1_gain, ln1_bias, w_qkv, b_query, b_value, w_out, b_out,
    ln2_gain, ln2_bias, w_fc1, b_fc1, w_fc2, b_fc2, cotangent,
):
    n_crop, n_head = lax.axis_size("crop"), lax.axis_size("head")
    cut = n_crop == 8 and n_head == 4
    small1, small2 = (ln1_gain, ln1_bias, b_query, b_value), (b_out, ln2_gain, ln2_bias, b_fc2, b_fc1)
    mixed, normed, grp, att, own, lse, gw, cott, gsum = front(
        n_crop, n_head, tokens, mix_weight, partner_row, crop_lengths, small1, w_qkv, cotangent, w_fc2
    )
    layer_out, attg, mg, jfc, gout, sm = middle(cut, att, mixed, cotangent, cott, gsum, small2, w_out, w_fc1, w_fc2, gw)
    grad, fin, sm = back(
        n_crop, n_head, cut, attg, grp, own, lse, jfc, gout, w_qkv, normed, mixed, mg, mix_weight, partner_row, crop_lengths, ln1_gain, sm
    )
    if not cut:
        return (layer_out, grad, *sum_everywhere((jfc, fin[0], fin[1]), sm, n_crop, n_head))
    outs = finish(n_crop, n_head, grad, fin, sm)
    return (layer_out, *outs)


def solution(mesh):
    rows, one = P(("crop", "head"), None), P(("crop", "head"))
    in_specs = (rows, one, one, P("crop", None)) + (P(),) * 13 + (rows,)
    vector, matrix = P("crop"), P("crop", None)
    out_specs = (
        rows, rows, vector, vector, matrix, vector, vector, matrix, vector, vector, vector, matrix, vector, matrix, vector,
    )
    return jax.shard_map(shards, mesh=mesh, in_specs=in_specs, out_specs=out_specs, check_vma=False)
```

```python
import functools
import itertools

import jax
import jax.numpy as jnp
from jax import lax
from jax.experimental import pallas as pl
from jax.experimental.pallas import tpu as pltpu
from jax.sharding import PartitionSpec as P

HEADS = 12
HEAD_DIM = 64
EPS = 1e-06
NEG = -1e30
KEYS = 64
LANES = 256
FC_TILE = 768
MESH = pl.DeviceIdType.MESH
F32 = jnp.float32
BF16 = jnp.bfloat16
MiB = 1 << 20


def dot(left, right):
    return jnp.dot(left, right, preferred_element_type=F32)


def dot_nt(left, right):
    return lax.dot_general(left, right, (((1,), (1,)), ((), ())), preferred_element_type=F32)


def dot_tn(left, right):
    return lax.dot_general(left, right, (((0,), (0,)), ((), ())), preferred_element_type=F32)


def as_line(ref):
    return ref[...].reshape(1, ref.shape[0])


def as_column(row):
    return jnp.transpose(jnp.broadcast_to(row, (8, row.shape[1])))[:, 0:1]


def as_row(column):
    return jnp.transpose(jnp.broadcast_to(column, (column.shape[0], 128)))[0:8]


def halves_to_lanes(block):
    half = block.shape[0] // 2
    return jnp.concatenate([block[:half], block[half:]], axis=1)


def lanes_to_halves(block):
    return jnp.concatenate([block[:, :HEAD_DIM], block[:, HEAD_DIM:]], axis=0)


def greet(peers):
    barrier = pltpu.get_barrier_semaphore()
    for peer in peers:
        pl.semaphore_signal(barrier, inc=1, device_id=peer, device_id_type=MESH)
    pl.semaphore_wait(barrier, len(peers))


def sorted_blocks(first_case, parts):
    end = lax.select(first_case, parts[0], parts[3])
    full = lax.select(first_case, parts[3], parts[0])
    q = end.shape[0] // 4
    near = lax.select(first_case, end[:q], end[3 * q :])
    either = lax.select(first_case, end[3 * q :], end[:q])
    return [near, end[q : 3 * q], either, full, parts[1], parts[2]]


def unsorted_blocks(first_case, block):
    n = block.shape[0] // 4
    q = n // 4
    low, mid, top = block[:q], block[q : 3 * q], block[3 * q : n]
    head = lax.select(first_case, low, top)
    tail = lax.select(first_case, top, low)
    end = jnp.concatenate([head, mid, tail], axis=0)
    full = block[n : 2 * n]
    return [
        lax.select(first_case, end, full),
        block[2 * n : 3 * n],
        block[3 * n :],
        lax.select(first_case, full, end),
    ]


def either_in_long(first_case, bound, shape, axis, group):
    place = lax.broadcasted_iota(jnp.int32, shape, axis)
    row = place + jnp.where(first_case, group // 4 - 128, group - group // 4)
    past = row >= bound
    return jnp.where(first_case, past.astype(F32), 1.0 - past.astype(F32))


def front_kernel(
    n_crop,
    n_head,
    tokens, mixw_r, prow_r, crop, gain_r, bias_r, bq_r, bv_r, wqkv, cot, w2_h,
    mixed_o, normed_o, grp_o, att_o, own_o, lse_o, gw_o, cott_o, gsum_o,
    prt, mixed_s, normed_s, msg, grp, q_s, k_s, v_s, o_s, qt_s, vt_s, ot_s, s_s, p_s, tot_s, own_s, att_r, w2, gw_s, cott_s,
    prt_sem, qkv_send, qkv_recv, att_send, att_recv, own_sem, out_sem, w2_sem, gw_sem,
):
    rows, width = tokens.shape
    group = rows * n_head
    local = HEADS // n_head
    c, h = lax.axis_index("crop"), lax.axis_index("head")
    far = lax.rem(c + n_crop // 2, n_crop)
    others = [lax.rem(h + o, n_head) for o in range(1, n_head)]
    greet([(far, h)] + [(c, other) for other in others])

    partner_copy = pltpu.make_async_remote_copy(
        src_ref=tokens, dst_ref=prt, send_sem=prt_sem.at[0], recv_sem=prt_sem.at[1], device_id=(far, h), device_id_type=MESH
    )
    partner_copy.start()
    mixw, prow = as_line(mixw_r), as_line(prow_r)
    gain, bias, query_bias, value_bias = [as_line(r).astype(F32) for r in (gain_r, bias_r, bq_r, bv_r)]
    share = as_column(mixw)
    chosen = lax.broadcasted_iota(jnp.int32, (rows, rows), 0) == prow
    chosen = chosen.astype(F32).astype(BF16)
    tiles = w2.shape[0]
    w2_copies = [
        pltpu.make_async_copy(w2_h.at[t * w2.shape[1] : (t + 1) * w2.shape[1]], w2.at[t], w2_sem.at[t]) for t in range(tiles)
    ]
    for copy in w2_copies:
        copy.start()
    gsum_o[...] = jnp.broadcast_to(jnp.sum(cot[...].astype(F32), axis=0, keepdims=True), gsum_o.shape)
    cott_s[...] = jnp.transpose(cot[...])
    gw_copies = [pltpu.make_async_copy(cott_s, cott_o, gw_sem.at[tiles])]
    gw_copies[0].start()
    for t in range(tiles):
        w2_copies[t].wait()
        gw_s[t] = dot_nt(cot[...], w2[t])
        gw_copies.append(pltpu.make_async_copy(gw_s.at[t], gw_o.at[t], gw_sem.at[t]))
        gw_copies[-1].start()
    partner_copy.wait()
    step = 128
    for r in range(0, rows, step):
        part = slice(r, r + step)
        gathered = dot_tn(chosen[:, part], prt[...])
        mix = share[part] * tokens[part].astype(F32) + (1.0 - share[part]) * gathered
        mixed_s[part] = mix
        mean = jnp.mean(mix, axis=1, keepdims=True)
        centered = mix - mean
        variance = jnp.mean(centered * centered, axis=1, keepdims=True)
        normed = centered * lax.rsqrt(variance + EPS) * gain + bias
        normed_s[part] = normed.astype(BF16)
    outs = [
        pltpu.make_async_copy(mixed_s, mixed_o, out_sem.at[0]),
        pltpu.make_async_copy(normed_s, normed_o, out_sem.at[1]),
    ]
    for out in outs:
        out.start()

    qkv_copies = []
    for j in range(local):
        for d in range(n_head):
            i = d * local + j
            odd = i % 2
            base = 3 * HEAD_DIM * i - HEAD_DIM * odd
            res = dot(normed_s[...], wqkv[:, base : base + 4 * HEAD_DIM])
            res = res[:, HEAD_DIM * odd : HEAD_DIM * odd + 3 * HEAD_DIM]
            bq = query_bias[:, HEAD_DIM * i : HEAD_DIM * (i + 1)]
            bv = value_bias[:, HEAD_DIM * i : HEAD_DIM * (i + 1)]
            res = res + jnp.concatenate([bq, jnp.zeros_like(bq), bv], axis=1)
            msg[i, 0:rows] = res[:, : 2 * HEAD_DIM].astype(BF16)
            msg[i, rows : rows + rows // 2] = halves_to_lanes(res[:, 2 * HEAD_DIM :]).astype(BF16)
        batch = [pltpu.make_async_copy(msg.at[h * local + j], grp.at[j, h], own_sem.at[j])]
        for o, other in enumerate(others):
            batch.append(
                pltpu.make_async_remote_copy(
                    src_ref=msg.at[other * local + j],
                    dst_ref=grp.at[j, h],
                    send_sem=qkv_send.at[j, o],
                    recv_sem=qkv_recv.at[j, o],
                    device_id=(c, other),
                    device_id_type=MESH,
                )
            )
        for copy in batch:
            copy.start()
        qkv_copies.append(batch)

    bound = crop[0, 0]
    first_case = bound < group // 2
    quarter = rows // 4
    short, long0 = 3 * quarter, 4 * quarter
    in_col = either_in_long(first_case, bound, (quarter, 1), 0, group) > 0.5
    in_row = either_in_long(first_case, bound, (1, quarter), 1, group) > 0.5
    col_long, col_short = jnp.where(in_col, 0.0, NEG), jnp.where(in_col, NEG, 0.0)
    row_long, row_short = jnp.where(in_row, 0.0, NEG), jnp.where(in_row, NEG, 0.0)
    att_copies = []
    for j in range(local):
        for copy in qkv_copies[j]:
            copy.wait()
        qk = sorted_blocks(first_case, [grp[j, s, 0:rows] for s in range(n_head)])
        vv = sorted_blocks(first_case, [lanes_to_halves(grp[j, s, rows : rows + rows // 2]) for s in range(n_head)])
        at = 0
        for a, b in zip(qk, vv):
            n = a.shape[0]
            q_s[at : at + n] = a[:, :HEAD_DIM] * BF16(HEAD_DIM**-0.5)
            k_s[at : at + n] = a[:, HEAD_DIM:]
            v_s[at : at + n] = b
            at += n

        qt_s[...] = jnp.transpose(q_s[...])
        vt_s[...] = jnp.transpose(v_s[...])

        def area(slot, q0, count, k0, k1, masks):
            lanes, number = slice(q0, q0 + count), k1 - k0
            s_s[slot, :number, :count] = dot(k_s[k0:k1], qt_s[:, lanes])
            for k, mask in masks.items():
                s_s[slot, k - k0 : k - k0 + quarter, :count] += mask
            for at in range(0, count, LANES):
                wide = min(LANES, count - at)
                here = slice(at, at + wide)
                top = jnp.full((8, wide), NEG, F32)
                for k in range(0, number, KEYS):
                    top = jnp.maximum(top, jnp.max(s_s[slot, k : k + KEYS, here].reshape(KEYS // 8, 8, wide), axis=0))
                top = jnp.max(top, axis=0, keepdims=True)
                total = jnp.zeros((8, wide), F32)
                for k in range(0, number, KEYS):
                    p = jnp.exp(s_s[slot, k : k + KEYS, here] - top)
                    total = total + jnp.sum(p.reshape(KEYS // 8, 8, wide), axis=0)
                    p_s[slot, k : k + KEYS, here] = p.astype(BF16)
                total = jnp.sum(total, axis=0, keepdims=True)
                tot_s[slot : slot + 1, here] = 1.0 / total
                lse_o[j : j + 1, q0 + at : q0 + at + wide] = top + jnp.log(total)
            out = dot(vt_s[:, k0:k1], p_s[slot, :number, :count])
            ot_s[:, lanes] = out * tot_s[slot : slot + 1, :count]

        area(0, 0, short, 0, long0, {short: col_short})
        either = {k: row_short for k in range(0, short, quarter)}
        either[short] = jnp.where(in_row, col_long, col_short)
        either.update({k: row_long for k in range(long0, group, quarter)})
        area(1, short, quarter, 0, group, either)
        for t in range(n_head - 1):
            area(t % 2, long0 + t * rows, rows, short, group, {short: col_long})
        o_s[...] = jnp.transpose(ot_s[...]).astype(BF16)

        for s, block in enumerate(unsorted_blocks(first_case, o_s[...])):
            own_s[j, s] = halves_to_lanes(block)
        batch = [pltpu.make_async_copy(own_s.at[j, h], att_r.at[h * local + j], own_sem.at[j])]
        for o, other in enumerate(others):
            batch.append(
                pltpu.make_async_remote_copy(
                    src_ref=own_s.at[j, other],
                    dst_ref=att_r.at[h * local + j],
                    send_sem=att_send.at[j, o],
                    recv_sem=att_recv.at[j, o],
                    device_id=(c, other),
                    device_id_type=MESH,
                )
            )
        for copy in batch:
            copy.start()
        att_copies.append(batch)
    late = [pltpu.make_async_copy(grp, grp_o, out_sem.at[2]), pltpu.make_async_copy(own_s, own_o, out_sem.at[3])]
    for out in late:
        out.start()
    outs += late
    for batch in att_copies:
        for copy in batch:
            copy.wait()
    for p in range(HEADS // 2):
        even, odd = att_r[2 * p], att_r[2 * p + 1]
        top = jnp.concatenate([even[:, :HEAD_DIM], odd[:, :HEAD_DIM]], axis=1)
        low = jnp.concatenate([even[:, HEAD_DIM:], odd[:, HEAD_DIM:]], axis=1)
        att_o[:, 128 * p : 128 * (p + 1)] = jnp.concatenate([top, low], axis=0)
    for out in outs + gw_copies:
        out.wait()


def front(n_crop, n_head, tokens, mixw, prow, crop, small, wqkv, cot, w2):
    rows, width = tokens.shape
    group, local = rows * n_head, HEADS // n_head
    dma = pltpu.SemaphoreType.DMA
    vmem = pl.BlockSpec(memory_space=pltpu.VMEM)
    hbm = pl.BlockSpec(memory_space=pl.ANY)
    block = rows + rows // 2
    shape = jax.ShapeDtypeStruct
    return pl.pallas_call(
        functools.partial(front_kernel, n_crop, n_head),
        out_shape=(
            shape((rows, width), F32),
            shape((rows, width), BF16),
            shape((local, n_head, block, 128), BF16),
            shape((rows, width), BF16),
            shape((local, n_head, rows // 2, 128), BF16),
            shape((8, group), F32),
            shape((w2.shape[0] // FC_TILE, rows, FC_TILE), F32),
            shape((width, rows), BF16),
            shape((8, width), F32),
        ),
        in_specs=[vmem, vmem, vmem, pl.BlockSpec(memory_space=pltpu.SMEM), vmem, vmem, vmem, vmem, vmem, vmem, hbm],
        out_specs=(hbm, hbm, hbm, vmem, hbm, vmem, hbm, hbm, vmem),
        scratch_shapes=[
            pltpu.VMEM((rows, width), BF16),
            pltpu.VMEM((rows, width), F32),
            pltpu.VMEM((rows, width), BF16),
            pltpu.VMEM((HEADS, block, 128), BF16),
            pltpu.VMEM((local, n_head, block, 128), BF16),
            pltpu.VMEM((group, HEAD_DIM), BF16),
            pltpu.VMEM((group, HEAD_DIM), BF16),
            pltpu.VMEM((group, HEAD_DIM), BF16),
            pltpu.VMEM((group, HEAD_DIM), BF16),
            pltpu.VMEM((HEAD_DIM, group), BF16),
            pltpu.VMEM((HEAD_DIM, group), BF16),
            pltpu.VMEM((HEAD_DIM, group), F32),
            pltpu.VMEM((2, group, rows), F32),
            pltpu.VMEM((2, group, rows), BF16),
            pltpu.VMEM((8, rows), F32),
            pltpu.VMEM((local, n_head, rows // 2, 128), BF16),
            pltpu.VMEM((HEADS, rows // 2, 128), BF16),
            pltpu.VMEM((w2.shape[0] // FC_TILE, FC_TILE, width), BF16),
            pltpu.VMEM((w2.shape[0] // FC_TILE, rows, FC_TILE), F32),
            pltpu.VMEM((width, rows), BF16),
            dma((2,)),
            dma((local, n_head - 1)),
            dma((local, n_head - 1)),
            dma((local, n_head - 1)),
            dma((local, n_head - 1)),
            dma((local,)),
            dma((4,)),
            dma((4,)),
            dma((5,)),
        ],
        compiler_params=pltpu.CompilerParams(collective_id=1, has_side_effects=True, vmem_limit_bytes=60 * MiB),
        cost_estimate=pl.CostEstimate(flops=10**10, bytes_accessed=2 * 10**7, transcendentals=10**7),
        name="front",
    )(tokens, mixw, prow, crop, *small, wqkv, cot, w2)


GELU_POLY = (0.254829592, -0.284496736, 1.421413741, -1.453152027, 1.061405429)
PIECE = 384


def gelu_and_slope(pre):
    bell = jnp.exp(-0.5 * pre * pre)
    t = 1.0 / (1.0 + (0.3275911 * 0.7071067811865476) * jnp.abs(pre))
    poly = GELU_POLY[4]
    for coefficient in GELU_POLY[3::-1]:
        poly = poly * t + coefficient
    tail = 0.5 * poly * t * bell
    phi = jnp.where(pre >= 0.0, 1.0 - tail, tail)
    return pre * phi, phi + pre * bell * 0.3989422804014327


def put_blocks(ref, lead, value):
    if len(ref.shape) == len(lead) + 5:
        rows = value.shape[0] // 8
        for c in range(8):
            ref[(*lead, c % 2, c // 2 % 2, c // 4)] = value[c * rows : (c + 1) * rows].astype(BF16)
    else:
        ref[lead] = value.astype(BF16)


def middle_kernel(
    cut,
    att, mixed, cot, cott, gsum, bout_r, gain_r, bias_r, bfc2_r, bfc1_r, wout_h, w1_h, w2_h, gw_h,
    layer_o, attg_o, mg_o, jfc_o, gout_o, sm_o,
    wout, w1, w2, mid_s, n2_s, n2t_s, out_s, dn_s, pre_s, gw_s, act_s, pg_s, proj_s, jfc,
    w_sem, j_sem,
):
    rows, width = cot.shape
    tiles = w1_h.shape[1] // FC_TILE
    wout_copy = pltpu.make_async_copy(wout_h, wout, w_sem.at[0, 0])
    wout_copy.start()
    w_copies = []
    for t in range(tiles):
        at = slice(t * FC_TILE, (t + 1) * FC_TILE)
        pair = (
            pltpu.make_async_copy(w1_h.at[:, at], w1.at[t], w_sem.at[1, t]),
            pltpu.make_async_copy(gw_h.at[t], gw_s.at[t], w_sem.at[3, t]),
            pltpu.make_async_copy(w2_h.at[at], w2.at[t], w_sem.at[2, t]),
        )
        for copy in pair:
            copy.start()
        w_copies.append(pair)
    sm_o[...] = jnp.zeros_like(sm_o)
    bout, gain, bias, bfc2, bfc1 = [as_line(r).astype(F32) for r in (bout_r, gain_r, bias_r, bfc2_r, bfc1_r)]
    wout_copy.wait()
    step = 128
    mid_s[...] = mixed[...] + dot(att[...], wout[...]) + bout

    def norm2(part):
        mid = mid_s[part]
        mean = jnp.mean(mid, axis=1, keepdims=True)
        centered = mid - mean
        rstd = lax.rsqrt(jnp.mean(centered * centered, axis=1, keepdims=True) + EPS)
        return mid, centered * rstd, rstd

    for r in range(0, rows, step):
        part = slice(r, r + step)
        mid, unit, _ = norm2(part)
        n2_s[part] = (unit * gain + bias).astype(BF16)
        out_s[part] = mid + bfc2
        dn_s[part] = jnp.zeros((step, width), F32)
    sm_o[7:8, :] = gsum[0:1, :]
    n2t_s[...] = jnp.transpose(n2_s[...])

    def first_products(t):
        for copy in w_copies[t]:
            copy.wait()
        pre_s[t % 2] = dot(n2_s[...], w1[t]) + bfc1[:, t * FC_TILE : (t + 1) * FC_TILE]

    j_copies = []
    first_products(0)
    for t in range(tiles):
        now, core, x = t % 2, t % 2, t // 2
        if t + 1 < tiles:
            first_products(t + 1)
        sums = jnp.zeros((1, FC_TILE), F32)
        for r in range(0, rows, 32):
            part = slice(r, r + 32)
            act, slope = gelu_and_slope(pre_s[now, part])
            act_s[now, part] = act.astype(BF16)
            pg = (gw_s[t, part] * slope).astype(BF16)
            pg_s[now, part] = pg
            sums = sums + jnp.sum(pg.astype(F32), axis=0, keepdims=True)
        sm_o[8 + t : 9 + t, :] = sums
        out_s[...] += dot(act_s[now], w2[t])
        dn_s[...] += dot_nt(pg_s[now], w1[t])
        g1 = dot(n2t_s[...], pg_s[now])
        for half in range(2):
            put_blocks(jfc, (half, core, x), g1[:, PIECE * half : PIECE * (half + 1)])
        g2 = dot(cott[...], act_s[now])
        places = [(0, core, x), (1, core, x)]
        if cut:
            for b in range(8):
                for s in range(2):
                    piece = g2[96 * b : 96 * (b + 1), PIECE * s : PIECE * (s + 1)].astype(BF16)
                    jfc[2 + b % 2, b // 2 % 2, b // 4, s, core, x] = piece
            places.append((slice(2, 4), slice(0, 2), slice(0, 2), slice(0, 2), core, x))
        else:
            for half in range(2):
                jfc[2 + half, core, x] = g2[:, PIECE * half : PIECE * (half + 1)].astype(BF16)
            places += [(2, core, x), (3, core, x)]
        for n, place in enumerate(places):
            j_copies.append(pltpu.make_async_copy(jfc.at[place], jfc_o.at[place], j_sem.at[t, n]))
            j_copies[-1].start()

    sums = [jnp.zeros((1, width), F32)] * 3
    for r in range(0, rows, step):
        part = slice(r, r + step)
        layer_o[part] = out_s[part].astype(BF16)
        _, unit, rstd = norm2(part)
        dn = dn_s[part]
        e = dn * gain
        inner = e - jnp.mean(e, axis=1, keepdims=True) - unit * jnp.mean(e * unit, axis=1, keepdims=True)
        mg = cot[part].astype(F32) + rstd * inner
        mg_o[part] = mg
        proj = mg.astype(BF16)
        proj_s[part] = proj
        for k, term in enumerate((proj.astype(F32), dn * unit, dn)):
            sums[k] = sums[k] + jnp.sum(term, axis=0, keepdims=True)
    for k in range(3):
        sm_o[4 + k : 5 + k, :] = sums[k]
    attg = dot_nt(proj_s[...], wout[...])
    for i in range(HEADS):
        attg_o[i] = halves_to_lanes(attg[:, HEAD_DIM * i : HEAD_DIM * (i + 1)]).astype(BF16)
    gout = dot_tn(att[...], proj_s[...])
    for k in range(2):
        put_blocks(gout_o, (k,), gout[:, PIECE * k : PIECE * (k + 1)])
    for copy in j_copies:
        copy.wait()


def middle(cut, att, mixed, cot, cott, gsum, small, wout, w1, w2, gw):
    rows, width = cot.shape
    vmem = pl.BlockSpec(memory_space=pltpu.VMEM)
    hbm = pl.BlockSpec(memory_space=pl.ANY)
    dma = pltpu.SemaphoreType.DMA
    shape = jax.ShapeDtypeStruct
    ff = w1.shape[1]
    jfc_dims = (4, 2, 2, 2, 2, 2, 96, PIECE) if cut else (4, 2, 2, width, PIECE)
    gout_dims = (2, 2, 2, 2, 96, PIECE) if cut else (2, width, PIECE)
    full = lambda kind: pltpu.VMEM((rows, width), kind)
    tile = lambda kind: pltpu.VMEM((2, rows, FC_TILE), kind)
    return pl.pallas_call(
        functools.partial(middle_kernel, cut),
        out_shape=(
            shape((rows, width), BF16),
            shape((HEADS, rows // 2, 128), BF16),
            shape((rows, width), F32),
            shape(jfc_dims, BF16),
            shape(gout_dims, BF16),
            shape((16, width), F32),
        ),
        in_specs=[vmem] * 10 + [hbm] * 4,
        out_specs=(vmem, vmem, vmem, hbm, vmem, vmem),
        scratch_shapes=[
            pltpu.VMEM((width, width), BF16),
            pltpu.VMEM((ff // FC_TILE, width, FC_TILE), BF16),
            pltpu.VMEM((ff // FC_TILE, FC_TILE, width), BF16),
            full(F32), full(BF16),
            pltpu.VMEM((width, rows), BF16),
            full(F32), full(F32), tile(F32), pltpu.VMEM(gw.shape, F32), tile(BF16), tile(BF16), full(BF16),
            pltpu.VMEM(jfc_dims, BF16),
            dma((4, 4)), dma((4, 4)),
        ],
        compiler_params=pltpu.CompilerParams(vmem_limit_bytes=60 * MiB),
        cost_estimate=pl.CostEstimate(flops=2 * 8 * 10**9, bytes_accessed=3 * 10**7, transcendentals=4 * 10**6),
        name="middle",
    )(att, mixed, cot, cott, gsum, *small, wout, w1, w2, gw)


class Reduction:
    AXES = ("x", "y", "lo", "hi")

    def __init__(self, acc, received, fin, send_sem, recv_sem, bits, peers, others, order):
        self.acc, self.received, self.fin = acc, received, fin
        self.send_sem, self.recv_sem = send_sem, recv_sem
        self.bits, self.peers, self.others, self.order = bits, peers, others, order

    def remote(self, k, src, dst, axis, peer=None):
        return pltpu.make_async_remote_copy(
            src_ref=src, dst_ref=dst, send_sem=self.send_sem.at[k], recv_sem=self.recv_sem.at[k],
            device_id=peer or self.peers[axis], device_id_type=MESH,
        )

    def add(self, into, received, lead, free):
        for place in itertools.product((0, 1), repeat=len(free)):
            index = list(lead)
            for axis, p in zip(free, place):
                index[self.AXES.index(axis)] = p
            index = tuple(index)
            into[index] = into[index] + received[place]

    def steps(self, source, core_half):
        copy = self.remote(0, source, self.received[0], "core")
        copy.start()
        if core_half is not None:
            core_half.start()
        yield
        copy.wait()
        if core_half is not None:
            core_half.wait()
        self.add(self.acc, self.received[0], [None] * 4, list(self.AXES))
        lead = [slice(None)] * 4
        free = list(self.AXES)
        for k, axis in enumerate(self.order):
            at = self.AXES.index(axis)
            lead[at] = 1 - self.bits[axis]
            copy = self.remote(1 + k, self.acc.at[tuple(lead)], self.received[1 + k], axis)
            copy.start()
            lead[at] = self.bits[axis]
            free.remove(axis)
            yield
            copy.wait()
            self.add(self.acc, self.received[1 + k], lead, free)
        bc, bx = self.bits["core"], self.bits["x"]
        self.fin[bc, bx] = self.acc[tuple(lead)]
        copies = [
            self.remote(5 + n, self.fin.at[bc, bx], self.fin.at[bc, bx], None, other) for n, other in enumerate(self.others)
        ]
        for copy in copies:
            copy.start()
        yield
        for copy in copies:
            copy.wait()


def tick(*jobs):
    for job in jobs:
        next(job, None)


def back_kernel(
    n_crop, n_head, cut,
    attg, grp_h, own, lse, jfc_h, gout, wqkv_h, normed_h, mixed_h, mg_h, mixw_r, prow_r, crop, gain_r, sm_in,
    *rest,
):
    (
        grad_o, fin_o, sm_o,
        grp, wqkv, normt, mixed, mg_s, dor, k_s, v_s, kt_s, qt_s, dot_s, dqt_s, s_s, dp_s, pds_s, dzq_s, dkv_s, dq_s, di_s, msg, ret, dn_s, sent_s, back_s,
        ja, jb, load_sem, do_send, do_recv, dq_send, dq_recv, own_sem, far_sem,
        *reduce_refs,
    ) = rest
    rows, width = mixed.shape
    group = rows * n_head
    local = HEADS // n_head
    c, h = lax.axis_index("crop"), lax.axis_index("head")
    far = lax.rem(c + n_crop // 2, n_crop)
    others = [lax.rem(h + o, n_head) for o in range(1, n_head)]
    peers = [(far, h)] + [(c, other) for other in others]
    if cut:
        bits = {"core": lax.rem(h, 2), "x": lax.div(h, 2), "y": lax.rem(c, 2), "lo": lax.rem(lax.div(c, 2), 2), "hi": lax.div(c, 4)}
        near = {
            "core": (c, h + 1 - 2 * bits["core"]),
            "x": (c, h + 2 - 4 * bits["x"]),
            "y": (c + 1 - 2 * bits["y"], h),
            "lo": (c + 2 - 4 * bits["lo"], h),
            "hi": (far, h),
        }
        peers += [near["y"], near["lo"]]
    greet(peers)

    def spread(j, source, target, send_sem, recv_sem):
        copies = [pltpu.make_async_copy(source(h), target(h), own_sem.at[j])]
        for o, other in enumerate(others):
            copies.append(
                pltpu.make_async_remote_copy(
                    src_ref=source(other), dst_ref=target(h), send_sem=send_sem.at[j, o], recv_sem=recv_sem.at[j, o],
                    device_id=(c, other), device_id_type=MESH,
                )
            )
        return copies

    def start(copies):
        for copy in copies:
            copy.start()

    do_copies = [
        spread(j, lambda d, j=j: attg.at[d * local + j], lambda s, j=j: dor.at[j, s], do_send, do_recv) for j in range(local)
    ]
    start(do_copies[0])
    loads = [
        pltpu.make_async_copy(a, b, load_sem.at[k])
        for k, (a, b) in enumerate([(grp_h, grp), (normed_h, sent_s), (wqkv_h, wqkv), (mixed_h, mixed), (mg_h, mg_s)])
    ]
    loads += [pltpu.make_async_copy(gout.at[k], ja.at[k, 0], load_sem.at[5 + k]) for k in range(2)]
    for load in loads:
        load.start()
    jobs, plan = [], {}
    if cut:
        send_sem, recv_sem, half_sem, sm_send, sm_recv, sm_r, acc_s, *received = reduce_refs
        orders = [
            ("y", "hi", "lo", "x"), ("lo", "y", "hi", "x"), ("y", "lo", "hi", "x"), ("lo", "y", "hi", "x"),
            ("lo", "x", "y", "hi"), ("y", "x", "lo", "hi"),
        ]
        for k in range(6):
            acc = acc_s.at[k] if k < 4 else (ja, jb)[k - 4].at[bits["core"]]
            red = Reduction(acc, [r.at[k] for r in received], fin_o.at[k], send_sem.at[k], recv_sem.at[k], bits, near, peers[1:n_head], orders[k])
            if k < 4:
                keep = pltpu.make_async_copy(jfc_h.at[k, bits["core"]], acc, half_sem.at[k])
                jobs.append(red.steps(jfc_h.at[k, 1 - bits["core"]], keep))
            else:
                jobs.append(red.steps((ja, jb)[k - 4].at[1 - bits["core"]], None))
        fc1, fc2, fc3, fc4, joba, jobb = jobs
        plan = {
            (0, "first"): (fc1, fc2),
            (0, 2): (fc1, fc2, fc3, fc4),
            (1, 2): (fc1, fc2, fc3, fc4),
            (1, "end"): (joba,),
            (2, 2): (fc1, fc2, fc4),
            (2, 5): (fc3, joba, fc1),
            (2, "end"): (fc2, fc4),
            "last": (jobb, fc3, fc1, fc4, fc2),
        }

    bound = crop[0, 0]
    first_case = bound < group // 2
    quarter = rows // 4
    short, long0 = 3 * quarter, 4 * quarter
    in_col = either_in_long(first_case, bound, (quarter, 1), 0, group) > 0.5
    in_row = either_in_long(first_case, bound, (1, quarter), 1, group) > 0.5
    col_long, col_short = jnp.where(in_col, 0.0, NEG), jnp.where(in_col, NEG, 0.0)
    row_long, row_short = jnp.where(in_row, 0.0, NEG), jnp.where(in_row, NEG, 0.0)
    lane = lax.broadcasted_iota(jnp.int32, (8, 128), 1) // HEAD_DIM
    ones = (lane == lax.broadcasted_iota(jnp.int32, (8, 128), 0)).astype(F32).astype(BF16)
    sums_q, sums_v = [None] * HEADS, [None] * HEADS
    dq_copies = []

    def head_grads(j):
        for copy in dq_copies[j]:
            copy.wait()
        total = dn_s[...] if j else 0.0
        for pair in range(n_head // 2):
            packs = []
            for d in (2 * pair, 2 * pair + 1):
                i = d * local + j
                vk = ret[i, 0:rows]
                dq = lanes_to_halves(ret[i, rows : rows + rows // 2])
                dk, dv = vk[:, HEAD_DIM:], vk[:, :HEAD_DIM]
                sums_q[i] = jnp.sum(dq.astype(F32), axis=0, keepdims=True)
                sums_v[i] = jnp.sum(dv.astype(F32), axis=0, keepdims=True)
                odd = i % 2
                base = 3 * HEAD_DIM * i - HEAD_DIM * odd
                none = jnp.zeros_like(dq)
                wide = jnp.concatenate([none, dq, dk, dv] if odd else [dq, dk, dv, none], axis=1)
                total = total + dot_nt(wide, wqkv[:, base : base + 4 * HEAD_DIM])
                packs += [dq, dk, dv]
            grad = dot(normt[...], jnp.concatenate(packs, axis=1))
            if j == 0:
                put_blocks(ja, (pair, 1), grad)
            else:
                put_blocks(jb, (pair, j - 1), grad)
        dn_s[...] = total

    for j in range(local):
        for copy in do_copies[j]:
            copy.wait()
        if j + 1 < local:
            start(do_copies[j + 1])
        if j == 0:
            loads[0].wait()
            tick(*plan.get((0, "first"), ()))
        rowd = []
        for s in range(n_head):
            prod = dor[j, s].astype(F32) * own[j, s].astype(F32)
            hi = prod.astype(BF16)
            d8 = dot_nt(ones, hi) + dot_nt(ones, (prod - hi.astype(F32)).astype(BF16))
            rowd.append(jnp.concatenate([d8[0:1], d8[1:2]], axis=1))
        end = lax.select(first_case, rowd[0], rowd[3])
        full = lax.select(first_case, rowd[3], rowd[0])
        ends = [end[:, quarter * k : quarter * (k + 1)] for k in range(4)]
        first, last = lax.select(first_case, ends[0], ends[3]), lax.select(first_case, ends[3], ends[0])
        di_s[0:1, :] = jnp.concatenate([first, ends[1], ends[2], last, full, rowd[1], rowd[2]], axis=1)
        qk = sorted_blocks(first_case, [grp[j, s, 0:rows] for s in range(n_head)])
        vv = sorted_blocks(first_case, [lanes_to_halves(grp[j, s, rows : rows + rows // 2]) for s in range(n_head)])
        dd = sorted_blocks(first_case, [lanes_to_halves(dor[j, s]) for s in range(n_head)])
        at = 0
        for a, b, d in zip(qk, vv, dd):
            n = a.shape[0]
            q = a[:, :HEAD_DIM] * BF16(HEAD_DIM**-0.5)
            k_s[at : at + n] = a[:, HEAD_DIM:]
            v_s[at : at + n] = b
            qt_s[:, at : at + n] = jnp.transpose(q)
            dot_s[:, at : at + n] = jnp.transpose(d)
            block, inner = at // rows, at % rows
            dzq_s[block, inner : inner + n] = jnp.concatenate([d, jnp.zeros_like(d)], axis=1)
            dzq_s[block, rows + inner : rows + inner + n] = jnp.concatenate([jnp.zeros_like(q), q], axis=1)
            at += n
        kt_s[...] = jnp.transpose(k_s[...])
        dqt_s[...] = jnp.zeros_like(dqt_s)
        dkv_s[...] = jnp.zeros_like(dkv_s)

        def area(q0, count, k0, k1, masks):
            lanes, number = slice(q0, q0 + count), k1 - k0
            s_s[:number, :count] = dot(k_s[k0:k1], qt_s[:, lanes])
            dp_s[:number, :count] = dot(v_s[k0:k1], dot_s[:, lanes])
            for k, mask in masks.items():
                if k0 <= k < k1:
                    s_s[k - k0 : k - k0 + quarter, :count] += mask
            for at in range(0, count, LANES):
                wide = min(LANES, count - at)
                here, place = slice(at, at + wide), slice(q0 + at, q0 + at + wide)
                lse_row, di_row = lse[j : j + 1, place], di_s[0:1, place]
                for k in range(0, number, KEYS):
                    keys = slice(k, k + KEYS)
                    p = jnp.exp(s_s[keys, here] - lse_row)
                    ds = p * (dp_s[keys, here] - di_row)
                    pds_s[keys, here] = p.astype(BF16)
                    pds_s[keys, rows + at : rows + at + wide] = ds.astype(BF16)
            block, inner = q0 // rows, q0 % rows
            if count == rows:
                add = dot(pds_s[:number], dzq_s[block])
            else:
                add = dot(pds_s[:number, :count], dzq_s[block, inner : inner + count])
                add = add + dot(pds_s[:number, rows : rows + count], dzq_s[block, rows + inner : rows + inner + count])
            dkv_s[k0:k1] += add
            dqt_s[:, lanes] += dot(kt_s[:, k0:k1], pds_s[:number, rows : rows + count])

        area(0, short, 0, long0, {short: col_short})
        either = {k: row_short for k in range(0, short, quarter)}
        either[short] = jnp.where(in_row, col_long, col_short)
        either.update({k: row_long for k in range(long0, group, quarter)})
        for k in range(0, group, rows):
            area(short, quarter, k, k + rows, either)
        tick(*plan.get((j, "near"), ()))
        half_keys = (group - short) // 2
        for t in range(n_head - 1):
            for half in range(2):
                k = short + half * half_keys
                area(long0 + t * rows, rows, k, k + half_keys, {short: col_long})
                tick(*plan.get((j, 2 * t + half), ()))
        dq_s[...] = jnp.transpose(dqt_s[...] * HEAD_DIM**-0.5).astype(BF16)

        dkv = unsorted_blocks(first_case, dkv_s[...])
        dqu = unsorted_blocks(first_case, dq_s[...])
        for s in range(n_head):
            msg[j, s, 0:rows] = dkv[s].astype(BF16)
            msg[j, s, rows : rows + rows // 2] = halves_to_lanes(dqu[s])
        dq_copies.append(spread(j, lambda d, j=j: msg.at[j, d], lambda s, j=j: ret.at[s * local + j], dq_send, dq_recv))
        start(dq_copies[j])
        if j == 0:
            for load in loads[1:]:
                load.wait()
            normt[...] = jnp.transpose(sent_s[...])
        else:
            head_grads(j - 1)
        tick(*plan.get((j, "end"), ()))

    head_grads(local - 1)
    tick(*plan.get("last", ()))
    share = as_column(as_line(mixw_r))
    gain = as_line(gain_r).astype(F32)
    sums = [jnp.zeros((1, width), F32)] * 2
    scaled = []
    step = 128
    for r in range(0, rows, step):
        part = slice(r, r + step)
        mix = mixed[part]
        mean = jnp.mean(mix, axis=1, keepdims=True)
        centered = mix - mean
        rstd = lax.rsqrt(jnp.mean(centered * centered, axis=1, keepdims=True) + EPS)
        unit = centered * rstd
        dn = dn_s[part]
        e = dn * gain
        inner = e - jnp.mean(e, axis=1, keepdims=True) - unit * jnp.mean(e * unit, axis=1, keepdims=True)
        grad = mg_s[part] + rstd * inner
        sums[0] = sums[0] + jnp.sum(dn * unit, axis=0, keepdims=True)
        sums[1] = sums[1] + jnp.sum(dn, axis=0, keepdims=True)
        mixed[part] = share[part] * grad
        dn_s[part] = (1.0 - share[part]) * grad
    chosen = lax.broadcasted_iota(jnp.int32, (rows, rows), 0) == as_line(prow_r)
    chosen = chosen.astype(F32).astype(BF16)
    given = dn_s[...]
    high = given.astype(BF16)
    low = (given - high.astype(F32)).astype(BF16)
    sent_s[...] = (dot(chosen, high) + dot(chosen, low)).astype(BF16)
    far_copy = pltpu.make_async_remote_copy(
        src_ref=sent_s, dst_ref=back_s, send_sem=far_sem.at[0], recv_sem=far_sem.at[1], device_id=(far, h), device_id_type=MESH
    )
    far_copy.start()
    sm_o[...] = sm_in[...]
    sm_o[0:1, :] = sums[0]
    sm_o[1:2, :] = sums[1]
    sm_o[2:3, :] = jnp.concatenate(sums_q, axis=1)
    sm_o[3:4, :] = jnp.concatenate(sums_v, axis=1)
    if cut:
        def small_sum():
            for k, axis in enumerate(("core", "x", "y", "lo", "hi")):
                copy = pltpu.make_async_remote_copy(
                    src_ref=sm_o, dst_ref=sm_r.at[k], send_sem=sm_send.at[k], recv_sem=sm_recv.at[k],
                    device_id=near[axis], device_id_type=MESH,
                )
                copy.start()
                yield
                copy.wait()
                sm_o[...] += sm_r[k]

        small = small_sum()
        tick(small, jobb, fc3, fc4, joba, fc1, fc2, small, fc3, fc4, joba, small, fc3, joba, jobb, small, jobb, small, jobb)
    else:
        fin_o[0] = ja[...]
        fin_o[1] = jb[...]
    far_copy.wait()
    for r in range(0, rows, step):
        part = slice(r, r + step)
        grad_o[part] = (mixed[part] + back_s[part].astype(F32)).astype(BF16)
    if cut:
        tick(small, joba, jobb, joba, jobb)


def back(n_crop, n_head, cut, attg, grp, own, lse, jfc, gout, wqkv, normed, mixed, mg, mixw, prow, crop, gain, sm):
    rows, width = mixed.shape
    group, local = rows * n_head, HEADS // n_head
    vmem = pl.BlockSpec(memory_space=pltpu.VMEM)
    hbm = pl.BlockSpec(memory_space=pl.ANY)
    smem = pl.BlockSpec(memory_space=pltpu.SMEM)
    dma = pltpu.SemaphoreType.DMA
    shape = jax.ShapeDtypeStruct
    block = rows + rows // 2
    jq_dims = (2, 2, 2, 2, 2, 96, PIECE) if cut else (2, 2, width, PIECE)
    finals = (6, 2, 2, 96, PIECE) if cut else (2, *jq_dims)
    square = lambda n, kind: pltpu.VMEM((group, n), kind)
    scratch = [
        pltpu.VMEM((local, n_head, block, 128), BF16),
        pltpu.VMEM(wqkv.shape, BF16),
        pltpu.VMEM((width, rows), BF16),
        pltpu.VMEM((rows, width), F32),
        pltpu.VMEM((rows, width), F32),
        pltpu.VMEM((local, n_head, rows // 2, 128), BF16),
        square(HEAD_DIM, BF16), square(HEAD_DIM, BF16),
        pltpu.VMEM((HEAD_DIM, group), BF16), pltpu.VMEM((HEAD_DIM, group), BF16), pltpu.VMEM((HEAD_DIM, group), BF16),
        pltpu.VMEM((HEAD_DIM, group), F32),
        pltpu.VMEM((832, rows), F32), pltpu.VMEM((832, rows), F32), pltpu.VMEM((832, 2 * rows), BF16),
        pltpu.VMEM((n_head, 2 * rows, 128), BF16), square(128, F32), square(HEAD_DIM, BF16),
        pltpu.VMEM((8, group), F32),
        pltpu.VMEM((local, n_head, block, 128), BF16),
        pltpu.VMEM((HEADS, block, 128), BF16),
        pltpu.VMEM((rows, width), F32),
        pltpu.VMEM((rows, width), BF16),
        pltpu.VMEM((rows, width), BF16),
        pltpu.VMEM(jq_dims, BF16),
        pltpu.VMEM(jq_dims, BF16),
        dma((7,)),
        dma((local, n_head - 1)), dma((local, n_head - 1)), dma((local, n_head - 1)), dma((local, n_head - 1)),
        dma((local,)),
        dma((2,)),
    ]
    if cut:
        scratch += [dma((6, 9)), dma((6, 9)), dma((4,)), dma((5,)), dma((5,)), pltpu.VMEM((5, 16, width), F32)]
        scratch.append(pltpu.VMEM((4, 2, 2, 2, 2, 96, PIECE), BF16))
        scratch += [pltpu.VMEM((6,) + (2,) * n + (96, PIECE), BF16) for n in (4, 3, 2, 1, 0)]
    return pl.pallas_call(
        functools.partial(back_kernel, n_crop, n_head, cut),
        out_shape=(shape((rows, width), BF16), shape(finals, BF16), shape((16, width), F32)),
        in_specs=[hbm, hbm, vmem, vmem, hbm, hbm, hbm, hbm, hbm, hbm, vmem, vmem, smem, vmem, vmem],
        out_specs=(vmem,) * 3,
        scratch_shapes=scratch,
        compiler_params=pltpu.CompilerParams(collective_id=2, has_side_effects=True, vmem_limit_bytes=60 * MiB),
        cost_estimate=pl.CostEstimate(flops=2 * 10**10, bytes_accessed=3 * 10**7, transcendentals=10**7),
        name="back",
    )(attg, grp, own, lse, jfc, gout, wqkv, normed, mixed, mg, mixw, prow, crop, gain, sm)


def finish_kernel(n_crop, n_head, grad, fin, sm, *outs):
    grad_o, g1_o, b1_o, gq_o, bq_o, bv_o, go_o, bo_o, g2_o, b2_o, gf1_o, bf1_o, gf2_o, bf2_o = outs
    c = lax.axis_index("crop")
    local = HEADS // n_head
    grad_o[...] = grad[...]
    parts = []
    for k in range(4):
        core, x = k % 2, k // 2
        for half in range(2):
            at = FC_TILE * k + PIECE * half
            gf1_o[:, at : at + PIECE] = fin[half, core, x].astype(F32)
        both = jnp.concatenate([fin[2, core, x], fin[3, core, x]], axis=0)
        parts.append(jnp.transpose(both.astype(F32)))
    gf2_o[...] = jnp.concatenate(parts, axis=1)
    for k in range(2):
        go_o[:, PIECE * k : PIECE * (k + 1)] = fin[4, k, 0].astype(F32)
    parts = []
    for i in range(HEADS):
        d, j = i // local, i % local
        piece = fin[4, d // 2, 1] if j == 0 else fin[5, d // 2, j - 1]
        parts.append(piece[:, 192 * (d % 2) : 192 * (d % 2 + 1)].astype(F32))
    gq_o[...] = jnp.concatenate(parts, axis=1)
    piece = jnp.zeros((16, 96), F32)
    wide = jnp.zeros((1, PIECE), F32)
    for k in range(n_crop):
        piece = lax.select(c == k, sm[:, 96 * k : 96 * (k + 1)], piece)
        wide = lax.select(c == k, sm[8 + k // 2 : 9 + k // 2, PIECE * (k % 2) : PIECE * (k % 2 + 1)], wide)
    for row, out in ((0, g1_o), (1, b1_o), (2, bq_o), (3, bv_o), (4, bo_o), (5, g2_o), (6, b2_o), (7, bf2_o)):
        out[...] = piece[row : row + 1].reshape(96)
    bf1_o[...] = wide.reshape(PIECE)


def finish(n_crop, n_head, grad, fin, sm):
    rows, width = grad.shape
    vmem = pl.BlockSpec(memory_space=pltpu.VMEM)
    shape = jax.ShapeDtypeStruct
    short = shape((96,), F32)
    outs = (
        shape((rows, width), BF16), short, short, shape((96, 3 * width), F32), short, short, shape((96, width), F32), short,
        short, short, shape((96, 4 * width), F32), shape((PIECE,), F32), shape((PIECE, width), F32), short,
    )
    return pl.pallas_call(
        functools.partial(finish_kernel, n_crop, n_head),
        out_shape=outs,
        in_specs=[vmem] * 3,
        out_specs=(vmem,) * len(outs),
        compiler_params=pltpu.CompilerParams(vmem_limit_bytes=60 * MiB),
        name="finish",
    )(grad, fin, sm)


def sum_everywhere(grads, small, n_crop, n_head):
    c = lax.axis_index("crop")

    def scatter(value):
        part = lax.psum_scatter(value.astype(F32), "crop", scatter_dimension=0, tiled=True)
        return lax.psum(part.astype(BF16), "head").astype(F32)

    jfc, ja, jb = grads
    width = jfc.shape[3]
    local = HEADS // n_head
    g1 = jnp.concatenate([jfc[half, t % 2, t // 2] for t in range(4) for half in range(2)], axis=1)
    g2 = jnp.concatenate([jfc[2 + half, t % 2, t // 2] for t in range(4) for half in range(2)], axis=1).T
    go = jnp.concatenate([ja[0, 0], ja[1, 0]], axis=1)
    parts = []
    for i in range(HEADS):
        d, j = i // local, i % local
        piece = ja[d // 2, 1] if j == 0 else jb[d // 2, j - 1]
        parts.append(piece[:, 192 * (d % 2) : 192 * (d % 2 + 1)])
    gq = jnp.concatenate(parts, axis=1)
    total = lax.psum(small, ("crop", "head"))

    def mine(vector):
        count = vector.shape[0] // n_crop
        return lax.dynamic_slice_in_dim(vector, c * count, count, 0)

    rows = [mine(total[k]) for k in range(8)]
    return [
        rows[0], rows[1], scatter(gq), rows[2], rows[3], scatter(go), rows[4], rows[5], rows[6],
        scatter(g1), mine(total[8:12].reshape(4 * width)), scatter(g2), rows[7],
    ]


def shards(
    tokens, mix_weight, partner_row, crop_lengths, ln1_gain, ln1_bias, w_qkv, b_query, b_value, w_out, b_out,
    ln2_gain, ln2_bias, w_fc1, b_fc1, w_fc2, b_fc2, cotangent,
):
    n_crop, n_head = lax.axis_size("crop"), lax.axis_size("head")
    cut = n_crop == 8 and n_head == 4
    small1, small2 = (ln1_gain, ln1_bias, b_query, b_value), (b_out, ln2_gain, ln2_bias, b_fc2, b_fc1)
    mixed, normed, grp, att, own, lse, gw, cott, gsum = front(
        n_crop, n_head, tokens, mix_weight, partner_row, crop_lengths, small1, w_qkv, cotangent, w_fc2
    )
    layer_out, attg, mg, jfc, gout, sm = middle(cut, att, mixed, cotangent, cott, gsum, small2, w_out, w_fc1, w_fc2, gw)
    grad, fin, sm = back(
        n_crop, n_head, cut, attg, grp, own, lse, jfc, gout, w_qkv, normed, mixed, mg, mix_weight, partner_row, crop_lengths, ln1_gain, sm
    )
    if not cut:
        return (layer_out, grad, *sum_everywhere((jfc, fin[0], fin[1]), sm, n_crop, n_head))
    outs = finish(n_crop, n_head, grad, fin, sm)
    return (layer_out, *outs)


def solution(mesh):
    rows, one = P(("crop", "head"), None), P(("crop", "head"))
    in_specs = (rows, one, one, P("crop", None)) + (P(),) * 13 + (rows,)
    vector, matrix = P("crop"), P("crop", None)
    out_specs = (
        rows, rows, vector, vector, matrix, vector, vector, matrix, vector, vector, vector, matrix, vector, matrix, vector,
    )
    return jax.shard_map(shards, mesh=mesh, in_specs=in_specs, out_specs=out_specs, check_vma=False)
```
